128 devices in a mesh: pipe: 4 (over z_lo, core), dp: 32 (over z_hi, x, y).
Axes of the slice: x: 4, y: 4, z: 4 (z_hi: 2, z_lo: 2; z = z_hi * 2 + z_lo), core: 2. Of those that a mesh axis runs over, the one named last changes fastest.
Arguments:
- inputs: float32 [2, 64, 88, 400], P(None, 'dp'), may hold values from -6 to 6
- resets: int32 [2, 64], P(None, 'dp'), may hold values from 1 to 87
- in_mask: int32 [2, 64, 400], P(None, 'dp'), may hold values 0 or 1
- mid_mask: int32 [2, 64, 1150], P(None, 'dp'), may hold values 0 or 1
- out_mask: int32 [2, 64, 1150], P(None, 'dp'), may hold values 0 or 1
- w_ih_one: bfloat16 [400, 4600], P(None, 'pipe'), may hold values from -0.3125 to 0.3125
- w_hh_one: bfloat16 [1150, 4600], P(None, 'pipe'), may hold values from -0.1875 to 0.1875
- bias_one: bfloat16 [4600], P('pipe'), may hold values from -3 to 3
- drop_one: int32 [1150, 4600], P(None, 'pipe'), may hold values 0 or 1
- w_ih_two: bfloat16 [1150, 4600], P(None, 'pipe'), may hold values from -0.1875 to 0.1875
- w_hh_two: bfloat16 [1150, 4600], P(None, 'pipe'), may hold values from -0.1875 to 0.1875
- bias_two: bfloat16 [4600], P('pipe'), may hold values from -3 to 3
- drop_two: int32 [1150, 4600], P(None, 'pipe'), may hold values 0 or 1
- cotangent: bfloat16 [2, 64, 88, 1150], P(None, 'dp'), may hold values from -6 to 6
Outputs:
- layer_outputs: bfloat16 [4, 64, 88, 1150], P('pipe', 'dp')
- grad_input: float32 [2, 64, 88, 400], P(None, 'dp', None, 'pipe')
- grad_w_ih_one: float32 [400, 4600], P(None, 'pipe')
- grad_w_hh_one: float32 [1150, 4600], P(None, 'pipe')
- grad_bias_one: float32 [4600], P('pipe')
- grad_w_ih_two: float32 [1150, 4600], P(None, 'pipe')
- grad_w_hh_two: float32 [1150, 4600], P(None, 'pipe')
- grad_bias_two: float32 [4600], P('pipe')
The draws below stay inside these ranges and needn't reach their ends.
Inputs may be any that keep to these rules, and one draw needn't show every extreme that they name: `resets`: the position in a stream before which its carried state is dropped.
All inputs are finite; a program needn't handle non-finite values. No bound on the sum of `in_mask` or of `mid_mask` or of `out_mask` or of `drop_one` or of `drop_two` on one device may be relied on, other than what follows from the above.
Results may differ from the reference program's by a relative error of at most 0.011.
Values may be sent and summed in bfloat16 or wider, within the bound.
A program may use at most 576 MiB of HBM per device.

```python
import jax
import jax.numpy as jnp
from jax import lax

D_IN = 400
HIDDEN_SIZE = 1150
GATES = 4600
LEN = 88
STREAMS = 64


def with_ends(result, rng, least, high):
    place = [jax.random.randint(jax.random.fold_in(rng, axis), (), 0, length) for axis, length in enumerate(result.shape)]
    longest = result.shape.index(max(result.shape))
    neighbour = place[:longest] + [(place[longest] + 1) % result.shape[longest]] + place[longest + 1:]
    return result.at[tuple(place)].set(least).at[tuple(neighbour)].set(high)


def levels(rng, shape, split, smallest, largest):
    factor_of = 1.0
    for dim, parts in split:
        heights = jax.random.uniform(jax.random.fold_in(jax.random.fold_in(rng, 6), dim), (parts,), jnp.float32, smallest / len(split), largest / len(split))
        factor_of = factor_of * jnp.repeat(jnp.exp(heights), shape[dim] // parts).reshape((-1,) + (1,) * (len(shape) - 1 - dim))
    return factor_of


def bell_draw(key, dims, width, most, split=(), kind=jnp.bfloat16):
    gain = levels(key, dims, split, -0.22, 0.18) if split else 1.0
    array = jax.random.normal(key, dims, jnp.float32) * width * gain
    return jnp.minimum(jnp.maximum(array, -most), most).astype(kind)


def setup_inputs(seed: int = 0) -> dict:
    keys = jax.random.split(jax.random.key(seed), 15)
    return {
        "inputs": bell_draw(keys[0], (2, STREAMS, LEN, D_IN), 1.0, 6.0, ((1, 32),), jnp.float32),
        "resets": with_ends(jax.random.randint(keys[1], (2, STREAMS), 1, LEN), jax.random.fold_in(keys[1], 1), 1, LEN - 1).astype(jnp.int32),
        "in_mask": with_ends((jax.random.randint(keys[2], (2, STREAMS, D_IN), 0, 4) < 3).astype(jnp.int32), jax.random.fold_in(keys[2], 1), 0, 1),
        "mid_mask": with_ends((jax.random.randint(keys[3], (2, STREAMS, HIDDEN_SIZE), 0, 4) < 3).astype(jnp.int32), jax.random.fold_in(keys[3], 1), 0, 1),
        "out_mask": with_ends((jax.random.randint(keys[4], (2, STREAMS, HIDDEN_SIZE), 0, 4) < 3).astype(jnp.int32), jax.random.fold_in(keys[4], 1), 0, 1),
        "w_ih_one": bell_draw(keys[5], (D_IN, GATES), D_IN ** -0.5, 0.3125, ((1, 4),)),
        "w_hh_one": bell_draw(keys[6], (HIDDEN_SIZE, GATES), HIDDEN_SIZE ** -0.5, 0.1875, ((1, 4),)),
        "bias_one": bell_draw(keys[7], (GATES,), 0.5, 3.0, ((0, 4),)),
        "drop_one": with_ends((jax.random.randint(keys[8], (HIDDEN_SIZE, GATES), 0, 2) < 1).astype(jnp.int32), jax.random.fold_in(keys[8], 1), 0, 1),
        "w_ih_two": bell_draw(keys[9], (HIDDEN_SIZE, GATES), HIDDEN_SIZE ** -0.5, 0.1875, ((1, 4),)),
        "w_hh_two": bell_draw(keys[10], (HIDDEN_SIZE, GATES), HIDDEN_SIZE ** -0.5, 0.1875, ((1, 4),)),
        "bias_two": bell_draw(keys[11], (GATES,), 0.5, 3.0, ((0, 4),)),
        "drop_two": with_ends((jax.random.randint(keys[12], (HIDDEN_SIZE, GATES), 0, 2) < 1).astype(jnp.int32), jax.random.fold_in(keys[12], 1), 0, 1),
        "cotangent": bell_draw(keys[13], (2, STREAMS, LEN, HIDDEN_SIZE), 1.0, 6.0, ((1, 32),)),
    }


@jax.custom_vjp
def low(v):
    return lax.optimization_barrier(v.astype(jnp.bfloat16)).astype(jnp.float32)

@jax.custom_vjp
def low_back(v):
    return v

def low_keep(v):
    return (low(v), None)

def low_pass(kept, grad):
    return (grad,)

def back_keep(v):
    return (v, None)

def back_low(kept, grad):
    return (low(grad),)
low.defvjp(low_keep, low_pass)
low_back.defvjp(back_keep, back_low)
keep_scale = 4.0 / 3.0
weight_scale = 2.0
highest = lax.Precision.HIGHEST

def run_layer(layer_input, w_input, w_recur, bias, resets_flat):
    hidden_size = w_recur.shape[0]
    batch = layer_input.shape[0]
    projected = jnp.einsum('bti,ig->tbg', layer_input, w_input, precision=highest) + bias

    def advance(carry, items):
        hidden, cell_state = carry
        proj_now, time_now = items
        keep_mask = (resets_flat != time_now)[:, None]
        hidden_prev = jnp.where(keep_mask, hidden, 0.0)
        cell_prev = jnp.where(keep_mask, cell_state, 0.0)
        gates = low_back(proj_now + jnp.dot(hidden_prev, w_recur, precision=highest))
        gate_in = jax.nn.sigmoid(gates[:, :hidden_size])
        gate_forget = jax.nn.sigmoid(gates[:, hidden_size:2 * hidden_size])
        gate_cand = jnp.tanh(gates[:, 2 * hidden_size:3 * hidden_size])
        gate_out = jax.nn.sigmoid(gates[:, 3 * hidden_size:])
        cell_state = gate_forget * cell_prev + gate_in * gate_cand
        hidden = low(gate_out * jnp.tanh(cell_state))
        return ((hidden, cell_state), hidden)
    start = (jnp.zeros((batch, hidden_size), jnp.float32), jnp.zeros((batch, hidden_size), jnp.float32))
    times = jnp.arange(LEN, dtype=jnp.int32)
    unused, outputs = lax.scan(jax.checkpoint(advance), start, (projected, times))
    return jnp.swapaxes(outputs, 0, 1)

def reference(inputs, resets, in_mask, mid_mask, out_mask, w_ih_one, w_hh_one, bias_one, drop_one, w_ih_two, w_hh_two, bias_two, drop_two, cotangent):
    batch = 2 * STREAMS
    resets_flat = resets.reshape(batch).astype(jnp.int32)
    keep_in = in_mask.reshape(2, STREAMS, 1, D_IN).astype(jnp.float32) * keep_scale
    keep_mid = mid_mask.reshape(batch, 1, HIDDEN_SIZE).astype(jnp.float32) * keep_scale
    keep_out = out_mask.reshape(batch, 1, HIDDEN_SIZE).astype(jnp.float32) * keep_scale
    drop_first = drop_one.astype(jnp.float32) * weight_scale
    drop_second = drop_two.astype(jnp.float32) * weight_scale

    def forward(source, in_first, rec_first, bias_first, in_second, rec_second, bias_second):
        first_input = low(source * keep_in).reshape(batch, LEN, D_IN)
        first_hidden = run_layer(first_input, in_first, rec_first * drop_first, bias_first, resets_flat)
        first_out = low(first_hidden * keep_mid)
        second_hidden = run_layer(low_back(first_out), in_second, rec_second * drop_second, bias_second, resets_flat)
        second_out = low(second_hidden * keep_out)
        return (first_out, second_out)
    outputs, pullback = jax.vjp(forward, inputs.astype(jnp.float32), w_ih_one.astype(jnp.float32), w_hh_one.astype(jnp.float32), bias_one.astype(jnp.float32), w_ih_two.astype(jnp.float32), w_hh_two.astype(jnp.float32), bias_two.astype(jnp.float32))
    first_out, second_out = outputs
    grads = pullback((jnp.zeros_like(first_out), cotangent.reshape(batch, LEN, HIDDEN_SIZE).astype(jnp.float32)))
    layer_outputs = jnp.concatenate([first_out.reshape(2, STREAMS, LEN, HIDDEN_SIZE), second_out.reshape(2, STREAMS, LEN, HIDDEN_SIZE)], 0).astype(jnp.bfloat16)
    return (layer_outputs, grads[0], grads[1], grads[2], grads[3], grads[4], grads[5], grads[6])
```

```python
import functools

import jax
import jax.numpy as jnp
from jax import lax
from jax.experimental import pallas as pl
from jax.experimental.pallas import tpu as pltpu
from jax.sharding import PartitionSpec as P

MESH = pl.DeviceIdType.MESH
HID = 1150
WIDE = 1152
D_IN = 400
D_WIDE = 416
STEPS = 88
ROWS = 4
CHUNKS = 44
GROUP = 4
HALF = WIDE // 2

keep_scale = 4.0 / 3.0
weight_scale = 2.0

LAYER_ONE, SOURCE_GRAD, LAYER_TWO, BETWEEN = 0, 1, 2, 3
W_ONE, R_ONE, R_TWO, W_TWO, R_ONE_T, R_TWO_T, W_TWO_T, W_ONE_T = range(8)
USER = {
    W_ONE: LAYER_ONE,
    R_ONE: LAYER_ONE,
    R_TWO: LAYER_TWO,
    W_TWO: BETWEEN,
    R_ONE_T: LAYER_ONE,
    R_TWO_T: LAYER_TWO,
    W_TWO_T: BETWEEN,
    W_ONE_T: SOURCE_GRAD,
}
FORWARD = (W_ONE, W_TWO, R_ONE, R_TWO)
BACKWARD = (R_TWO_T, W_TWO_T, R_ONE_T, W_ONE_T)


def sigmoid(value):
    return 0.5 * jnp.tanh(0.5 * value) + 0.5


def dot(left, right):
    return jnp.dot(left, right, preferred_element_type=jnp.float32)


def relay_kernel(
    w_one, r_one, r_two, w_two, r_one_t, r_two_t, w_two_t, w_one_t,
    source, keep, layer_keep, cotangent,
    o_u, o_hp_one, o_hp_two, o_out, o_dz_one, o_dz_two, o_dx,
    w_front, w_back, w_in, zx, extra, dz, du, dx, hidden, cell, stage_a, stage_b, stage_z,
    block_send, block_recv, block_local,
    u_send, u_recv, z_send, z_recv, dz_send, dz_recv, du_send, du_recv,
    bulk_send, bulk_recv, part_send, part_recv, dx_send, dx_recv, local_sem,
):
    pipe = lax.axis_index("pipe")
    dp = lax.axis_index("dp")
    dp_count = lax.axis_size("dp")
    dp_far = lax.rem(dp + dp_count // 2, dp_count)

    barrier = pltpu.get_barrier_semaphore()
    for step in range(1, 4):
        pl.semaphore_signal(
            barrier, inc=1, device_id={"pipe": lax.rem(pipe + step, 4), "dp": dp}, device_id_type=MESH
        )
    for step in range(4):
        pl.semaphore_signal(
            barrier, inc=1, device_id={"pipe": lax.rem(pipe + step, 4), "dp": dp_far}, device_id_type=MESH
        )
    pl.semaphore_wait(barrier, 7)

    blocks = {
        W_ONE: w_one, R_ONE: r_one, R_TWO: r_two, W_TWO: w_two,
        R_ONE_T: r_one_t, R_TWO_T: r_two_t, W_TWO_T: w_two_t, W_ONE_T: w_one_t,
    }

    def landing(kind, p):
        if kind == W_ONE:
            return w_in.at[p]
        if kind in (R_ONE, R_TWO, W_TWO):
            return w_front.at[p]
        if kind == W_ONE_T:
            return w_front.at[p, :, pl.ds(0, 512)]
        return w_back.at[p]

    def block_copies(kind, p):
        user = USER[kind]
        source_ref, target = blocks[kind], landing(kind, p)
        if p == user:
            return [pltpu.make_async_copy(source_ref, target, block_local.at[kind])]
        if p // 2 == user // 2:
            return [
                pltpu.make_async_remote_copy(
                    source_ref, target, block_send.at[kind, 0], block_recv.at[kind, p, 0],
                    device_id={"pipe": user, "dp": dp}, device_id_type=MESH,
                )
            ]
        rows = source_ref.shape[0] // 2
        return [
            pltpu.make_async_remote_copy(
                source_ref.at[pl.ds(part * rows, rows)], target.at[pl.ds(part * rows, rows)],
                block_send.at[kind, part], block_recv.at[kind, p, part],
                device_id={"pipe": user, "dp": (dp, dp_far)[part]}, device_id_type=MESH,
            )
            for part in range(2)
        ]

    def start_blocks(kinds, p):
        for kind in kinds:
            for copy in block_copies(kind, p):
                copy.start()

    def finish_blocks(kinds, p):
        for kind in kinds:
            if p != USER[kind]:
                for copy in block_copies(kind, p):
                    copy.wait_send()

    def await_blocks(kind):
        for p in range(4):
            for copy in block_copies(kind, p):
                if p == USER[kind]:
                    copy.wait()
                else:
                    copy.wait_recv()

    def to(pipe_to, source_ref, target, send, recv):
        return pltpu.make_async_remote_copy(
            source_ref, target, send, recv,
            device_id={"pipe": pipe_to, "dp": dp}, device_id_type=MESH,
        )

    def copy_u(c):
        return to(BETWEEN, o_u.at[c], o_u.at[c], u_send, u_recv.at[c])

    def copy_z(c):
        return to(LAYER_TWO, zx.at[c], zx.at[c], z_send, z_recv.at[c])

    def copy_dz(pipe_to, c):
        return to(pipe_to, dz.at[:, c], dz.at[:, c], dz_send, dz_recv.at[c])

    def copy_du(c):
        return to(LAYER_ONE, du.at[c], du.at[c], du_send, du_recv.at[c])

    def copy_part(pipe_to, output, group, slot, gate):
        span = pl.ds(group * GROUP, GROUP)
        return to(pipe_to, dz.at[gate, span], output.at[span], part_send.at[slot], part_recv.at[group])

    def copy_dx(pipe_to, group, slot):
        span = pl.ds(group * GROUP, GROUP)
        return to(
            pipe_to, dx.at[span, :, pl.ds(pipe_to * 128, 128)], o_dx.at[span], dx_send.at[slot], dx_recv.at[group]
        )

    def copy_bulk(pipe_to, ref, slot, which):
        return to(pipe_to, ref, ref, bulk_send.at[slot], bulk_recv.at[which])

    def keep_rows(c, j):
        return jnp.broadcast_to(keep[c, ROWS * j : ROWS * j + ROWS, 0:1], (ROWS, WIDE))

    def clear():
        hidden[...] = jnp.zeros_like(hidden)
        cell[...] = jnp.zeros_like(cell)

    def forward_pair(c, mask, with_one, o_hp, o_layer):
        column = lax.broadcasted_iota(jnp.int32, (ROWS, WIDE), 1)
        for j in range(2):
            rows = pl.ds(ROWS * j, ROWS)
            kept = keep_rows(c, j)
            hidden_prev = hidden[...] * kept
            cell_prev = cell[...] * kept
            left = hidden_prev.astype(jnp.bfloat16)
            gates = [
                dot(left, w_front[g]) + zx[c, rows, pl.ds(g * WIDE, WIDE)] for g in range(4)
            ]
            gate_in, gate_forget = sigmoid(gates[0]), sigmoid(gates[1])
            gate_cand, gate_out = jnp.tanh(gates[2]), sigmoid(gates[3])
            cell_now = gate_forget * cell_prev + gate_in * gate_cand
            cell_tanh = jnp.tanh(cell_now)
            hidden_now = (gate_out * cell_tanh).astype(jnp.bfloat16).astype(jnp.float32)
            cell[...] = cell_now
            hidden[...] = hidden_now
            stage_a[rows, :] = hidden_prev
            layer = hidden_now * mask
            if with_one:
                layer = jnp.where(column == HID, 1.0, layer)
            stage_b[rows, :] = layer
            zx[c, rows, pl.ds(0, WIDE)] = gate_cand * gate_in * (1.0 - gate_in)
            zx[c, rows, pl.ds(WIDE, WIDE)] = cell_prev * gate_forget * (1.0 - gate_forget)
            zx[c, rows, pl.ds(2 * WIDE, WIDE)] = gate_in * (1.0 - gate_cand * gate_cand)
            zx[c, rows, pl.ds(3 * WIDE, WIDE)] = cell_tanh * gate_out * (1.0 - gate_out)
            extra[c, rows, pl.ds(0, WIDE)] = gate_out * (1.0 - cell_tanh * cell_tanh)
            extra[c, rows, pl.ds(WIDE, WIDE)] = gate_forget * kept
        o_hp[c] = stage_a[...].astype(jnp.bfloat16)
        o_layer[c] = stage_b[...].astype(jnp.bfloat16)

    def backward_pair(c, mask, upstream):
        above = upstream[c].astype(jnp.float32)
        for j in (1, 0):
            rows = pl.ds(ROWS * j, ROWS)
            total = hidden[...] + above[ROWS * j : ROWS * j + ROWS] * mask
            out_grad = total * zx[c, rows, pl.ds(3 * WIDE, WIDE)]
            cell_total = cell[...] + total * extra[c, rows, pl.ds(0, WIDE)]
            cell[...] = cell_total * extra[c, rows, pl.ds(WIDE, WIDE)]
            grads = [cell_total * zx[c, rows, pl.ds(g * WIDE, WIDE)] for g in range(3)] + [out_grad]
            back = None
            for g in range(4):
                stage_z[rows, pl.ds(g * WIDE, WIDE)] = grads[g]
                part = dot(grads[g].astype(jnp.bfloat16), w_back[g])
                back = part if back is None else back + part
            hidden[...] = back * keep_rows(c, j)
        for g in range(4):
            dz[g, c] = stage_z[:, pl.ds(g * WIDE, WIDE)].astype(jnp.bfloat16)

    last = CHUNKS - 1
    groups = CHUNKS // GROUP

    @pl.when(pipe == LAYER_ONE)
    def _():
        me = LAYER_ONE
        start_blocks(FORWARD, me)
        await_blocks(W_ONE)
        for g in range(4):
            zx[:, :, pl.ds(g * WIDE, WIDE)] = dot(source[...], w_in[g]).reshape(CHUNKS, 2 * ROWS, WIDE)
        await_blocks(R_ONE)
        start_blocks(BACKWARD, me)
        clear()

        def ahead(c, carry):
            forward_pair(c, layer_keep[0], True, o_hp_one, o_u)
            copy_u(c).start()
            return carry

        lax.fori_loop(0, CHUNKS, ahead, 0)
        bulk = [
            copy_bulk(SOURCE_GRAD, o_u, 0, 0), copy_bulk(LAYER_TWO, o_u, 1, 0),
            copy_bulk(SOURCE_GRAD, o_hp_one, 2, 1), copy_bulk(LAYER_TWO, o_hp_one, 3, 1),
            copy_bulk(BETWEEN, o_hp_one, 4, 1),
        ]
        for copy in bulk:
            copy.start()
        await_blocks(R_ONE_T)
        clear()

        def behind(i, carry):
            c = last - i
            copy_du(c).wait_recv()
            backward_pair(c, layer_keep[0], du)
            copy_dz(SOURCE_GRAD, c).start()

            @pl.when(lax.rem(c, GROUP) == 0)
            def _():
                group = c // GROUP
                copy_part(LAYER_TWO, o_dz_one, group, 0, LAYER_TWO).start()
                copy_part(BETWEEN, o_dz_one, group, 1, BETWEEN).start()

            return carry

        lax.fori_loop(0, CHUNKS, behind, 0)
        own = pltpu.make_async_copy(dz.at[me], o_dz_one, local_sem.at[0])
        own.start()
        finish_blocks(FORWARD + BACKWARD, me)
        to(BETWEEN, o_u, o_u, u_send, u_recv.at[0]).wait_send()
        for copy in bulk:
            copy.wait_send()
        to(SOURCE_GRAD, dz, dz, dz_send, dz_recv.at[0]).wait_send()
        to(LAYER_TWO, dz.at[me], o_dz_one, part_send.at[0], part_recv.at[0]).wait_send()
        to(BETWEEN, dz.at[me], o_dz_one, part_send.at[1], part_recv.at[0]).wait_send()
        own.wait()

        copy_bulk(me, o_hp_two, 0, 2).wait_recv()
        for group in range(groups):
            copy_part(me, o_dz_two, group, 0, me).wait_recv()
            copy_dx(me, group, 0).wait_recv()

    @pl.when(pipe == LAYER_TWO)
    def _():
        me = LAYER_TWO
        start_blocks(FORWARD, me)
        await_blocks(R_TWO)
        start_blocks(BACKWARD, me)
        clear()

        def ahead(c, carry):
            copy_z(c).wait_recv()
            forward_pair(c, layer_keep[1], False, o_hp_two, o_out)
            return carry

        lax.fori_loop(0, CHUNKS, ahead, 0)
        bulk = [
            copy_bulk(LAYER_ONE, o_hp_two, 0, 2), copy_bulk(SOURCE_GRAD, o_hp_two, 1, 2),
            copy_bulk(BETWEEN, o_hp_two, 2, 2), copy_bulk(BETWEEN, o_out, 3, 3),
        ]
        for copy in bulk:
            copy.start()
        await_blocks(R_TWO_T)
        clear()

        def behind(i, carry):
            c = last - i
            backward_pair(c, layer_keep[1], cotangent)
            copy_dz(BETWEEN, c).start()

            @pl.when(lax.rem(c, GROUP) == 0)
            def _():
                group = c // GROUP
                copy_part(LAYER_ONE, o_dz_two, group, 0, LAYER_ONE).start()
                copy_part(SOURCE_GRAD, o_dz_two, group, 1, SOURCE_GRAD).start()

            return carry

        lax.fori_loop(0, CHUNKS, behind, 0)
        own = pltpu.make_async_copy(dz.at[me], o_dz_two, local_sem.at[0])
        own.start()
        finish_blocks(FORWARD + BACKWARD, me)
        for copy in bulk:
            copy.wait_send()
        to(BETWEEN, dz, dz, dz_send, dz_recv.at[0]).wait_send()
        to(LAYER_ONE, dz.at[me], o_dz_two, part_send.at[0], part_recv.at[0]).wait_send()
        to(SOURCE_GRAD, dz.at[me], o_dz_two, part_send.at[1], part_recv.at[0]).wait_send()
        own.wait()

        copy_bulk(me, o_u, 0, 0).wait_recv()
        copy_bulk(me, o_hp_one, 0, 1).wait_recv()
        for group in range(groups):
            copy_part(me, o_dz_one, group, 0, me).wait_recv()
            copy_dx(me, group, 0).wait_recv()

    @pl.when(pipe == BETWEEN)
    def _():
        me = BETWEEN
        start_blocks(FORWARD, me)
        await_blocks(W_TWO)
        start_blocks(BACKWARD, me)

        def ahead(c, carry):
            copy_u(c).wait_recv()
            for g in range(4):
                zx[c, :, pl.ds(g * WIDE, WIDE)] = dot(o_u[c], w_front[g])
            copy_z(c).start()
            return carry

        lax.fori_loop(0, CHUNKS, ahead, 0)
        await_blocks(W_TWO_T)

        def behind(i, carry):
            c = last - i
            copy_dz(me, c).wait_recv()
            back = None
            for g in range(4):
                part = dot(dz[g, c], w_back[g])
                back = part if back is None else back + part
            du[c] = back.astype(jnp.bfloat16)
            copy_du(c).start()
            return carry

        lax.fori_loop(0, CHUNKS, behind, 0)
        own = pltpu.make_async_copy(dz.at[me], o_dz_two, local_sem.at[0])
        own.start()
        finish_blocks(FORWARD + BACKWARD, me)
        to(LAYER_TWO, zx, zx, z_send, z_recv.at[0]).wait_send()
        to(LAYER_ONE, du, du, du_send, du_recv.at[0]).wait_send()
        own.wait()

        copy_bulk(me, o_hp_one, 0, 1).wait_recv()
        copy_bulk(me, o_hp_two, 0, 2).wait_recv()
        copy_bulk(me, o_out, 0, 3).wait_recv()
        for group in range(groups):
            copy_part(me, o_dz_one, group, 0, me).wait_recv()
            copy_dx(me, group, 0).wait_recv()

    @pl.when(pipe == SOURCE_GRAD)
    def _():
        me = SOURCE_GRAD
        start_blocks(FORWARD, me)
        finish_blocks(FORWARD, me)
        start_blocks(BACKWARD, me)
        await_blocks(W_ONE_T)

        def behind(i, carry):
            c = last - i
            copy_dz(me, c).wait_recv()
            back = None
            for g in range(4):
                part = dot(dz[g, c], w_front[g, :, :512])
                back = part if back is None else back + part
            dx[c] = back

            @pl.when(lax.rem(c, GROUP) == 0)
            def _():
                group = c // GROUP
                copy_dx(LAYER_ONE, group, 0).start()
                copy_dx(LAYER_TWO, group, 1).start()
                copy_dx(BETWEEN, group, 2).start()

            return carry

        lax.fori_loop(0, CHUNKS, behind, 0)
        own = pltpu.make_async_copy(dz.at[me], o_dz_one, local_sem.at[0])
        own.start()
        own_dx = pltpu.make_async_copy(dx.at[:, :, pl.ds(me * 128, 128)], o_dx, local_sem.at[1])
        own_dx.start()
        finish_blocks(BACKWARD, me)
        for slot, pipe_to in enumerate((LAYER_ONE, LAYER_TWO, BETWEEN)):
            to(pipe_to, o_dx, o_dx, dx_send.at[slot], dx_recv.at[0]).wait_send()
        own.wait()
        own_dx.wait()

        copy_bulk(me, o_u, 0, 0).wait_recv()
        copy_bulk(me, o_hp_one, 0, 1).wait_recv()
        copy_bulk(me, o_hp_two, 0, 2).wait_recv()
        for group in range(groups):
            copy_part(me, o_dz_two, group, 0, me).wait_recv()


def relay(blocks, source, keep, layer_keep, cotangent):
    whole = pl.BlockSpec(memory_space=pltpu.VMEM)
    rows = (CHUNKS, 2 * ROWS, WIDE)
    half, full = jnp.bfloat16, jnp.float32
    shapes = [jax.ShapeDtypeStruct(rows, half)] * 6 + [
        jax.ShapeDtypeStruct((CHUNKS, 2 * ROWS, 128), full)
    ]
    dma = pltpu.SemaphoreType.DMA
    return pl.pallas_call(
        relay_kernel,
        out_shape=shapes,
        in_specs=[pl.BlockSpec(memory_space=pl.ANY)] * 8 + [whole] * 4,
        out_specs=[whole] * 7,
        scratch_shapes=[
            pltpu.VMEM((4, WIDE, WIDE), half),
            pltpu.VMEM((4, WIDE, WIDE), half),
            pltpu.VMEM((4, D_WIDE, WIDE), half),
            pltpu.VMEM((CHUNKS, 2 * ROWS, 4 * WIDE), full),
            pltpu.VMEM((CHUNKS, 2 * ROWS, 2 * WIDE), full),
            pltpu.VMEM((4,) + rows, half),
            pltpu.VMEM(rows, half),
            pltpu.VMEM((CHUNKS, 2 * ROWS, 512), full),
            pltpu.VMEM((ROWS, WIDE), full),
            pltpu.VMEM((ROWS, WIDE), full),
            pltpu.VMEM((2 * ROWS, WIDE), full),
            pltpu.VMEM((2 * ROWS, WIDE), full),
            pltpu.VMEM((2 * ROWS, 4 * WIDE), full),
            dma((8, 2)), dma((8, 4, 2)), dma((8,)),
            dma, dma((CHUNKS,)), dma, dma((CHUNKS,)), dma, dma((CHUNKS,)), dma, dma((CHUNKS,)),
            dma((5,)), dma((4,)), dma((2,)), dma((CHUNKS // GROUP,)), dma((3,)), dma((CHUNKS // GROUP,)), dma((2,)),
        ],
        compiler_params=pltpu.CompilerParams(
            vmem_limit_bytes=60 << 20, collective_id=0, has_side_effects=True
        ),
        name="relay",
    )(*blocks, source, keep, layer_keep, cotangent)


def padded(array, rows, columns):
    return jnp.pad(array, ((0, rows - array.shape[0]), (0, columns - array.shape[1])))


def by_time(array):
    ordered = jnp.transpose(array, (2, 0, 1, 3))
    return ordered.reshape(CHUNKS, 2 * ROWS, array.shape[3])


def local(
    inputs, resets, in_mask, mid_mask, out_mask,
    w_ih_one, w_hh_one, bias_one, drop_one, w_ih_two, w_hh_two, bias_two, drop_two, cotangent,
):
    pipe = lax.axis_index("pipe")
    rec_one, rec_two = (
        (weights.astype(jnp.float32) * drop.astype(jnp.float32) * weight_scale).astype(jnp.bfloat16)
        for weights, drop in ((w_hh_one, drop_one), (w_hh_two, drop_two))
    )
    blocks = (
        padded(jnp.concatenate([w_ih_one, bias_one[None]], 0), D_WIDE, WIDE),
        padded(rec_one, WIDE, WIDE),
        padded(rec_two, WIDE, WIDE),
        padded(jnp.concatenate([w_ih_two, bias_two[None]], 0), WIDE, WIDE),
        padded(rec_one.T, WIDE, WIDE),
        padded(rec_two.T, WIDE, WIDE),
        padded(w_ih_two.T, WIDE, WIDE),
        jnp.pad(w_ih_one.T.reshape(HID, 4, 100), ((0, 2), (0, 0), (0, 28))).reshape(WIDE, 512),
    )
    keep_in = in_mask.astype(jnp.float32) * keep_scale
    source = by_time((inputs * keep_in[:, :, None, :]).astype(jnp.bfloat16)).reshape(STEPS * ROWS, D_IN)
    ones = jnp.ones((STEPS * ROWS, 1), jnp.bfloat16)
    source = padded(jnp.concatenate([source, ones], 1), STEPS * ROWS, D_WIDE)
    positions = jnp.arange(STEPS, dtype=jnp.int32)
    keep = (resets.reshape(1, ROWS) != positions[:, None]).astype(jnp.float32)
    keep = jnp.broadcast_to(keep.reshape(CHUNKS, 2 * ROWS, 1), (CHUNKS, 2 * ROWS, 128))
    layer_keep = jnp.stack([mid_mask.reshape(ROWS, HID), out_mask.reshape(ROWS, HID)]).astype(jnp.float32)
    layer_keep = jnp.pad(layer_keep * keep_scale, ((0, 0), (0, 0), (0, WIDE - HID)))
    cot = jnp.pad(by_time(cotangent), ((0, 0), (0, 0), (0, WIDE - HID)))

    u_two, hp_one, hp_two, out_two, dz_one, dz_two, dx = relay(blocks, source, keep, layer_keep, cot)

    layer = jnp.where(pipe < 2, u_two, out_two).reshape(STEPS, 2, 2, WIDE)[..., :HID]
    layer = lax.dynamic_index_in_dim(layer, pipe % 2, 1, keepdims=False)
    layer_outputs = jnp.swapaxes(layer, 0, 1)[None]
    grad_input = jnp.transpose(dx.reshape(STEPS, 2, 2, 128)[..., :100], (1, 2, 0, 3))
    keep_part = lax.dynamic_slice_in_dim(keep_in, pipe * 100, 100, 2)
    grad_input = grad_input * keep_part[:, :, None, :]

    def grads(left, right):
        return lax.dot_general(
            left.reshape(STEPS * ROWS, -1), right.reshape(STEPS * ROWS, WIDE),
            (((0,), (0,)), ((), ())), preferred_element_type=jnp.float32,
        ).astype(jnp.bfloat16)

    parts = (grads(source, dz_one), grads(hp_one, dz_one), grads(u_two, dz_two), grads(hp_two, dz_two))
    total = lax.psum(jnp.concatenate(parts, 0), "dp").astype(jnp.float32)
    in_one, total = total[:D_WIDE], total[D_WIDE:]
    rec_one_grad, in_two, rec_two_grad = total[:WIDE], total[WIDE : 2 * WIDE], total[2 * WIDE :]
    return (
        layer_outputs,
        grad_input,
        in_one[:D_IN, :HID],
        rec_one_grad[:HID, :HID] * drop_one.astype(jnp.float32) * weight_scale,
        in_one[D_IN, :HID],
        in_two[:HID, :HID],
        rec_two_grad[:HID, :HID] * drop_two.astype(jnp.float32) * weight_scale,
        in_two[HID, :HID],
    )


def solution(mesh):
    placed = (
        P(None, "dp", None, None),
        P(None, "dp"),
        P(None, "dp", None),
        P(None, "dp", None),
        P(None, "dp", None),
        P(None, "pipe"),
        P(None, "pipe"),
        P("pipe"),
        P(None, "pipe"),
        P(None, "pipe"),
        P(None, "pipe"),
        P("pipe"),
        P(None, "pipe"),
        P(None, "dp", None, None),
    )
    return jax.shard_map(
        local,
        mesh=mesh,
        in_specs=placed,
        out_specs=(
            P("pipe", "dp", None, None),
            P(None, "dp", None, "pipe"),
            P(None, "pipe"),
            P(None, "pipe"),
            P("pipe"),
            P(None, "pipe"),
            P(None, "pipe"),
            P("pipe"),
        ),
        check_vma=False,
    )
```

```python
import functools

import jax
import jax.numpy as jnp
from jax import lax
from jax.experimental import pallas as pl
from jax.experimental.pallas import tpu as pltpu
from jax.sharding import PartitionSpec as P

MESH = pl.DeviceIdType.MESH
HID = 1150
WIDE = 1152
D_IN = 400
D_WIDE = 416
STEPS = 88
ROWS = 4
CHUNKS = 44
GROUP = 4
UNIT = 128
HALF_UNIT = 64
UNITS = 32
HP_ONE, SOURCE, U_TWO, HP_TWO = 0, 1152, 1792, 2944
SOURCE_WIDE = 640
SWITCH = 14

keep_scale = 4.0 / 3.0
weight_scale = 2.0

LAYER_ONE, SOURCE_GRAD, LAYER_TWO, BETWEEN = 0, 1, 2, 3
W_ONE, R_ONE, R_TWO, W_TWO, R_ONE_T, R_TWO_T, W_TWO_T, W_ONE_T = range(8)
USER = {
    W_ONE: LAYER_ONE,
    R_ONE: LAYER_ONE,
    R_TWO: LAYER_TWO,
    W_TWO: BETWEEN,
    R_ONE_T: LAYER_ONE,
    R_TWO_T: LAYER_TWO,
    W_TWO_T: BETWEEN,
    W_ONE_T: SOURCE_GRAD,
}
FORWARD = (W_ONE, W_TWO, R_ONE, R_TWO)
BACKWARD = (R_TWO_T, W_TWO_T, R_ONE_T, W_ONE_T)


def sigmoid(value):
    return 0.5 * jnp.tanh(0.5 * value) + 0.5


def dot(left, right):
    return jnp.dot(left, right, preferred_element_type=jnp.float32)


def relay_kernel(
    w_one, r_one, r_two, w_two, r_one_t, r_two_t, w_two_t, w_one_t,
    source, keep, layer_keep, cotangent,
    o_left, o_out, o_dz, o_dx,
    w_front, w_back, w_in, zx, extra, dz, du, dx, hidden, cell, stage_a, stage_b, stage_z,
    block_send, block_recv, block_local,
    u_send, u_recv, z_send, z_recv, dz_send, dz_recv, du_send, du_recv,
    bulk_send, bulk_recv, part_send, part_recv, dx_send, dx_recv, local_sem,
):
    o_hp_one, o_u, o_hp_two = (o_left.at[:, :, pl.ds(start, WIDE)] for start in (HP_ONE, U_TWO, HP_TWO))
    o_dz_one, o_dz_two = o_dz.at[0], o_dz.at[1]
    pipe = lax.axis_index("pipe")
    dp = lax.axis_index("dp")
    dp_count = lax.axis_size("dp")
    dp_far = lax.rem(dp + dp_count // 2, dp_count)

    barrier = pltpu.get_barrier_semaphore()
    for step in range(1, 4):
        pl.semaphore_signal(
            barrier, inc=1, device_id={"pipe": lax.rem(pipe + step, 4), "dp": dp}, device_id_type=MESH
        )
    for step in range(4):
        pl.semaphore_signal(
            barrier, inc=1, device_id={"pipe": lax.rem(pipe + step, 4), "dp": dp_far}, device_id_type=MESH
        )
    pl.semaphore_wait(barrier, 7)

    o_left[:, :, pl.ds(SOURCE, SOURCE_WIDE)] = source[...].reshape(CHUNKS, 2 * ROWS, SOURCE_WIDE)

    blocks = {
        W_ONE: w_one, R_ONE: r_one, R_TWO: r_two, W_TWO: w_two,
        R_ONE_T: r_one_t, R_TWO_T: r_two_t, W_TWO_T: w_two_t, W_ONE_T: w_one_t,
    }

    def landing(kind, p):
        if kind == W_ONE:
            return w_in.at[p]
        if kind in (R_ONE, R_TWO, W_TWO):
            return w_front.at[p]
        if kind == W_ONE_T:
            return w_front.at[p, :, pl.ds(0, 512)]
        return w_back.at[p]

    def block_copies(kind, p):
        user = USER[kind]
        source_ref, target = blocks[kind], landing(kind, p)
        if p == user:
            return [pltpu.make_async_copy(source_ref, target, block_local.at[kind])]
        if p // 2 == user // 2:
            return [
                pltpu.make_async_remote_copy(
                    source_ref, target, block_send.at[kind, 0], block_recv.at[kind, p, 0],
                    device_id={"pipe": user, "dp": dp}, device_id_type=MESH,
                )
            ]
        rows = source_ref.shape[0] // 2
        return [
            pltpu.make_async_remote_copy(
                source_ref.at[pl.ds(part * rows, rows)], target.at[pl.ds(part * rows, rows)],
                block_send.at[kind, part], block_recv.at[kind, p, part],
                device_id={"pipe": user, "dp": (dp, dp_far)[part]}, device_id_type=MESH,
            )
            for part in range(2)
        ]

    def start_blocks(kinds, p):
        for kind in kinds:
            for copy in block_copies(kind, p):
                copy.start()

    def finish_blocks(kinds, p):
        for kind in kinds:
            if p != USER[kind]:
                for copy in block_copies(kind, p):
                    copy.wait_send()

    def await_blocks(kind):
        for p in range(4):
            for copy in block_copies(kind, p):
                if p == USER[kind]:
                    copy.wait()
                else:
                    copy.wait_recv()

    def to(pipe_to, source_ref, target, send, recv):
        return pltpu.make_async_remote_copy(
            source_ref, target, send, recv,
            device_id={"pipe": pipe_to, "dp": dp}, device_id_type=MESH,
        )

    def copy_u(c):
        return to(BETWEEN, o_u.at[c], o_u.at[c], u_send, u_recv.at[c])

    def copy_z(c):
        return to(LAYER_TWO, zx.at[c], zx.at[c], z_send, z_recv.at[c])

    def copy_dz(pipe_to, c):
        return to(pipe_to, dz.at[:, c], dz.at[:, c], dz_send, dz_recv.at[c])

    def copy_du(c):
        return to(LAYER_ONE, du.at[c], du.at[c], du_send, du_recv.at[c])

    def copy_part(pipe_to, output, group, slot, gate):
        span = pl.ds(group * GROUP, GROUP)
        return to(pipe_to, dz.at[gate, span], output.at[span], part_send.at[slot], part_recv.at[group])

    def copy_dx(pipe_to, group, slot):
        span = pl.ds(group * GROUP, GROUP)
        return to(
            pipe_to, dx.at[span, :, pl.ds(pipe_to * 128, 128)], o_dx.at[span], dx_send.at[slot], dx_recv.at[group]
        )

    def copy_bulk(pipe_to, ref, slot, which):
        return to(pipe_to, ref, ref, bulk_send.at[slot], bulk_recv.at[which])

    def keep_rows(c, j):
        return jnp.broadcast_to(keep[c, ROWS * j : ROWS * j + ROWS, 0:1], (ROWS, WIDE))

    def clear():
        hidden[...] = jnp.zeros_like(hidden)
        cell[...] = jnp.zeros_like(cell)

    def forward_pair(c, mask, with_one, o_hp, o_layer):
        column = lax.broadcasted_iota(jnp.int32, (ROWS, WIDE), 1)
        for j in range(2):
            rows = pl.ds(ROWS * j, ROWS)
            kept = keep_rows(c, j)
            hidden_prev = hidden[...] * kept
            cell_prev = cell[...] * kept
            left = hidden_prev.astype(jnp.bfloat16)
            gates = [
                dot(left, w_front[g]) + zx[c, rows, pl.ds(g * WIDE, WIDE)] for g in range(4)
            ]
            gate_in, gate_forget = sigmoid(gates[0]), sigmoid(gates[1])
            gate_cand, gate_out = jnp.tanh(gates[2]), sigmoid(gates[3])
            cell_now = gate_forget * cell_prev + gate_in * gate_cand
            cell_tanh = jnp.tanh(cell_now)
            hidden_now = (gate_out * cell_tanh).astype(jnp.bfloat16).astype(jnp.float32)
            cell[...] = cell_now
            hidden[...] = hidden_now
            stage_a[rows, :] = hidden_prev
            layer = hidden_now * mask
            if with_one:
                layer = jnp.where(column == HID, 1.0, layer)
            stage_b[rows, :] = layer
            zx[c, rows, pl.ds(0, WIDE)] = gate_cand * gate_in * (1.0 - gate_in)
            zx[c, rows, pl.ds(WIDE, WIDE)] = cell_prev * gate_forget * (1.0 - gate_forget)
            zx[c, rows, pl.ds(2 * WIDE, WIDE)] = gate_in * (1.0 - gate_cand * gate_cand)
            zx[c, rows, pl.ds(3 * WIDE, WIDE)] = cell_tanh * gate_out * (1.0 - gate_out)
            extra[c, rows, pl.ds(0, WIDE)] = gate_out * (1.0 - cell_tanh * cell_tanh)
            extra[c, rows, pl.ds(WIDE, WIDE)] = gate_forget * kept
        o_hp[c] = stage_a[...].astype(jnp.bfloat16)
        o_layer[c] = stage_b[...].astype(jnp.bfloat16)

    def backward_pair(c, mask, upstream):
        above = upstream[c].astype(jnp.float32)
        for j in (1, 0):
            rows = pl.ds(ROWS * j, ROWS)
            total = hidden[...] + above[ROWS * j : ROWS * j + ROWS] * mask
            out_grad = total * zx[c, rows, pl.ds(3 * WIDE, WIDE)]
            cell_total = cell[...] + total * extra[c, rows, pl.ds(0, WIDE)]
            cell[...] = cell_total * extra[c, rows, pl.ds(WIDE, WIDE)]
            grads = [cell_total * zx[c, rows, pl.ds(g * WIDE, WIDE)] for g in range(3)] + [out_grad]
            back = None
            for g in range(4):
                stage_z[rows, pl.ds(g * WIDE, WIDE)] = grads[g]
                part = dot(grads[g].astype(jnp.bfloat16), w_back[g])
                back = part if back is None else back + part
            hidden[...] = back * keep_rows(c, j)
        for g in range(4):
            dz[g, c] = stage_z[:, pl.ds(g * WIDE, WIDE)].astype(jnp.bfloat16)

    last = CHUNKS - 1
    groups = CHUNKS // GROUP

    @pl.when(pipe == LAYER_ONE)
    def _():
        me = LAYER_ONE
        start_blocks(FORWARD, me)
        await_blocks(W_ONE)
        for g in range(4):
            zx[:, :, pl.ds(g * WIDE, WIDE)] = dot(source[:, :D_WIDE], w_in[g]).reshape(CHUNKS, 2 * ROWS, WIDE)
        await_blocks(R_ONE)
        start_blocks(BACKWARD, me)
        clear()

        def ahead(c, carry):
            forward_pair(c, layer_keep[0], True, o_hp_one, o_u)
            copy_u(c).start()
            return carry

        lax.fori_loop(0, CHUNKS, ahead, 0)
        bulk = [
            copy_bulk(SOURCE_GRAD, o_u, 0, 0), copy_bulk(LAYER_TWO, o_u, 1, 0),
            copy_bulk(SOURCE_GRAD, o_hp_one, 2, 1), copy_bulk(LAYER_TWO, o_hp_one, 3, 1),
            copy_bulk(BETWEEN, o_hp_one, 4, 1),
        ]
        for copy in bulk:
            copy.start()
        await_blocks(R_ONE_T)
        clear()

        def behind(i, carry):
            c = last - i
            copy_du(c).wait_recv()
            backward_pair(c, layer_keep[0], du)
            copy_dz(SOURCE_GRAD, c).start()

            @pl.when(lax.rem(c, GROUP) == 0)
            def _():
                group = c // GROUP
                copy_part(LAYER_TWO, o_dz_one, group, 0, LAYER_TWO).start()
                copy_part(BETWEEN, o_dz_one, group, 1, BETWEEN).start()

            return carry

        lax.fori_loop(0, CHUNKS, behind, 0)
        own = pltpu.make_async_copy(dz.at[me], o_dz_one, local_sem.at[0])
        own.start()
        finish_blocks(FORWARD + BACKWARD, me)
        to(BETWEEN, o_u, o_u, u_send, u_recv.at[0]).wait_send()
        for copy in bulk:
            copy.wait_send()
        to(SOURCE_GRAD, dz, dz, dz_send, dz_recv.at[0]).wait_send()
        to(LAYER_TWO, dz.at[me], o_dz_one, part_send.at[0], part_recv.at[0]).wait_send()
        to(BETWEEN, dz.at[me], o_dz_one, part_send.at[1], part_recv.at[0]).wait_send()
        own.wait()

        copy_bulk(me, o_hp_two, 0, 2).wait_recv()
        for group in range(groups):
            copy_part(me, o_dz_two, group, 0, me).wait_recv()
            copy_dx(me, group, 0).wait_recv()

    @pl.when(pipe == LAYER_TWO)
    def _():
        me = LAYER_TWO
        start_blocks(FORWARD, me)
        await_blocks(R_TWO)
        start_blocks(BACKWARD, me)
        clear()

        def ahead(c, carry):
            copy_z(c).wait_recv()
            forward_pair(c, layer_keep[1], False, o_hp_two, o_out)
            return carry

        lax.fori_loop(0, CHUNKS, ahead, 0)
        bulk = [
            copy_bulk(LAYER_ONE, o_hp_two, 0, 2), copy_bulk(SOURCE_GRAD, o_hp_two, 1, 2),
            copy_bulk(BETWEEN, o_hp_two, 2, 2), copy_bulk(BETWEEN, o_out, 3, 3),
        ]
        for copy in bulk:
            copy.start()
        await_blocks(R_TWO_T)
        clear()

        def behind(i, carry):
            c = last - i
            backward_pair(c, layer_keep[1], cotangent)
            copy_dz(BETWEEN, c).start()

            @pl.when(lax.rem(c, GROUP) == 0)
            def _():
                group = c // GROUP
                copy_part(LAYER_ONE, o_dz_two, group, 0, LAYER_ONE).start()
                copy_part(SOURCE_GRAD, o_dz_two, group, 1, SOURCE_GRAD).start()

            return carry

        lax.fori_loop(0, CHUNKS, behind, 0)
        own = pltpu.make_async_copy(dz.at[me], o_dz_two, local_sem.at[0])
        own.start()
        finish_blocks(FORWARD + BACKWARD, me)
        for copy in bulk:
            copy.wait_send()
        to(BETWEEN, dz, dz, dz_send, dz_recv.at[0]).wait_send()
        to(LAYER_ONE, dz.at[me], o_dz_two, part_send.at[0], part_recv.at[0]).wait_send()
        to(SOURCE_GRAD, dz.at[me], o_dz_two, part_send.at[1], part_recv.at[0]).wait_send()
        own.wait()

        copy_bulk(me, o_u, 0, 0).wait_recv()
        copy_bulk(me, o_hp_one, 0, 1).wait_recv()
        for group in range(groups):
            copy_part(me, o_dz_one, group, 0, me).wait_recv()
            copy_dx(me, group, 0).wait_recv()

    @pl.when(pipe == BETWEEN)
    def _():
        me = BETWEEN
        start_blocks(FORWARD, me)
        await_blocks(W_TWO)
        start_blocks(BACKWARD, me)

        def ahead(c, carry):
            copy_u(c).wait_recv()
            for g in range(4):
                zx[c, :, pl.ds(g * WIDE, WIDE)] = dot(o_u[c], w_front[g])
            copy_z(c).start()
            return carry

        lax.fori_loop(0, CHUNKS, ahead, 0)
        await_blocks(W_TWO_T)

        def behind(i, carry):
            c = last - i
            copy_dz(me, c).wait_recv()
            back = None
            for g in range(4):
                part = dot(dz[g, c], w_back[g])
                back = part if back is None else back + part
            du[c] = back.astype(jnp.bfloat16)
            copy_du(c).start()
            return carry

        lax.fori_loop(0, CHUNKS, behind, 0)
        own = pltpu.make_async_copy(dz.at[me], o_dz_two, local_sem.at[0])
        own.start()
        finish_blocks(FORWARD + BACKWARD, me)
        to(LAYER_TWO, zx, zx, z_send, z_recv.at[0]).wait_send()
        to(LAYER_ONE, du, du, du_send, du_recv.at[0]).wait_send()
        own.wait()

        copy_bulk(me, o_hp_one, 0, 1).wait_recv()
        copy_bulk(me, o_hp_two, 0, 2).wait_recv()
        copy_bulk(me, o_out, 0, 3).wait_recv()
        for group in range(groups):
            copy_part(me, o_dz_one, group, 0, me).wait_recv()
            copy_dx(me, group, 0).wait_recv()

    @pl.when(pipe == SOURCE_GRAD)
    def _():
        me = SOURCE_GRAD
        start_blocks(FORWARD, me)
        finish_blocks(FORWARD, me)
        start_blocks(BACKWARD, me)
        await_blocks(W_ONE_T)

        def behind(i, carry):
            c = last - i
            copy_dz(me, c).wait_recv()
            back = None
            for g in range(4):
                part = dot(dz[g, c], w_front[g, :, :512])
                back = part if back is None else back + part
            dx[c] = back

            @pl.when(lax.rem(c, GROUP) == 0)
            def _():
                group = c // GROUP
                copy_dx(LAYER_ONE, group, 0).start()
                copy_dx(LAYER_TWO, group, 1).start()
                copy_dx(BETWEEN, group, 2).start()

            return carry

        lax.fori_loop(0, CHUNKS, behind, 0)
        own = pltpu.make_async_copy(dz.at[me], o_dz_one, local_sem.at[0])
        own.start()
        own_dx = pltpu.make_async_copy(dx.at[:, :, pl.ds(me * 128, 128)], o_dx, local_sem.at[1])
        own_dx.start()
        finish_blocks(BACKWARD, me)
        for slot, pipe_to in enumerate((LAYER_ONE, LAYER_TWO, BETWEEN)):
            to(pipe_to, o_dx, o_dx, dx_send.at[slot], dx_recv.at[0]).wait_send()
        own.wait()
        own_dx.wait()

        copy_bulk(me, o_u, 0, 0).wait_recv()
        copy_bulk(me, o_hp_one, 0, 1).wait_recv()
        copy_bulk(me, o_hp_two, 0, 2).wait_recv()
        for group in range(groups):
            copy_part(me, o_dz_two, group, 0, me).wait_recv()


def relay(blocks, source, keep, layer_keep, cotangent):
    whole = pl.BlockSpec(memory_space=pltpu.VMEM)
    rows = (CHUNKS, 2 * ROWS, WIDE)
    half, full = jnp.bfloat16, jnp.float32
    shapes = [
        jax.ShapeDtypeStruct((CHUNKS, 2 * ROWS, UNITS * UNIT), half),
        jax.ShapeDtypeStruct(rows, half),
        jax.ShapeDtypeStruct((2,) + rows, half),
        jax.ShapeDtypeStruct((CHUNKS, 2 * ROWS, 128), full),
    ]
    dma = pltpu.SemaphoreType.DMA
    return pl.pallas_call(
        relay_kernel,
        out_shape=shapes,
        in_specs=[pl.BlockSpec(memory_space=pl.ANY)] * 8 + [whole] * 4,
        out_specs=[whole] * 4,
        scratch_shapes=[
            pltpu.VMEM((4, WIDE, WIDE), half),
            pltpu.VMEM((4, WIDE, WIDE), half),
            pltpu.VMEM((4, D_WIDE, WIDE), half),
            pltpu.VMEM((CHUNKS, 2 * ROWS, 4 * WIDE), full),
            pltpu.VMEM((CHUNKS, 2 * ROWS, 2 * WIDE), full),
            pltpu.VMEM((4,) + rows, half),
            pltpu.VMEM(rows, half),
            pltpu.VMEM((CHUNKS, 2 * ROWS, 512), full),
            pltpu.VMEM((ROWS, WIDE), full),
            pltpu.VMEM((ROWS, WIDE), full),
            pltpu.VMEM((2 * ROWS, WIDE), full),
            pltpu.VMEM((2 * ROWS, WIDE), full),
            pltpu.VMEM((2 * ROWS, 4 * WIDE), full),
            dma((8, 2)), dma((8, 4, 2)), dma((8,)),
            dma, dma((CHUNKS,)), dma, dma((CHUNKS,)), dma, dma((CHUNKS,)), dma, dma((CHUNKS,)),
            dma((5,)), dma((4,)), dma((2,)), dma((CHUNKS // GROUP,)), dma((3,)), dma((CHUNKS // GROUP,)), dma((2,)),
        ],
        compiler_params=pltpu.CompilerParams(
            vmem_limit_bytes=60 << 20, collective_id=0, has_side_effects=True
        ),
        name="relay",
    )(*blocks, source, keep, layer_keep, cotangent)


def reduce_kernel(
    left, dz, total, own, near, far, part, cross,
    near_send, near_recv, far_send, far_recv, part_send, part_recv, last_send, last_recv,
    cross_send, cross_recv, back_send, back_recv, wide_send, wide_recv,
):
    pipe = lax.axis_index("pipe")
    dp = lax.axis_index("dp")
    z, x, y = dp // 16, lax.rem(dp // 4, 4), lax.rem(dp, 4)

    def device(z_, x_, y_):
        return {"pipe": pipe, "dp": z_ * 16 + lax.rem(x_ + 4, 4) * 4 + lax.rem(y_ + 4, 4)}

    first = (lambda d: device(z, x + d, y), lambda d: device(z, x, y + d))
    second = (lambda d: device(z, x, y + d), lambda d: device(z, x + d, y))
    across = device(1 - z, x, y)
    place = ((x, y), (y, x))

    barrier = pltpu.get_barrier_semaphore()
    for target in (first[0](1), first[0](-1), first[1](1), first[1](-1), across):
        pl.semaphore_signal(barrier, inc=1, device_id=target, device_id_type=MESH)
    pl.semaphore_wait(barrier, 5)

    def unit(p, block, rel):
        a, b = place[p]
        return p * 16 + lax.rem(a + block + 4, 4) * 4 + lax.rem(b + rel, 4)

    def send(source, target, s, r, to):
        return pltpu.make_async_remote_copy(source, target, s, r, device_id=to, device_id_type=MESH)

    rows_of = (pl.ds(0, UNIT), pl.ds(0, HALF_UNIT), pl.ds(HALF_UNIT, HALF_UNIT))

    def add(index, others, start=0, count=UNIT):
        def body(i, carry):
            rows = pl.ds(pl.multiple_of(start + i * 16, 16), 16)
            value = own[index, rows].astype(jnp.float32)
            for ref in others:
                value = value + ref[rows].astype(jnp.float32)
            own[index, rows] = value.astype(jnp.bfloat16)
            return carry

        lax.fori_loop(0, count // 16, body, 0)

    def product(p, block, rel):
        u = unit(p, block, rel)
        columns = pl.ds(pl.multiple_of(u * UNIT, UNIT), UNIT)
        which = jnp.where(u < SWITCH, 0, 1)
        own[u] = lax.dot_general(
            left[:, columns], dz[which], (((0,), (0,)), ((), ())), preferred_element_type=jnp.float32
        ).astype(jnp.bfloat16)

    RIGHT, LEFT = (2, 1), (3, 0)
    side = {1: RIGHT, -1: LEFT}
    pairs = [(p, d) for d in (1, -1) for p in (0, 1)]
    slot = {1: 0, -1: 1}

    def near_copy(p, d, k):
        rel = side[d][k]
        return send(own.at[unit(p, 2, rel)], near.at[p, slot[d], k], near_send.at[p, slot[d], k],
                    near_recv.at[p, slot[d], k], first[p](d))

    def far_copy(p, d, k):
        rel = (side[-d] + side[d])[k]
        return send(own.at[unit(p, d, rel)], far.at[p, slot[d], rel], far_send.at[p, slot[d], k],
                    far_recv.at[p, slot[d], rel], first[p](d))

    def far_arrival(p, d, rel):
        return send(own.at[unit(p, 0, rel)], far.at[p, slot[d], rel], far_send.at[p, slot[d], 0],
                    far_recv.at[p, slot[d], rel], first[p](d))

    started = []

    def go(copy):
        copy.start()
        started.append(copy)

    for k in range(2):
        for p, d in pairs:
            product(p, 2, side[d][k])
            go(near_copy(p, d, k))
    for k in range(2):
        for p, d in pairs:
            product(p, d, side[-d][k])
            go(far_copy(p, d, k))
    for k in range(2):
        for p, d in pairs:
            product(p, d, side[d][k])
    for p in (0, 1):
        for rel in range(4):
            product(p, 0, rel)
    for k in range(2):
        for p, d in pairs:
            near_copy(p, d, k).wait_recv()
            add(unit(p, d, side[d][k]), [near.at[p, slot[d], k]])
            go(far_copy(p, d, 2 + k))

    def collect(p, rel):
        for d in (1, -1):
            far_arrival(p, d, rel).wait_recv()
        add(unit(p, 0, rel), [far.at[p, 0, rel], far.at[p, 1, rel]])

    def part_copy(p, d):
        rows = rows_of[1 if d == 1 else 2]
        return send(own.at[unit(p, 0, 2), rows], part.at[p, slot[d], rows], part_send.at[p, slot[d]],
                    part_recv.at[p, slot[d]], second[p](d))

    def last_copy(p, d, k):
        rel = 1 if d == 1 else 3
        half = (2 - k) if d == 1 else (1 + k)
        rows = rows_of[half]
        return send(own.at[unit(p, 0, rel), rows], part.at[p, 2 + slot[d], rows], last_send.at[p, slot[d], k],
                    last_recv.at[p, slot[d], k], second[p](d))

    for p in (0, 1):
        collect(p, 2)
        for d in (1, -1):
            go(part_copy(p, d))
    for rel, d in ((3, -1), (1, 1)):
        for p in (0, 1):
            collect(p, rel)
            go(last_copy(p, d, 0))
    for p in (0, 1):
        collect(p, 0)
    for d in (1, -1):
        for p in (0, 1):
            part_copy(p, d).wait_recv()
            rel = 1 if d == 1 else 3
            add(unit(p, 0, rel), [part.at[p, slot[d]]], 0 if d == 1 else HALF_UNIT, HALF_UNIT)
            go(last_copy(p, d, 1))

    def cross_copy(p):
        return send(own.at[unit(p, 0, 0)], cross.at[p], cross_send.at[p], cross_recv.at[p], across)

    for p in (0, 1):
        for d in (1, -1):
            for k in range(2):
                last_copy(p, d, k).wait_recv()
        add(unit(p, 0, 0), [part.at[p, 2], part.at[p, 3]])
        go(cross_copy(p))

    def back_copy(p, d):
        u = unit(p, 0, 0)
        return send(total.at[u], total.at[u], back_send.at[p, slot[d], 0], back_recv.at[p, slot[d], 0], second[p](d))

    def back_arrival(p, d):
        u = unit(p, 0, -d % 4)
        return send(total.at[u], total.at[u], back_send.at[p, slot[d], 0], back_recv.at[p, slot[d], 0], second[p](d))

    def back_on(p, d):
        u = unit(p, 0, -d % 4)
        rows = rows_of[1 if d == 1 else 2]
        return send(total.at[u, rows], total.at[u, rows], back_send.at[p, slot[d], 1], back_recv.at[p, slot[d], 1],
                    second[p](d))

    def back_on_arrival(p, d):
        u = unit(p, 0, 2)
        rows = rows_of[1 if d == 1 else 2]
        return send(total.at[u, rows], total.at[u, rows], back_send.at[p, slot[d], 1], back_recv.at[p, slot[d], 1],
                    second[p](d))

    def wide_copy(p, d, rel):
        u = unit(p, 0, rel)
        return send(total.at[u], total.at[u], wide_send.at[p, slot[d], rel], wide_recv.at[p, slot[d], rel], first[p](d))

    def wide_arrival(p, d, rel):
        u = unit(p, -d % 4, rel)
        return send(total.at[u], total.at[u], wide_send.at[p, slot[d], rel], wide_recv.at[p, slot[d], rel], first[p](d))

    ON = {1: (0, 1), -1: (3, 2)}

    def wide_on(p, d, k):
        u = unit(p, -d % 4, ON[d][k])
        return send(total.at[u], total.at[u], wide_send.at[p, slot[d], 4 + k], wide_recv.at[p, slot[d], 4 + k], first[p](d))

    def wide_on_arrival(p, d, k):
        u = unit(p, 2, ON[d][k])
        return send(total.at[u], total.at[u], wide_send.at[p, slot[d], 4 + k], wide_recv.at[p, slot[d], 4 + k], first[p](d))

    for p in (0, 1):
        cross_copy(p).wait_recv()
        u = unit(p, 0, 0)

        def body(i, carry):
            rows = pl.ds(pl.multiple_of(i * 16, 16), 16)
            value = own[u, rows].astype(jnp.float32) + cross[p, rows].astype(jnp.float32)
            total[u, rows] = value.astype(jnp.bfloat16)
            return carry

        lax.fori_loop(0, UNIT // 16, body, 0)
        for d in (1, -1):
            go(back_copy(p, d))
        for d in (1, -1):
            go(wide_copy(p, d, 0))
    for d in (1, -1):
        for p in (0, 1):
            back_arrival(p, d).wait_recv()
            go(back_on(p, d))
            for e in (1, -1):
                go(wide_copy(p, e, -d % 4))
    for p in (0, 1):
        for d in (1, -1):
            back_on_arrival(p, d).wait_recv()
        for d in (1, -1):
            go(wide_copy(p, d, 2))
    for k in range(2):
        for d in (1, -1):
            for p in (0, 1):
                wide_arrival(p, d, ON[d][k]).wait_recv()
                go(wide_on(p, d, k))
    for p in (0, 1):
        for d in (1, -1):
            for rel in range(4):
                if rel not in ON[d]:
                    wide_arrival(p, d, rel).wait_recv()
            for k in range(2):
                wide_on_arrival(p, d, k).wait_recv()
    for copy in started:
        copy.wait_send()


def reduce_over_dp(left, dz):
    whole = pl.BlockSpec(memory_space=pltpu.VMEM)
    half = jnp.bfloat16
    dma = pltpu.SemaphoreType.DMA
    return pl.pallas_call(
        reduce_kernel,
        out_shape=jax.ShapeDtypeStruct((UNITS, UNIT, WIDE), half),
        in_specs=[whole] * 2,
        out_specs=whole,
        scratch_shapes=[
            pltpu.VMEM((UNITS, UNIT, WIDE), half),
            pltpu.VMEM((2, 2, 2, UNIT, WIDE), half),
            pltpu.VMEM((2, 2, 4, UNIT, WIDE), half),
            pltpu.VMEM((2, 4, UNIT, WIDE), half),
            pltpu.VMEM((2, UNIT, WIDE), half),
            dma((2, 2, 2)), dma((2, 2, 2)), dma((2, 2, 4)), dma((2, 2, 4)), dma((2, 2)), dma((2, 2)),
            dma((2, 2, 2)), dma((2, 2, 2)), dma((2,)), dma((2,)), dma((2, 2, 2)), dma((2, 2, 2)),
            dma((2, 2, 6)), dma((2, 2, 6)),
        ],
        compiler_params=pltpu.CompilerParams(
            vmem_limit_bytes=60 << 20, collective_id=1, has_side_effects=True
        ),
        name="reduce",
    )(left, dz)


def prepare_kernel(
    w_one, bias_one, r_one, drop_one, w_two, bias_two, r_two, drop_two,
    o_w_one, o_r_one, o_r_two, o_w_two, o_r_one_t, o_r_two_t, o_w_two_t, o_w_one_t,
    square, small, apart,
):
    column = pl.program_id(0) * UNIT + lax.broadcasted_iota(jnp.int32, (WIDE, UNIT), 1)
    inside = column < HID

    def finish(o_plain, o_turned, turned_rows):
        value = jnp.where(inside, square[...], 0.0)
        o_plain[...] = value.astype(jnp.bfloat16)
        row = lax.broadcasted_iota(jnp.int32, (WIDE, UNIT), 0)
        if turned_rows < WIDE:
            value = jnp.where(row < turned_rows, value, 0.0)
        o_turned[...] = value.T.astype(jnp.bfloat16)

    square[...] = jnp.zeros_like(square)
    for weights, drop, o_plain, o_turned in (
        (r_one, drop_one, o_r_one, o_r_one_t), (r_two, drop_two, o_r_two, o_r_two_t),
    ):
        square[:HID, :] = weights[...].astype(jnp.float32) * drop[...].astype(jnp.float32) * weight_scale
        finish(o_plain, o_turned, WIDE)
    square[:HID, :] = w_two[...].astype(jnp.float32)
    square[HID : HID + 1, :] = bias_two[...].astype(jnp.float32)
    finish(o_w_two, o_w_two_t, HID)

    w_one_f = w_one[...].astype(jnp.float32)
    small[...] = jnp.zeros_like(small)
    small[:D_IN, :] = w_one_f
    small[D_IN : D_IN + 1, :] = bias_one[...].astype(jnp.float32)
    o_w_one[...] = jnp.where(inside[:D_WIDE], small[...], 0.0).astype(jnp.bfloat16)
    apart[...] = jnp.zeros_like(apart)
    for q in range(4):
        apart[q * UNIT : q * UNIT + 100, :] = small[q * 100 : q * 100 + 100, :]
    o_w_one_t[...] = jnp.where(inside[:512], apart[...], 0.0).T.astype(jnp.bfloat16)


def prepare(w_one, bias_one, r_one, drop_one, w_two, bias_two, r_two, drop_two):
    half = jnp.bfloat16

    def slab(rows):
        return pl.BlockSpec((rows, UNIT), lambda j: (0, j))

    def turned(columns):
        return pl.BlockSpec((UNIT, columns), lambda j: (j, 0))

    square = jax.ShapeDtypeStruct((WIDE, WIDE), half)
    return pl.pallas_call(
        prepare_kernel,
        grid=(WIDE // UNIT,),
        in_specs=[slab(D_IN), slab(1), slab(HID), slab(HID), slab(HID), slab(1), slab(HID), slab(HID)],
        out_specs=[slab(D_WIDE)] + [slab(WIDE)] * 3 + [turned(WIDE)] * 3 + [turned(512)],
        out_shape=[jax.ShapeDtypeStruct((D_WIDE, WIDE), half)] + [square] * 6
        + [jax.ShapeDtypeStruct((WIDE, 512), half)],
        scratch_shapes=[
            pltpu.VMEM((WIDE, UNIT), jnp.float32), pltpu.VMEM((D_WIDE, UNIT), jnp.float32),
            pltpu.VMEM((512, UNIT), jnp.float32),
        ],
        compiler_params=pltpu.CompilerParams(vmem_limit_bytes=32 << 20),
        name="prepare",
    )(w_one, bias_one[None], r_one, drop_one, w_two, bias_two[None], r_two, drop_two)


def padded(array, rows, columns):
    return jnp.pad(array, ((0, rows - array.shape[0]), (0, columns - array.shape[1])))


def by_time(array):
    ordered = jnp.transpose(array, (2, 0, 1, 3))
    return ordered.reshape(CHUNKS, 2 * ROWS, array.shape[3])


def local(
    inputs, resets, in_mask, mid_mask, out_mask,
    w_ih_one, w_hh_one, bias_one, drop_one, w_ih_two, w_hh_two, bias_two, drop_two, cotangent,
):
    pipe = lax.axis_index("pipe")
    blocks = prepare(w_ih_one, bias_one, w_hh_one, drop_one, w_ih_two, bias_two, w_hh_two, drop_two)
    keep_in = in_mask.astype(jnp.float32) * keep_scale
    source = by_time((inputs * keep_in[:, :, None, :]).astype(jnp.bfloat16)).reshape(STEPS * ROWS, D_IN)
    ones = jnp.ones((STEPS * ROWS, 1), jnp.bfloat16)
    source = padded(jnp.concatenate([source, ones], 1), STEPS * ROWS, SOURCE_WIDE)
    positions = jnp.arange(STEPS, dtype=jnp.int32)
    keep = (resets.reshape(1, ROWS) != positions[:, None]).astype(jnp.float32)
    keep = jnp.broadcast_to(keep.reshape(CHUNKS, 2 * ROWS, 1), (CHUNKS, 2 * ROWS, 128))
    layer_keep = jnp.stack([mid_mask.reshape(ROWS, HID), out_mask.reshape(ROWS, HID)]).astype(jnp.float32)
    layer_keep = jnp.pad(layer_keep * keep_scale, ((0, 0), (0, 0), (0, WIDE - HID)))
    cot = jnp.pad(by_time(cotangent), ((0, 0), (0, 0), (0, WIDE - HID)))

    left, out_two, dz, dx = relay(blocks, source, keep, layer_keep, cot)
    left = left.reshape(STEPS * ROWS, UNITS * UNIT)
    total = reduce_over_dp(left, dz.reshape(2, STEPS * ROWS, WIDE)).reshape(UNITS * UNIT, WIDE)

    u_two = left[:, U_TWO : U_TWO + WIDE].reshape(out_two.shape)
    layer = jnp.where(pipe < 2, u_two, out_two).reshape(STEPS, 2, 2, WIDE)[..., :HID]
    layer = lax.dynamic_index_in_dim(layer, pipe % 2, 1, keepdims=False)
    layer_outputs = jnp.swapaxes(layer, 0, 1)[None]
    grad_input = jnp.transpose(dx.reshape(STEPS, 2, 2, 128)[..., :100], (1, 2, 0, 3))
    keep_part = lax.dynamic_slice_in_dim(keep_in, pipe * 100, 100, 2)
    grad_input = grad_input * keep_part[:, :, None, :]

    def grads(start, rows):
        return total[start : start + rows, :HID].astype(jnp.float32)

    return (
        layer_outputs,
        grad_input,
        grads(SOURCE, D_IN),
        grads(HP_ONE, HID) * drop_one.astype(jnp.float32) * weight_scale,
        grads(SOURCE + D_IN, 1)[0],
        grads(U_TWO, HID),
        grads(HP_TWO, HID) * drop_two.astype(jnp.float32) * weight_scale,
        grads(U_TWO + HID, 1)[0],
    )


def solution(mesh):
    placed = (
        P(None, "dp", None, None),
        P(None, "dp"),
        P(None, "dp", None),
        P(None, "dp", None),
        P(None, "dp", None),
        P(None, "pipe"),
        P(None, "pipe"),
        P("pipe"),
        P(None, "pipe"),
        P(None, "pipe"),
        P(None, "pipe"),
        P("pipe"),
        P(None, "pipe"),
        P(None, "dp", None, None),
    )
    return jax.shard_map(
        local,
        mesh=mesh,
        in_specs=placed,
        out_specs=(
            P("pipe", "dp", None, None),
            P(None, "dp", None, "pipe"),
            P(None, "pipe"),
            P(None, "pipe"),
            P("pipe"),
            P(None, "pipe"),
            P(None, "pipe"),
            P("pipe"),
        ),
        check_vma=False,
    )
```

```python
import functools

import jax
import jax.numpy as jnp
from jax import lax
from jax.experimental import pallas as pl
from jax.experimental.pallas import tpu as pltpu
from jax.sharding import PartitionSpec as P

MESH = pl.DeviceIdType.MESH
HID = 1150
WIDE = 1152
D_IN = 400
D_WIDE = 416
STEPS = 88
ROWS = 4
CHUNKS = 44
GROUP = 4
LATER = 3
TURNS = 36
UNIT = 128
HALF_UNIT = 64
UNITS = 32
HP_ONE, SOURCE, U_TWO, HP_TWO = 0, 1152, 1792, 2944
SOURCE_WIDE = 640
SWITCH = 14

keep_scale = 4.0 / 3.0
weight_scale = 2.0

LAYER_ONE, SOURCE_GRAD, LAYER_TWO, BETWEEN = 0, 1, 2, 3
W_ONE, R_ONE, R_TWO, W_TWO, R_ONE_T, R_TWO_T, W_TWO_T, W_ONE_T = range(8)
USER = {
    W_ONE: LAYER_ONE,
    R_ONE: LAYER_ONE,
    R_TWO: LAYER_TWO,
    W_TWO: BETWEEN,
    R_ONE_T: LAYER_ONE,
    R_TWO_T: LAYER_TWO,
    W_TWO_T: BETWEEN,
    W_ONE_T: SOURCE_GRAD,
}
FORWARD = (W_ONE,)
BACKWARD = (R_TWO_T, W_TWO_T, R_ONE_T, W_ONE_T)


def sigmoid(value):
    return 0.5 * jnp.tanh(0.5 * value) + 0.5


def dot(left, right):
    return jnp.dot(left, right, preferred_element_type=jnp.float32)


def relay_kernel(
    w_one, r_one, r_two, w_two, r_one_t, r_two_t, w_two_t, w_one_t,
    source, keep, layer_keep, cotangent,
    o_left, o_out, o_dz, o_dx,
    w_front, w_back, w_in, zx, extra, dz, du, dx, hidden, cell, stage_a, stage_b, stage_z,
    block_send, block_recv, block_local, cross_send, cross_recv, ring_send, ring_recv, go_on,
    u_send, u_recv, z_send, z_recv, dz_send, dz_recv, du_send, du_recv,
    bulk_send, bulk_recv, part_send, part_recv, dx_send, dx_recv, local_sem,
):
    o_hp_one, o_u, o_hp_two = (o_left.at[:, :, pl.ds(start, WIDE)] for start in (HP_ONE, U_TWO, HP_TWO))
    o_dz_one, o_dz_two = o_dz.at[0], o_dz.at[1]
    pipe = lax.axis_index("pipe")
    dp = lax.axis_index("dp")
    dp_count = lax.axis_size("dp")
    dp_far = lax.rem(dp + dp_count // 2, dp_count)

    barrier = pltpu.get_barrier_semaphore()
    for step in range(1, 4):
        pl.semaphore_signal(
            barrier, inc=1, device_id={"pipe": lax.rem(pipe + step, 4), "dp": dp}, device_id_type=MESH
        )
    for step in range(4):
        pl.semaphore_signal(
            barrier, inc=1, device_id={"pipe": lax.rem(pipe + step, 4), "dp": dp_far}, device_id_type=MESH
        )
    z, x, y = dp // 16, lax.rem(dp // 4, 4), lax.rem(dp, 4)
    rings = (
        lambda d: {"pipe": pipe, "dp": z * 16 + lax.rem(x + d + 4, 4) * 4 + y},
        lambda d: {"pipe": pipe, "dp": z * 16 + x * 4 + lax.rem(y + d + 4, 4)},
    )
    for ring in rings:
        for d in (1, -1):
            pl.semaphore_signal(barrier, inc=1, device_id=ring(d), device_id_type=MESH)
    pl.semaphore_wait(barrier, 11)

    o_left[:, :, pl.ds(SOURCE, SOURCE_WIDE)] = source[...].reshape(CHUNKS, 2 * ROWS, SOURCE_WIDE)

    blocks = {
        W_ONE: w_one, R_ONE: r_one, R_TWO: r_two, W_TWO: w_two,
        R_ONE_T: r_one_t, R_TWO_T: r_two_t, W_TWO_T: w_two_t, W_ONE_T: w_one_t,
    }

    def landing(kind, p):
        if kind == W_ONE:
            return w_in.at[p]
        if kind in (R_ONE, R_TWO, W_TWO):
            return w_front.at[p]
        if kind == W_ONE_T:
            return w_front.at[p, :, pl.ds(0, 512)]
        return w_back.at[p]

    def block_copies(kind, p, turn=None):
        user = USER[kind]
        source_ref, target = blocks[kind], landing(kind, p)
        if p == user:
            return [pltpu.make_async_copy(source_ref, target, block_local.at[kind])]
        if p // 2 == user // 2:
            return [
                pltpu.make_async_remote_copy(
                    source_ref, target, block_send.at[kind, 0], block_recv.at[kind, p, 0],
                    device_id={"pipe": user, "dp": dp}, device_id_type=MESH,
                )
            ]
        rows = source_ref.shape[0] // 2
        if turn is None:
            spans = [pl.ds(part * rows, rows) for part in range(2)]
        else:
            piece = rows // TURNS
            spans = [pl.ds(pl.multiple_of(part * rows + turn * piece, piece), piece) for part in range(2)]
        return [
            pltpu.make_async_remote_copy(
                source_ref.at[spans[part]], target.at[spans[part]],
                block_send.at[kind, part], block_recv.at[kind, p, part],
                device_id={"pipe": user, "dp": (dp, dp_far)[part]}, device_id_type=MESH,
            )
            for part in range(2)
        ]

    def rows_at(first, count=UNIT):
        return pl.ds(pl.multiple_of(first, 64), count)

    def part_rows(ring, step):
        place = (x, y)[ring]
        return UNIT * (1 + 4 * ring + lax.rem(place + step + 4, 4))

    def from_other_plane(kind):
        return [p for p in range(4) if p // 2 != USER[kind] // 2]

    def cross_copy(kind, p, k, slot):
        rows = rows_at((part_rows(0, 0), part_rows(1, 0), 0)[k])
        return pltpu.make_async_remote_copy(
            blocks[kind].at[rows], w_front.at[p, rows], cross_send.at[slot, k], cross_recv.at[p % 2, k],
            device_id={"pipe": USER[kind], "dp": (dp, dp_far)[p % 2]}, device_id_type=MESH,
        )

    def ring_copy(p, ring, d, on):
        k = 2 * on + (0 if d == 1 else 1)
        if on:
            rows = rows_at(part_rows(ring, -d) + (0 if d == 1 else HALF_UNIT), HALF_UNIT)
        else:
            rows = rows_at(part_rows(ring, 0))
        ref = w_front.at[p, rows]
        return pltpu.make_async_remote_copy(
            ref, ref, ring_send.at[p % 2, ring, k], ring_recv.at[p % 2, ring, k],
            device_id=rings[ring](d), device_id_type=MESH,
        )

    def ring_arrival(p, ring, d, on):
        k = 2 * on + (0 if d == 1 else 1)
        if on:
            rows = rows_at(part_rows(ring, 2) + (0 if d == 1 else HALF_UNIT), HALF_UNIT)
        else:
            rows = rows_at(part_rows(ring, -d))
        ref = w_front.at[p, rows]
        return pltpu.make_async_remote_copy(
            ref, ref, ring_send.at[p % 2, ring, k], ring_recv.at[p % 2, ring, k],
            device_id=rings[ring](d), device_id_type=MESH,
        )

    SPREAD = (W_TWO, R_TWO, R_ONE)

    def start_spread(me):
        kinds = [kind for kind in SPREAD if me // 2 != USER[kind] // 2]
        for k in range(3):
            for slot, kind in enumerate(kinds):
                cross_copy(kind, me, k, slot).start()
        for kind in SPREAD:
            if me // 2 == USER[kind] // 2:
                block_copies(kind, me)[0].start()

    def finish_spread(me):
        kinds = [kind for kind in SPREAD if me // 2 != USER[kind] // 2]
        for slot, kind in enumerate(kinds):
            for k in range(3):
                cross_copy(kind, me, k, slot).wait_send()
        for kind in SPREAD:
            if me // 2 == USER[kind] // 2 and me != USER[kind]:
                block_copies(kind, me)[0].wait_send()

    def receive_spread(kind):
        me = USER[kind]
        others = from_other_plane(kind)
        for ring in range(2):
            for p in others:
                cross_copy(kind, p, ring, 0).wait_recv()
                for d in (1, -1):
                    ring_copy(p, ring, d, 0).start()
        for d in (1, -1):
            for p in others:
                for ring in range(2):
                    ring_arrival(p, ring, d, 0).wait_recv()
                    ring_copy(p, ring, d, 1).start()
        for p in others:
            cross_copy(kind, p, 2, 0).wait_recv()
            for ring in range(2):
                for d in (1, -1):
                    ring_arrival(p, ring, d, 1).wait_recv()
        for p in (me, me ^ 1):
            copy = block_copies(kind, p)[0]
            if p == me:
                copy.wait()
            else:
                copy.wait_recv()

    def finish_rings(kind):
        for p in from_other_plane(kind):
            for ring in range(2):
                for d in (1, -1):
                    for on in range(2):
                        ring_copy(p, ring, d, on).wait_send()

    def start_blocks(kinds, p):
        for kind in kinds:
            for copy in block_copies(kind, p):
                copy.start()

    def start_near(p):
        for kind in BACKWARD:
            if p // 2 == USER[kind] // 2:
                for copy in block_copies(kind, p):
                    copy.start()

    def start_turn(p, turn):
        for kind in BACKWARD:
            if p // 2 != USER[kind] // 2:
                for copy in block_copies(kind, p, turn):
                    copy.start()

    def finish_blocks(kinds, p):
        for kind in kinds:
            if p != USER[kind]:
                for copy in block_copies(kind, p):
                    copy.wait_send()

    def await_blocks(kind):
        for p in range(4):
            for copy in block_copies(kind, p):
                if p == USER[kind]:
                    copy.wait()
                else:
                    copy.wait_recv()

    def to(pipe_to, source_ref, target, send, recv):
        return pltpu.make_async_remote_copy(
            source_ref, target, send, recv,
            device_id={"pipe": pipe_to, "dp": dp}, device_id_type=MESH,
        )

    def copy_u(c):
        return to(BETWEEN, o_u.at[c], o_u.at[c], u_send, u_recv.at[c])

    def copy_z(c):
        return to(LAYER_TWO, zx.at[c], zx.at[c], z_send, z_recv.at[c])

    def copy_dz(pipe_to, c):
        return to(pipe_to, dz.at[:, c], dz.at[:, c], dz_send, dz_recv.at[c])

    def copy_du(c):
        return to(LAYER_ONE, du.at[c], du.at[c], du_send, du_recv.at[c])

    def copy_part(pipe_to, output, group, slot, gate):
        span = pl.ds(group * GROUP, GROUP)
        return to(pipe_to, dz.at[gate, span], output.at[span], part_send.at[slot], part_recv.at[group])

    def copy_dx(pipe_to, group, slot):
        span = pl.ds(group * GROUP, GROUP)
        return to(
            pipe_to, dx.at[span, :, pl.ds(pipe_to * 128, 128)], o_dx.at[span], dx_send.at[slot], dx_recv.at[group]
        )

    def copy_bulk(pipe_to, ref, slot, which):
        return to(pipe_to, ref, ref, bulk_send.at[slot], bulk_recv.at[which])

    def keep_rows(c, j):
        return jnp.broadcast_to(keep[c, ROWS * j : ROWS * j + ROWS, 0:1], (ROWS, WIDE))

    def clear():
        hidden[...] = jnp.zeros_like(hidden)
        cell[...] = jnp.zeros_like(cell)

    def forward_pair(c, mask, with_one, o_hp, o_layer):
        column = lax.broadcasted_iota(jnp.int32, (ROWS, WIDE), 1)
        for j in range(2):
            rows = pl.ds(ROWS * j, ROWS)
            kept = keep_rows(c, j)
            hidden_prev = hidden[...] * kept
            cell_prev = cell[...] * kept
            left = hidden_prev.astype(jnp.bfloat16)
            gates = [
                dot(left, w_front[g]) + zx[c, rows, pl.ds(g * WIDE, WIDE)] for g in range(4)
            ]
            gate_in, gate_forget = sigmoid(gates[0]), sigmoid(gates[1])
            gate_cand, gate_out = jnp.tanh(gates[2]), sigmoid(gates[3])
            cell_now = gate_forget * cell_prev + gate_in * gate_cand
            cell_tanh = jnp.tanh(cell_now)
            hidden_now = (gate_out * cell_tanh).astype(jnp.bfloat16).astype(jnp.float32)
            cell[...] = cell_now
            hidden[...] = hidden_now
            stage_a[rows, :] = hidden_prev
            layer = hidden_now * mask
            if with_one:
                layer = jnp.where(column == HID, 1.0, layer)
            stage_b[rows, :] = layer
            zx[c, rows, pl.ds(0, WIDE)] = gate_cand * gate_in * (1.0 - gate_in)
            zx[c, rows, pl.ds(WIDE, WIDE)] = cell_prev * gate_forget * (1.0 - gate_forget)
            zx[c, rows, pl.ds(2 * WIDE, WIDE)] = gate_in * (1.0 - gate_cand * gate_cand)
            zx[c, rows, pl.ds(3 * WIDE, WIDE)] = cell_tanh * gate_out * (1.0 - gate_out)
            extra[c, rows, pl.ds(0, WIDE)] = gate_out * (1.0 - cell_tanh * cell_tanh)
            extra[c, rows, pl.ds(WIDE, WIDE)] = gate_forget * kept
        o_hp[c] = stage_a[...].astype(jnp.bfloat16)
        o_layer[c] = stage_b[...].astype(jnp.bfloat16)

    def backward_pair(c, mask, upstream):
        above = upstream[c].astype(jnp.float32)
        for j in (1, 0):
            rows = pl.ds(ROWS * j, ROWS)
            total = hidden[...] + above[ROWS * j : ROWS * j + ROWS] * mask
            out_grad = total * zx[c, rows, pl.ds(3 * WIDE, WIDE)]
            cell_total = cell[...] + total * extra[c, rows, pl.ds(0, WIDE)]
            cell[...] = cell_total * extra[c, rows, pl.ds(WIDE, WIDE)]
            grads = [cell_total * zx[c, rows, pl.ds(g * WIDE, WIDE)] for g in range(3)] + [out_grad]
            back = None
            for g in range(4):
                stage_z[rows, pl.ds(g * WIDE, WIDE)] = grads[g]
                part = dot(grads[g].astype(jnp.bfloat16), w_back[g])
                back = part if back is None else back + part
            hidden[...] = back * keep_rows(c, j)
        for g in range(4):
            dz[g, c] = stage_z[:, pl.ds(g * WIDE, WIDE)].astype(jnp.bfloat16)

    last = CHUNKS - 1
    groups = CHUNKS // GROUP

    @pl.when(pipe == LAYER_ONE)
    def _():
        me = LAYER_ONE
        start_spread(me)
        start_blocks(FORWARD, me)
        await_blocks(W_ONE)
        for g in range(4):
            zx[:, :, pl.ds(g * WIDE, WIDE)] = dot(source[:, :D_WIDE], w_in[g]).reshape(CHUNKS, 2 * ROWS, WIDE)
        receive_spread(R_ONE)
        clear()

        def ahead(c, carry):
            forward_pair(c, layer_keep[0], True, o_hp_one, o_u)
            copy_u(c).start()

            @pl.when((c >= LATER) & (c < LATER + TURNS))
            def _():
                pl.semaphore_signal(
                    go_on, inc=1, device_id={"pipe": SOURCE_GRAD, "dp": dp}, device_id_type=MESH
                )
                start_turn(me, c - LATER)

            @pl.when(c == LATER)
            def _():
                start_near(me)

            return carry

        lax.fori_loop(0, CHUNKS, ahead, 0)
        bulk = [
            copy_bulk(SOURCE_GRAD, o_u, 0, 0), copy_bulk(LAYER_TWO, o_u, 1, 0),
            copy_bulk(SOURCE_GRAD, o_hp_one, 2, 1), copy_bulk(LAYER_TWO, o_hp_one, 3, 1),
            copy_bulk(BETWEEN, o_hp_one, 4, 1),
        ]
        for copy in bulk:
            copy.start()
        await_blocks(R_ONE_T)
        clear()

        def behind(i, carry):
            c = last - i
            copy_du(c).wait_recv()
            backward_pair(c, layer_keep[0], du)
            copy_dz(SOURCE_GRAD, c).start()

            @pl.when(lax.rem(c, GROUP) == 0)
            def _():
                group = c // GROUP
                copy_part(LAYER_TWO, o_dz_one, group, 0, LAYER_TWO).start()
                copy_part(BETWEEN, o_dz_one, group, 1, BETWEEN).start()

            return carry

        lax.fori_loop(0, CHUNKS, behind, 0)
        own = pltpu.make_async_copy(dz.at[me], o_dz_one, local_sem.at[0])
        own.start()
        finish_rings(R_ONE)
        finish_spread(me)
        finish_blocks(FORWARD + BACKWARD, me)
        to(BETWEEN, o_u, o_u, u_send, u_recv.at[0]).wait_send()
        for copy in bulk:
            copy.wait_send()
        to(SOURCE_GRAD, dz, dz, dz_send, dz_recv.at[0]).wait_send()
        to(LAYER_TWO, dz.at[me], o_dz_one, part_send.at[0], part_recv.at[0]).wait_send()
        to(BETWEEN, dz.at[me], o_dz_one, part_send.at[1], part_recv.at[0]).wait_send()
        own.wait()

        copy_bulk(me, o_hp_two, 0, 2).wait_recv()
        for group in range(groups):
            copy_part(me, o_dz_two, group, 0, me).wait_recv()
            copy_dx(me, group, 0).wait_recv()

    @pl.when(pipe == LAYER_TWO)
    def _():
        me = LAYER_TWO
        start_spread(me)
        start_blocks(FORWARD, me)
        receive_spread(R_TWO)
        clear()

        def ahead(c, carry):
            copy_z(c).wait_recv()

            @pl.when((c >= LATER) & (c < LATER + TURNS))
            def _():
                start_turn(me, c - LATER)

            @pl.when(c == LATER)
            def _():
                start_near(me)

            forward_pair(c, layer_keep[1], False, o_hp_two, o_out)
            return carry

        lax.fori_loop(0, CHUNKS, ahead, 0)
        bulk = [
            copy_bulk(LAYER_ONE, o_hp_two, 0, 2), copy_bulk(SOURCE_GRAD, o_hp_two, 1, 2),
            copy_bulk(BETWEEN, o_hp_two, 2, 2), copy_bulk(BETWEEN, o_out, 3, 3),
        ]
        for copy in bulk:
            copy.start()
        await_blocks(R_TWO_T)
        clear()

        def behind(i, carry):
            c = last - i
            backward_pair(c, layer_keep[1], cotangent)
            copy_dz(BETWEEN, c).start()

            @pl.when(lax.rem(c, GROUP) == 0)
            def _():
                group = c // GROUP
                copy_part(LAYER_ONE, o_dz_two, group, 0, LAYER_ONE).start()
                copy_part(SOURCE_GRAD, o_dz_two, group, 1, SOURCE_GRAD).start()

            return carry

        lax.fori_loop(0, CHUNKS, behind, 0)
        own = pltpu.make_async_copy(dz.at[me], o_dz_two, local_sem.at[0])
        own.start()
        finish_rings(R_TWO)
        finish_spread(me)
        finish_blocks(FORWARD + BACKWARD, me)
        for copy in bulk:
            copy.wait_send()
        to(BETWEEN, dz, dz, dz_send, dz_recv.at[0]).wait_send()
        to(LAYER_ONE, dz.at[me], o_dz_two, part_send.at[0], part_recv.at[0]).wait_send()
        to(SOURCE_GRAD, dz.at[me], o_dz_two, part_send.at[1], part_recv.at[0]).wait_send()
        own.wait()

        copy_bulk(me, o_u, 0, 0).wait_recv()
        copy_bulk(me, o_hp_one, 0, 1).wait_recv()
        for group in range(groups):
            copy_part(me, o_dz_one, group, 0, me).wait_recv()
            copy_dx(me, group, 0).wait_recv()

    @pl.when(pipe == BETWEEN)
    def _():
        me = BETWEEN
        start_spread(me)
        start_blocks(FORWARD, me)
        receive_spread(W_TWO)

        def ahead(c, carry):
            copy_u(c).wait_recv()
            for g in range(4):
                zx[c, :, pl.ds(g * WIDE, WIDE)] = dot(o_u[c], w_front[g])
            copy_z(c).start()

            @pl.when((c >= LATER) & (c < LATER + TURNS))
            def _():
                start_turn(me, c - LATER)

            @pl.when(c == LATER)
            def _():
                start_near(me)

            return carry

        lax.fori_loop(0, CHUNKS, ahead, 0)
        await_blocks(W_TWO_T)

        def behind(i, carry):
            c = last - i
            copy_dz(me, c).wait_recv()
            back = None
            for g in range(4):
                part = dot(dz[g, c], w_back[g])
                back = part if back is None else back + part
            du[c] = back.astype(jnp.bfloat16)
            copy_du(c).start()
            return carry

        lax.fori_loop(0, CHUNKS, behind, 0)
        own = pltpu.make_async_copy(dz.at[me], o_dz_two, local_sem.at[0])
        own.start()
        finish_rings(W_TWO)
        finish_spread(me)
        finish_blocks(FORWARD + BACKWARD, me)
        to(LAYER_TWO, zx, zx, z_send, z_recv.at[0]).wait_send()
        to(LAYER_ONE, du, du, du_send, du_recv.at[0]).wait_send()
        own.wait()

        copy_bulk(me, o_hp_one, 0, 1).wait_recv()
        copy_bulk(me, o_hp_two, 0, 2).wait_recv()
        copy_bulk(me, o_out, 0, 3).wait_recv()
        for group in range(groups):
            copy_part(me, o_dz_one, group, 0, me).wait_recv()
            copy_dx(me, group, 0).wait_recv()

    @pl.when(pipe == SOURCE_GRAD)
    def _():
        me = SOURCE_GRAD
        start_spread(me)
        start_blocks(FORWARD, me)

        def pass_on(turn, carry):
            pl.semaphore_wait(go_on, 1)
            start_turn(me, turn)
            return carry

        lax.fori_loop(0, TURNS, pass_on, 0)
        start_near(me)
        await_blocks(W_ONE_T)

        def behind(i, carry):
            c = last - i
            copy_dz(me, c).wait_recv()
            back = None
            for g in range(4):
                part = dot(dz[g, c], w_front[g, :, :512])
                back = part if back is None else back + part
            dx[c] = back

            @pl.when(lax.rem(c, GROUP) == 0)
            def _():
                group = c // GROUP
                copy_dx(LAYER_ONE, group, 0).start()
                copy_dx(LAYER_TWO, group, 1).start()
                copy_dx(BETWEEN, group, 2).start()

            return carry

        lax.fori_loop(0, CHUNKS, behind, 0)
        own = pltpu.make_async_copy(dz.at[me], o_dz_one, local_sem.at[0])
        own.start()
        own_dx = pltpu.make_async_copy(dx.at[:, :, pl.ds(me * 128, 128)], o_dx, local_sem.at[1])
        own_dx.start()
        finish_spread(me)
        finish_blocks(FORWARD + BACKWARD, me)
        for slot, pipe_to in enumerate((LAYER_ONE, LAYER_TWO, BETWEEN)):
            to(pipe_to, o_dx, o_dx, dx_send.at[slot], dx_recv.at[0]).wait_send()
        own.wait()
        own_dx.wait()

        copy_bulk(me, o_u, 0, 0).wait_recv()
        copy_bulk(me, o_hp_one, 0, 1).wait_recv()
        copy_bulk(me, o_hp_two, 0, 2).wait_recv()
        for group in range(groups):
            copy_part(me, o_dz_two, group, 0, me).wait_recv()


def relay(blocks, source, keep, layer_keep, cotangent):
    whole = pl.BlockSpec(memory_space=pltpu.VMEM)
    rows = (CHUNKS, 2 * ROWS, WIDE)
    half, full = jnp.bfloat16, jnp.float32
    shapes = [
        jax.ShapeDtypeStruct((CHUNKS, 2 * ROWS, UNITS * UNIT), half),
        jax.ShapeDtypeStruct(rows, half),
        jax.ShapeDtypeStruct((2,) + rows, half),
        jax.ShapeDtypeStruct((CHUNKS, 2 * ROWS, 128), full),
    ]
    dma = pltpu.SemaphoreType.DMA
    return pl.pallas_call(
        relay_kernel,
        out_shape=shapes,
        in_specs=[pl.BlockSpec(memory_space=pl.ANY)] * 8 + [whole] * 4,
        out_specs=[whole] * 4,
        scratch_shapes=[
            pltpu.VMEM((4, WIDE, WIDE), half),
            pltpu.VMEM((4, WIDE, WIDE), half),
            pltpu.VMEM((4, D_WIDE, WIDE), half),
            pltpu.VMEM((CHUNKS, 2 * ROWS, 4 * WIDE), full),
            pltpu.VMEM((CHUNKS, 2 * ROWS, 2 * WIDE), full),
            pltpu.VMEM((4,) + rows, half),
            pltpu.VMEM(rows, half),
            pltpu.VMEM((CHUNKS, 2 * ROWS, 512), full),
            pltpu.VMEM((ROWS, WIDE), full),
            pltpu.VMEM((ROWS, WIDE), full),
            pltpu.VMEM((2 * ROWS, WIDE), full),
            pltpu.VMEM((2 * ROWS, WIDE), full),
            pltpu.VMEM((2 * ROWS, 4 * WIDE), full),
            dma((8, 2)), dma((8, 4, 2)), dma((8,)),
            dma((2, 3)), dma((2, 3)), dma((2, 2, 4)), dma((2, 2, 4)), pltpu.SemaphoreType.REGULAR,
            dma, dma((CHUNKS,)), dma, dma((CHUNKS,)), dma, dma((CHUNKS,)), dma, dma((CHUNKS,)),
            dma((5,)), dma((4,)), dma((2,)), dma((CHUNKS // GROUP,)), dma((3,)), dma((CHUNKS // GROUP,)), dma((2,)),
        ],
        compiler_params=pltpu.CompilerParams(
            vmem_limit_bytes=60 << 20, collective_id=0, has_side_effects=True
        ),
        name="relay",
    )(*blocks, source, keep, layer_keep, cotangent)


def reduce_kernel(
    left, dz, total, own, near, far, part, cross,
    near_send, near_recv, far_send, far_recv, part_send, part_recv, last_send, last_recv,
    cross_send, cross_recv, back_send, back_recv, wide_send, wide_recv,
):
    pipe = lax.axis_index("pipe")
    dp = lax.axis_index("dp")
    z, x, y = dp // 16, lax.rem(dp // 4, 4), lax.rem(dp, 4)

    def device(z_, x_, y_):
        return {"pipe": pipe, "dp": z_ * 16 + lax.rem(x_ + 4, 4) * 4 + lax.rem(y_ + 4, 4)}

    first = (lambda d: device(z, x + d, y), lambda d: device(z, x, y + d))
    second = (lambda d: device(z, x, y + d), lambda d: device(z, x + d, y))
    across = device(1 - z, x, y)
    place = ((x, y), (y, x))

    barrier = pltpu.get_barrier_semaphore()
    for target in (first[0](1), first[0](-1), first[1](1), first[1](-1), across):
        pl.semaphore_signal(barrier, inc=1, device_id=target, device_id_type=MESH)
    pl.semaphore_wait(barrier, 5)

    def unit(p, block, rel):
        a, b = place[p]
        return p * 16 + lax.rem(a + block + 4, 4) * 4 + lax.rem(b + rel, 4)

    def send(source, target, s, r, to):
        return pltpu.make_async_remote_copy(source, target, s, r, device_id=to, device_id_type=MESH)

    rows_of = (pl.ds(0, UNIT), pl.ds(0, HALF_UNIT), pl.ds(HALF_UNIT, HALF_UNIT))

    def add(index, others, start=0, count=UNIT):
        def body(i, carry):
            rows = pl.ds(pl.multiple_of(start + i * 16, 16), 16)
            value = own[index, rows].astype(jnp.float32)
            for ref in others:
                value = value + ref[rows].astype(jnp.float32)
            own[index, rows] = value.astype(jnp.bfloat16)
            return carry

        lax.fori_loop(0, count // 16, body, 0)

    def product(p, block, rel):
        u = unit(p, block, rel)
        columns = pl.ds(pl.multiple_of(u * UNIT, UNIT), UNIT)
        which = jnp.where(u < SWITCH, 0, 1)
        own[u] = lax.dot_general(
            left[:, columns], dz[which], (((0,), (0,)), ((), ())), preferred_element_type=jnp.float32
        ).astype(jnp.bfloat16)

    RIGHT, LEFT = (2, 1), (3, 0)
    side = {1: RIGHT, -1: LEFT}
    pairs = [(p, d) for d in (1, -1) for p in (0, 1)]
    slot = {1: 0, -1: 1}

    def near_copy(p, d, k):
        rel = side[d][k]
        return send(own.at[unit(p, 2, rel)], near.at[p, slot[d], k], near_send.at[p, slot[d], k],
                    near_recv.at[p, slot[d], k], first[p](d))

    def far_copy(p, d, k):
        rel = (side[-d] + side[d])[k]
        return send(own.at[unit(p, d, rel)], far.at[p, slot[d], rel], far_send.at[p, slot[d], k],
                    far_recv.at[p, slot[d], rel], first[p](d))

    def far_arrival(p, d, rel):
        return send(own.at[unit(p, 0, rel)], far.at[p, slot[d], rel], far_send.at[p, slot[d], 0],
                    far_recv.at[p, slot[d], rel], first[p](d))

    started = []

    def go(copy):
        copy.start()
        started.append(copy)

    for k in range(2):
        for p, d in pairs:
            product(p, 2, side[d][k])
            go(near_copy(p, d, k))
    for k in range(2):
        for p, d in pairs:
            product(p, d, side[-d][k])
            go(far_copy(p, d, k))
    for k in range(2):
        for p, d in pairs:
            product(p, d, side[d][k])
    for p in (0, 1):
        for rel in range(4):
            product(p, 0, rel)
    for k in range(2):
        for p, d in pairs:
            near_copy(p, d, k).wait_recv()
            add(unit(p, d, side[d][k]), [near.at[p, slot[d], k]])
            go(far_copy(p, d, 2 + k))

    def collect(p, rel):
        for d in (1, -1):
            far_arrival(p, d, rel).wait_recv()
        add(unit(p, 0, rel), [far.at[p, 0, rel], far.at[p, 1, rel]])

    def part_copy(p, d):
        rows = rows_of[1 if d == 1 else 2]
        return send(own.at[unit(p, 0, 2), rows], part.at[p, slot[d], rows], part_send.at[p, slot[d]],
                    part_recv.at[p, slot[d]], second[p](d))

    def last_copy(p, d, k):
        rel = 1 if d == 1 else 3
        half = (2 - k) if d == 1 else (1 + k)
        rows = rows_of[half]
        return send(own.at[unit(p, 0, rel), rows], part.at[p, 2 + slot[d], rows], last_send.at[p, slot[d], k],
                    last_recv.at[p, slot[d], k], second[p](d))

    for p in (0, 1):
        collect(p, 2)
        for d in (1, -1):
            go(part_copy(p, d))
    for rel, d in ((3, -1), (1, 1)):
        for p in (0, 1):
            collect(p, rel)
            go(last_copy(p, d, 0))
    for p in (0, 1):
        collect(p, 0)
    for d in (1, -1):
        for p in (0, 1):
            part_copy(p, d).wait_recv()
            rel = 1 if d == 1 else 3
            add(unit(p, 0, rel), [part.at[p, slot[d]]], 0 if d == 1 else HALF_UNIT, HALF_UNIT)
            go(last_copy(p, d, 1))

    def cross_copy(p):
        return send(own.at[unit(p, 0, 0)], cross.at[p], cross_send.at[p], cross_recv.at[p], across)

    for p in (0, 1):
        for d in (1, -1):
            for k in range(2):
                last_copy(p, d, k).wait_recv()
        add(unit(p, 0, 0), [part.at[p, 2], part.at[p, 3]])
        go(cross_copy(p))

    def back_copy(p, d):
        u = unit(p, 0, 0)
        return send(total.at[u], total.at[u], back_send.at[p, slot[d], 0], back_recv.at[p, slot[d], 0], second[p](d))

    def back_arrival(p, d):
        u = unit(p, 0, -d % 4)
        return send(total.at[u], total.at[u], back_send.at[p, slot[d], 0], back_recv.at[p, slot[d], 0], second[p](d))

    def back_on(p, d):
        u = unit(p, 0, -d % 4)
        rows = rows_of[1 if d == 1 else 2]
        return send(total.at[u, rows], total.at[u, rows], back_send.at[p, slot[d], 1], back_recv.at[p, slot[d], 1],
                    second[p](d))

    def back_on_arrival(p, d):
        u = unit(p, 0, 2)
        rows = rows_of[1 if d == 1 else 2]
        return send(total.at[u, rows], total.at[u, rows], back_send.at[p, slot[d], 1], back_recv.at[p, slot[d], 1],
                    second[p](d))

    def wide_copy(p, d, rel):
        u = unit(p, 0, rel)
        return send(total.at[u], total.at[u], wide_send.at[p, slot[d], rel], wide_recv.at[p, slot[d], rel], first[p](d))

    def wide_arrival(p, d, rel):
        u = unit(p, -d % 4, rel)
        return send(total.at[u], total.at[u], wide_send.at[p, slot[d], rel], wide_recv.at[p, slot[d], rel], first[p](d))

    ON = {1: (0, 1), -1: (3, 2)}

    def wide_on(p, d, k):
        u = unit(p, -d % 4, ON[d][k])
        return send(total.at[u], total.at[u], wide_send.at[p, slot[d], 4 + k], wide_recv.at[p, slot[d], 4 + k], first[p](d))

    def wide_on_arrival(p, d, k):
        u = unit(p, 2, ON[d][k])
        return send(total.at[u], total.at[u], wide_send.at[p, slot[d], 4 + k], wide_recv.at[p, slot[d], 4 + k], first[p](d))

    for p in (0, 1):
        cross_copy(p).wait_recv()
        u = unit(p, 0, 0)

        def body(i, carry):
            rows = pl.ds(pl.multiple_of(i * 16, 16), 16)
            value = own[u, rows].astype(jnp.float32) + cross[p, rows].astype(jnp.float32)
            total[u, rows] = value.astype(jnp.bfloat16)
            return carry

        lax.fori_loop(0, UNIT // 16, body, 0)
        for d in (1, -1):
            go(back_copy(p, d))
        for d in (1, -1):
            go(wide_copy(p, d, 0))
    for d in (1, -1):
        for p in (0, 1):
            back_arrival(p, d).wait_recv()
            go(back_on(p, d))
            for e in (1, -1):
                go(wide_copy(p, e, -d % 4))
    for p in (0, 1):
        for d in (1, -1):
            back_on_arrival(p, d).wait_recv()
        for d in (1, -1):
            go(wide_copy(p, d, 2))
    for k in range(2):
        for d in (1, -1):
            for p in (0, 1):
                wide_arrival(p, d, ON[d][k]).wait_recv()
                go(wide_on(p, d, k))
    for p in (0, 1):
        for d in (1, -1):
            for rel in range(4):
                if rel not in ON[d]:
                    wide_arrival(p, d, rel).wait_recv()
            for k in range(2):
                wide_on_arrival(p, d, k).wait_recv()
    for copy in started:
        copy.wait_send()


def reduce_over_dp(left, dz):
    whole = pl.BlockSpec(memory_space=pltpu.VMEM)
    half = jnp.bfloat16
    dma = pltpu.SemaphoreType.DMA
    return pl.pallas_call(
        reduce_kernel,
        out_shape=jax.ShapeDtypeStruct((UNITS, UNIT, WIDE), half),
        in_specs=[whole] * 2,
        out_specs=whole,
        scratch_shapes=[
            pltpu.VMEM((UNITS, UNIT, WIDE), half),
            pltpu.VMEM((2, 2, 2, UNIT, WIDE), half),
            pltpu.VMEM((2, 2, 4, UNIT, WIDE), half),
            pltpu.VMEM((2, 4, UNIT, WIDE), half),
            pltpu.VMEM((2, UNIT, WIDE), half),
            dma((2, 2, 2)), dma((2, 2, 2)), dma((2, 2, 4)), dma((2, 2, 4)), dma((2, 2)), dma((2, 2)),
            dma((2, 2, 2)), dma((2, 2, 2)), dma((2,)), dma((2,)), dma((2, 2, 2)), dma((2, 2, 2)),
            dma((2, 2, 6)), dma((2, 2, 6)),
        ],
        compiler_params=pltpu.CompilerParams(
            vmem_limit_bytes=60 << 20, collective_id=1, has_side_effects=True
        ),
        name="reduce",
    )(left, dz)


def prepare_kernel(
    w_one, bias_one, r_one, drop_one, w_two, bias_two, r_two, drop_two,
    o_w_one, o_r_one, o_r_two, o_w_two, o_r_one_t, o_r_two_t, o_w_two_t, o_w_one_t,
    square, small, apart,
):
    column = pl.program_id(0) * UNIT + lax.broadcasted_iota(jnp.int32, (WIDE, UNIT), 1)
    inside = column < HID

    def finish(o_plain, o_turned, turned_rows):
        value = jnp.where(inside, square[...], 0.0)
        o_plain[...] = value.astype(jnp.bfloat16)
        row = lax.broadcasted_iota(jnp.int32, (WIDE, UNIT), 0)
        if turned_rows < WIDE:
            value = jnp.where(row < turned_rows, value, 0.0)
        o_turned[...] = value.T.astype(jnp.bfloat16)

    square[...] = jnp.zeros_like(square)
    for weights, drop, o_plain, o_turned in (
        (r_one, drop_one, o_r_one, o_r_one_t), (r_two, drop_two, o_r_two, o_r_two_t),
    ):
        square[:HID, :] = weights[...].astype(jnp.float32) * drop[...].astype(jnp.float32) * weight_scale
        finish(o_plain, o_turned, WIDE)
    square[:HID, :] = w_two[...].astype(jnp.float32)
    square[HID : HID + 1, :] = bias_two[...].astype(jnp.float32)
    finish(o_w_two, o_w_two_t, HID)

    w_one_f = w_one[...].astype(jnp.float32)
    small[...] = jnp.zeros_like(small)
    small[:D_IN, :] = w_one_f
    small[D_IN : D_IN + 1, :] = bias_one[...].astype(jnp.float32)
    o_w_one[...] = jnp.where(inside[:D_WIDE], small[...], 0.0).astype(jnp.bfloat16)
    apart[...] = jnp.zeros_like(apart)
    for q in range(4):
        apart[q * UNIT : q * UNIT + 100, :] = small[q * 100 : q * 100 + 100, :]
    o_w_one_t[...] = jnp.where(inside[:512], apart[...], 0.0).T.astype(jnp.bfloat16)


def prepare(w_one, bias_one, r_one, drop_one, w_two, bias_two, r_two, drop_two):
    half = jnp.bfloat16

    def slab(rows):
        return pl.BlockSpec((rows, UNIT), lambda j: (0, j))

    def turned(columns):
        return pl.BlockSpec((UNIT, columns), lambda j: (j, 0))

    square = jax.ShapeDtypeStruct((WIDE, WIDE), half)
    return pl.pallas_call(
        prepare_kernel,
        grid=(WIDE // UNIT,),
        in_specs=[slab(D_IN), slab(1), slab(HID), slab(HID), slab(HID), slab(1), slab(HID), slab(HID)],
        out_specs=[slab(D_WIDE)] + [slab(WIDE)] * 3 + [turned(WIDE)] * 3 + [turned(512)],
        out_shape=[jax.ShapeDtypeStruct((D_WIDE, WIDE), half)] + [square] * 6
        + [jax.ShapeDtypeStruct((WIDE, 512), half)],
        scratch_shapes=[
            pltpu.VMEM((WIDE, UNIT), jnp.float32), pltpu.VMEM((D_WIDE, UNIT), jnp.float32),
            pltpu.VMEM((512, UNIT), jnp.float32),
        ],
        compiler_params=pltpu.CompilerParams(vmem_limit_bytes=60 << 20),
        name="prepare",
    )(w_one, bias_one[None], r_one, drop_one, w_two, bias_two[None], r_two, drop_two)


def padded(array, rows, columns):
    return jnp.pad(array, ((0, rows - array.shape[0]), (0, columns - array.shape[1])))


def by_time(array):
    ordered = jnp.transpose(array, (2, 0, 1, 3))
    return ordered.reshape(CHUNKS, 2 * ROWS, array.shape[3])


def local(
    inputs, resets, in_mask, mid_mask, out_mask,
    w_ih_one, w_hh_one, bias_one, drop_one, w_ih_two, w_hh_two, bias_two, drop_two, cotangent,
):
    pipe = lax.axis_index("pipe")
    blocks = prepare(w_ih_one, bias_one, w_hh_one, drop_one, w_ih_two, bias_two, w_hh_two, drop_two)
    keep_in = in_mask.astype(jnp.float32) * keep_scale
    source = by_time((inputs * keep_in[:, :, None, :]).astype(jnp.bfloat16)).reshape(STEPS * ROWS, D_IN)
    ones = jnp.ones((STEPS * ROWS, 1), jnp.bfloat16)
    source = padded(jnp.concatenate([source, ones], 1), STEPS * ROWS, SOURCE_WIDE)
    positions = jnp.arange(STEPS, dtype=jnp.int32)
    keep = (resets.reshape(1, ROWS) != positions[:, None]).astype(jnp.float32)
    keep = jnp.broadcast_to(keep.reshape(CHUNKS, 2 * ROWS, 1), (CHUNKS, 2 * ROWS, 128))
    layer_keep = jnp.stack([mid_mask.reshape(ROWS, HID), out_mask.reshape(ROWS, HID)]).astype(jnp.float32)
    layer_keep = jnp.pad(layer_keep * keep_scale, ((0, 0), (0, 0), (0, WIDE - HID)))
    cot = jnp.pad(by_time(cotangent), ((0, 0), (0, 0), (0, WIDE - HID)))

    left, out_two, dz, dx = relay(blocks, source, keep, layer_keep, cot)
    left = left.reshape(STEPS * ROWS, UNITS * UNIT)
    total = reduce_over_dp(left, dz.reshape(2, STEPS * ROWS, WIDE)).reshape(UNITS * UNIT, WIDE)

    u_two = left[:, U_TWO : U_TWO + WIDE].reshape(out_two.shape)
    layer = jnp.where(pipe < 2, u_two, out_two).reshape(STEPS, 2, 2, WIDE)[..., :HID]
    layer = lax.dynamic_index_in_dim(layer, pipe % 2, 1, keepdims=False)
    layer_outputs = jnp.swapaxes(layer, 0, 1)[None]
    grad_input = jnp.transpose(dx.reshape(STEPS, 2, 2, 128)[..., :100], (1, 2, 0, 3))
    keep_part = lax.dynamic_slice_in_dim(keep_in, pipe * 100, 100, 2)
    grad_input = grad_input * keep_part[:, :, None, :]

    def grads(start, rows):
        return total[start : start + rows, :HID].astype(jnp.float32)

    return (
        layer_outputs,
        grad_input,
        grads(SOURCE, D_IN),
        grads(HP_ONE, HID) * drop_one.astype(jnp.float32) * weight_scale,
        grads(SOURCE + D_IN, 1)[0],
        grads(U_TWO, HID),
        grads(HP_TWO, HID) * drop_two.astype(jnp.float32) * weight_scale,
        grads(U_TWO + HID, 1)[0],
    )


def solution(mesh):
    placed = (
        P(None, "dp", None, None),
        P(None, "dp"),
        P(None, "dp", None),
        P(None, "dp", None),
        P(None, "dp", None),
        P(None, "pipe"),
        P(None, "pipe"),
        P("pipe"),
        P(None, "pipe"),
        P(None, "pipe"),
        P(None, "pipe"),
        P("pipe"),
        P(None, "pipe"),
        P(None, "dp", None, None),
    )
    return jax.shard_map(
        local,
        mesh=mesh,
        in_specs=placed,
        out_specs=(
            P("pipe", "dp", None, None),
            P(None, "dp", None, "pipe"),
            P(None, "pipe"),
            P(None, "pipe"),
            P("pipe"),
            P(None, "pipe"),
            P(None, "pipe"),
            P("pipe"),
        ),
        check_vma=False,
    )
```

```python
import functools

import jax
import jax.numpy as jnp
from jax import lax
from jax.experimental import pallas as pl
from jax.experimental.pallas import tpu as pltpu
from jax.sharding import PartitionSpec as P

MESH = pl.DeviceIdType.MESH
HID = 1150
WIDE = 1152
D_IN = 400
D_WIDE = 416
STEPS = 88
ROWS = 4
CHUNKS = 44
GROUP = 4
LATER = 3
TURNS = 36
UNIT = 128
HALF_UNIT = 64
UNITS = 32
HP_ONE, SOURCE, U_TWO, HP_TWO = 0, 1152, 1792, 2944
SOURCE_WIDE = 640
SWITCH = 14
BIG, SMALL = 96, 16
THIRD = 32 * BIG
SHARE = 32 * SMALL

keep_scale = 4.0 / 3.0
weight_scale = 2.0

LAYER_ONE, SOURCE_GRAD, LAYER_TWO, BETWEEN = 0, 1, 2, 3
W_ONE, R_ONE, R_TWO, W_TWO, R_ONE_T, R_TWO_T, W_TWO_T, W_ONE_T = range(8)
USER = {
    W_ONE: LAYER_ONE,
    R_ONE: LAYER_ONE,
    R_TWO: LAYER_TWO,
    W_TWO: BETWEEN,
    R_ONE_T: LAYER_ONE,
    R_TWO_T: LAYER_TWO,
    W_TWO_T: BETWEEN,
    W_ONE_T: SOURCE_GRAD,
}
FORWARD = (W_ONE,)
BACKWARD = (R_TWO_T, W_TWO_T, R_ONE_T, W_ONE_T)


def sigmoid(value):
    return 0.5 * jnp.tanh(0.5 * value) + 0.5


def dot(left, right):
    return jnp.dot(left, right, preferred_element_type=jnp.float32)


def relay_kernel(
    w_one, r_one, r_two, w_two, r_one_t, r_two_t, w_two_t, w_one_t,
    inputs, in_mask, mid_mask, out_mask, cotangent, resets,
    o_left, o_out, o_dz, o_dx,
    w_front, w_back, w_in, zx, extra, dz, du, dx, above, line, spread, keep, layer_keep, hidden, cell, stage_a, stage_b, stage_z,
    block_send, block_recv, block_local, cross_send, cross_recv, ring_send, ring_recv, go_on,
    u_send, u_recv, z_send, z_recv, dz_send, dz_recv, du_send, du_recv,
    bulk_send, bulk_recv, part_send, part_recv, dx_send, dx_recv, local_sem,
):
    o_hp_one, o_u, o_hp_two = (o_left.at[:, :, pl.ds(start, WIDE)] for start in (HP_ONE, U_TWO, HP_TWO))
    o_dz_one, o_dz_two = o_dz.at[0], o_dz.at[1]
    pipe = lax.axis_index("pipe")
    dp = lax.axis_index("dp")
    dp_count = lax.axis_size("dp")
    dp_far = lax.rem(dp + dp_count // 2, dp_count)

    barrier = pltpu.get_barrier_semaphore()
    for step in range(1, 4):
        pl.semaphore_signal(
            barrier, inc=1, device_id={"pipe": lax.rem(pipe + step, 4), "dp": dp}, device_id_type=MESH
        )
    for step in range(4):
        pl.semaphore_signal(
            barrier, inc=1, device_id={"pipe": lax.rem(pipe + step, 4), "dp": dp_far}, device_id_type=MESH
        )
    z, x, y = dp // 16, lax.rem(dp // 4, 4), lax.rem(dp, 4)
    rings = (
        lambda d: {"pipe": pipe, "dp": z * 16 + lax.rem(x + d + 4, 4) * 4 + y},
        lambda d: {"pipe": pipe, "dp": z * 16 + x * 4 + lax.rem(y + d + 4, 4)},
    )
    for ring in rings:
        for d in (1, -1):
            pl.semaphore_signal(barrier, inc=1, device_id=ring(d), device_id_type=MESH)
    pl.semaphore_wait(barrier, 11)

    blocks = {
        W_ONE: w_one, R_ONE: r_one, R_TWO: r_two, W_TWO: w_two,
        R_ONE_T: r_one_t, R_TWO_T: r_two_t, W_TWO_T: w_two_t, W_ONE_T: w_one_t,
    }

    def landing(kind, p):
        if kind == W_ONE:
            return w_in.at[p]
        if kind in (R_ONE, R_TWO, W_TWO):
            return w_front.at[p]
        if kind == W_ONE_T:
            return w_front.at[p, :, pl.ds(0, 512)]
        return w_back.at[p]

    def block_copies(kind, p, turn=None):
        user = USER[kind]
        source_ref, target = blocks[kind], landing(kind, p)
        if p == user:
            return [pltpu.make_async_copy(source_ref, target, block_local.at[kind])]
        if p // 2 == user // 2:
            return [
                pltpu.make_async_remote_copy(
                    source_ref, target, block_send.at[kind, 0], block_recv.at[kind, p, 0],
                    device_id={"pipe": user, "dp": dp}, device_id_type=MESH,
                )
            ]
        rows = source_ref.shape[0] // 2
        if turn is None:
            spans = [pl.ds(part * rows, rows) for part in range(2)]
        else:
            piece = rows // TURNS
            spans = [pl.ds(pl.multiple_of(part * rows + turn * piece, piece), piece) for part in range(2)]
        return [
            pltpu.make_async_remote_copy(
                source_ref.at[spans[part]], target.at[spans[part]],
                block_send.at[kind, part], block_recv.at[kind, p, part],
                device_id={"pipe": user, "dp": (dp, dp_far)[part]}, device_id_type=MESH,
            )
            for part in range(2)
        ]

    def rows_at(first, count=UNIT):
        return pl.ds(pl.multiple_of(first, 64), count)

    def part_rows(ring, step):
        place = (x, y)[ring]
        return UNIT * (1 + 4 * ring + lax.rem(place + step + 4, 4))

    def from_other_plane(kind):
        return [p for p in range(4) if p // 2 != USER[kind] // 2]

    def cross_copy(kind, p, k, slot):
        rows = rows_at((part_rows(0, 0), part_rows(1, 0), 0)[k])
        return pltpu.make_async_remote_copy(
            blocks[kind].at[rows], w_front.at[p, rows], cross_send.at[slot, k], cross_recv.at[p % 2, k],
            device_id={"pipe": USER[kind], "dp": (dp, dp_far)[p % 2]}, device_id_type=MESH,
        )

    def ring_copy(p, ring, d, on):
        k = 2 * on + (0 if d == 1 else 1)
        if on:
            rows = rows_at(part_rows(ring, -d) + (0 if d == 1 else HALF_UNIT), HALF_UNIT)
        else:
            rows = rows_at(part_rows(ring, 0))
        ref = w_front.at[p, rows]
        return pltpu.make_async_remote_copy(
            ref, ref, ring_send.at[p % 2, ring, k], ring_recv.at[p % 2, ring, k],
            device_id=rings[ring](d), device_id_type=MESH,
        )

    def ring_arrival(p, ring, d, on):
        k = 2 * on + (0 if d == 1 else 1)
        if on:
            rows = rows_at(part_rows(ring, 2) + (0 if d == 1 else HALF_UNIT), HALF_UNIT)
        else:
            rows = rows_at(part_rows(ring, -d))
        ref = w_front.at[p, rows]
        return pltpu.make_async_remote_copy(
            ref, ref, ring_send.at[p % 2, ring, k], ring_recv.at[p % 2, ring, k],
            device_id=rings[ring](d), device_id_type=MESH,
        )

    SPREAD = (W_TWO, R_TWO, R_ONE)

    def start_spread(me):
        kinds = [kind for kind in SPREAD if me // 2 != USER[kind] // 2]
        for k in range(3):
            for slot, kind in enumerate(kinds):
                cross_copy(kind, me, k, slot).start()
            if k == 1:
                start_blocks(FORWARD, me)
        for kind in SPREAD:
            if me // 2 == USER[kind] // 2:
                block_copies(kind, me)[0].start()

    def finish_spread(me):
        kinds = [kind for kind in SPREAD if me // 2 != USER[kind] // 2]
        for slot, kind in enumerate(kinds):
            for k in range(3):
                cross_copy(kind, me, k, slot).wait_send()
        for kind in SPREAD:
            if me // 2 == USER[kind] // 2 and me != USER[kind]:
                block_copies(kind, me)[0].wait_send()

    def share_blocks(kind):
        others = from_other_plane(kind)
        for ring in range(2):
            for p in others:
                cross_copy(kind, p, ring, 0).wait_recv()
                for d in (1, -1):
                    ring_copy(p, ring, d, 0).start()
        for d in (1, -1):
            for p in others:
                for ring in range(2):
                    ring_arrival(p, ring, d, 0).wait_recv()
                    ring_copy(p, ring, d, 1).start()

    def receive_rest(kind):
        me = USER[kind]
        others = from_other_plane(kind)
        for p in others:
            cross_copy(kind, p, 2, 0).wait_recv()
            for ring in range(2):
                for d in (1, -1):
                    ring_arrival(p, ring, d, 1).wait_recv()
        for p in (me, me ^ 1):
            copy = block_copies(kind, p)[0]
            if p == me:
                copy.wait()
            else:
                copy.wait_recv()

    def finish_rings(kind):
        for p in from_other_plane(kind):
            for ring in range(2):
                for d in (1, -1):
                    for on in range(2):
                        ring_copy(p, ring, d, on).wait_send()

    def start_blocks(kinds, p):
        for kind in kinds:
            for copy in block_copies(kind, p):
                copy.start()

    def start_near(p):
        for kind in BACKWARD:
            if p // 2 == USER[kind] // 2:
                for copy in block_copies(kind, p):
                    copy.start()

    def start_turn(p, turn):
        for kind in BACKWARD:
            if p // 2 != USER[kind] // 2:
                for copy in block_copies(kind, p, turn):
                    copy.start()

    def finish_blocks(kinds, p):
        for kind in kinds:
            if p != USER[kind]:
                for copy in block_copies(kind, p):
                    copy.wait_send()

    def await_blocks(kind):
        for p in range(4):
            for copy in block_copies(kind, p):
                if p == USER[kind]:
                    copy.wait()
                else:
                    copy.wait_recv()

    def to(pipe_to, source_ref, target, send, recv):
        return pltpu.make_async_remote_copy(
            source_ref, target, send, recv,
            device_id={"pipe": pipe_to, "dp": dp}, device_id_type=MESH,
        )

    def copy_u(c):
        return to(BETWEEN, o_u.at[c], o_u.at[c], u_send, u_recv.at[c])

    def copy_z(c):
        return to(LAYER_TWO, zx.at[c], zx.at[c], z_send, z_recv.at[c])

    def copy_dz(pipe_to, c):
        return to(pipe_to, dz.at[:, c], dz.at[:, c], dz_send, dz_recv.at[c])

    def copy_du(c):
        return to(LAYER_ONE, du.at[c], du.at[c], du_send, du_recv.at[c])

    def copy_part(pipe_to, output, group, slot, gate):
        span = pl.ds(group * GROUP, GROUP)
        return to(pipe_to, dz.at[gate, span], output.at[span], part_send.at[slot], part_recv.at[group])

    def copy_dx(pipe_to, group, slot):
        count = GROUP * 2 * ROWS
        span = pl.ds(pl.multiple_of(group * count, count), count)
        return to(
            pipe_to, dx.at[span, pl.ds(pipe_to * 128, 128)], o_dx.at[span], dx_send.at[slot], dx_recv.at[group]
        )

    def copy_bulk(pipe_to, ref, slot, which):
        return to(pipe_to, ref, ref, bulk_send.at[slot], bulk_recv.at[which])

    def keep_rows(c, j):
        return jnp.broadcast_to(keep[c, ROWS * j : ROWS * j + ROWS, 0:1], (ROWS, WIDE))

    def by_time(target, width, whole, value_of):
        for start in range(0, whole, 128):
            count = min(128, width - start)
            if count < 128:
                line[...] = jnp.zeros_like(line)
            for i in range(ROWS):
                value = value_of(i, slice(start, start + count))
                if count < 128:
                    line[:, :count] = value
                    value = line[...]
                spread[pl.ds(i, STEPS, stride=ROWS), :] = value
            target[:, start : start + 128] = spread[...]

    def set_up():
        shape = (CHUNKS, 2 * ROWS, 128)
        row = lax.broadcasted_iota(jnp.int32, shape, 1)
        time = 2 * lax.broadcasted_iota(jnp.int32, shape, 0) + row // ROWS
        stream = lax.rem(row, ROWS)
        reset = jnp.zeros(shape, jnp.int32)
        for i in range(ROWS):
            reset = jnp.where(stream == i, resets[i // 2, i % 2], reset)
        keep[...] = jnp.where(time == reset, 0.0, 1.0)
        layer_keep[...] = jnp.zeros_like(layer_keep)
        for i in range(ROWS):
            h, s = i // 2, i % 2
            for m, mask in enumerate((mid_mask, out_mask)):
                layer_keep[m, i : i + 1, :HID] = mask[h, s : s + 1, :].astype(jnp.float32) * keep_scale

        def masked(i, lanes):
            h, s = i // 2, i % 2
            kept = in_mask[h, s : s + 1, lanes].astype(jnp.float32) * keep_scale
            return (inputs[h, s, :, lanes] * kept).astype(jnp.bfloat16).astype(jnp.float32)

        by_time(dx, D_IN, 512, masked)
        column = lax.broadcasted_iota(jnp.int32, (STEPS * ROWS, 512), 1)
        value = jnp.where(column == D_IN, 1.0, dx[...])
        dx[...] = value
        o_left[:, :, pl.ds(SOURCE, 512)] = value.astype(jnp.bfloat16).reshape(CHUNKS, 2 * ROWS, 512)
        o_left[:, :, pl.ds(SOURCE + 512, 128)] = jnp.zeros((CHUNKS, 2 * ROWS, 128), jnp.bfloat16)

    def set_up_above():
        def masked(i, lanes):
            return cotangent[i // 2, i % 2, :, lanes].astype(jnp.float32) * layer_keep[1, i : i + 1, lanes]

        by_time(above, HID, WIDE, masked)

    def clear():
        hidden[...] = jnp.zeros_like(hidden)
        cell[...] = jnp.zeros_like(cell)

    def forward_pair(c, mask, with_one, o_hp, o_layer):
        column = lax.broadcasted_iota(jnp.int32, (ROWS, WIDE), 1)
        for j in range(2):
            rows = pl.ds(ROWS * j, ROWS)
            kept = keep_rows(c, j)
            hidden_prev = hidden[...] * kept
            cell_prev = cell[...] * kept
            left = hidden_prev.astype(jnp.bfloat16)
            gates = [
                dot(left, w_front[g]) + zx[c, rows, pl.ds(g * WIDE, WIDE)] for g in range(4)
            ]
            gate_in, gate_forget = sigmoid(gates[0]), sigmoid(gates[1])
            gate_cand, gate_out = jnp.tanh(gates[2]), sigmoid(gates[3])
            cell_now = gate_forget * cell_prev + gate_in * gate_cand
            cell_tanh = jnp.tanh(cell_now)
            hidden_now = (gate_out * cell_tanh).astype(jnp.bfloat16).astype(jnp.float32)
            cell[...] = cell_now
            hidden[...] = hidden_now
            stage_a[rows, :] = hidden_prev
            layer = hidden_now * mask
            if with_one:
                layer = jnp.where(column == HID, 1.0, layer)
            stage_b[rows, :] = layer
            zx[c, rows, pl.ds(0, WIDE)] = gate_cand * gate_in * (1.0 - gate_in)
            zx[c, rows, pl.ds(WIDE, WIDE)] = cell_prev * gate_forget * (1.0 - gate_forget)
            zx[c, rows, pl.ds(2 * WIDE, WIDE)] = gate_in * (1.0 - gate_cand * gate_cand)
            zx[c, rows, pl.ds(3 * WIDE, WIDE)] = cell_tanh * gate_out * (1.0 - gate_out)
            extra[c, rows, pl.ds(0, WIDE)] = gate_out * (1.0 - cell_tanh * cell_tanh)
            extra[c, rows, pl.ds(WIDE, WIDE)] = gate_forget * kept
        o_hp[c] = stage_a[...].astype(jnp.bfloat16)
        o_layer[c] = stage_b[...].astype(jnp.bfloat16)

    def backward_pair(c, upstream):
        for j in (1, 0):
            rows = pl.ds(ROWS * j, ROWS)
            total = hidden[...] + upstream[ROWS * j : ROWS * j + ROWS]
            out_grad = total * zx[c, rows, pl.ds(3 * WIDE, WIDE)]
            cell_total = cell[...] + total * extra[c, rows, pl.ds(0, WIDE)]
            cell[...] = cell_total * extra[c, rows, pl.ds(WIDE, WIDE)]
            grads = [cell_total * zx[c, rows, pl.ds(g * WIDE, WIDE)] for g in range(3)] + [out_grad]
            back = None
            for g in range(4):
                stage_z[rows, pl.ds(g * WIDE, WIDE)] = grads[g]
                part = dot(grads[g].astype(jnp.bfloat16), w_back[g])
                back = part if back is None else back + part
            hidden[...] = back * keep_rows(c, j)
        for g in range(4):
            dz[g, c] = stage_z[:, pl.ds(g * WIDE, WIDE)].astype(jnp.bfloat16)

    last = CHUNKS - 1
    groups = CHUNKS // GROUP

    @pl.when(pipe == LAYER_ONE)
    def _():
        me = LAYER_ONE
        start_spread(me)
        set_up()
        share_blocks(R_ONE)
        await_blocks(W_ONE)
        source = dx[:, :D_WIDE].astype(jnp.bfloat16)
        for g in range(4):
            zx[:, :, pl.ds(g * WIDE, WIDE)] = dot(source, w_in[g]).reshape(CHUNKS, 2 * ROWS, WIDE)
        receive_rest(R_ONE)
        clear()

        def ahead(c, carry):
            forward_pair(c, layer_keep[0], True, o_hp_one, o_u)
            copy_u(c).start()

            @pl.when((c >= LATER) & (c < LATER + TURNS))
            def _():
                pl.semaphore_signal(
                    go_on, inc=1, device_id={"pipe": SOURCE_GRAD, "dp": dp}, device_id_type=MESH
                )
                start_turn(me, c - LATER)

            @pl.when(c == LATER)
            def _():
                start_near(me)

            return carry

        lax.fori_loop(0, CHUNKS, ahead, 0)
        bulk = [
            copy_bulk(SOURCE_GRAD, o_u, 0, 0), copy_bulk(LAYER_TWO, o_u, 1, 0),
            copy_bulk(SOURCE_GRAD, o_hp_one, 2, 1), copy_bulk(LAYER_TWO, o_hp_one, 3, 1),
            copy_bulk(BETWEEN, o_hp_one, 4, 1),
        ]
        for copy in bulk:
            copy.start()
        await_blocks(R_ONE_T)
        clear()

        def behind(i, carry):
            c = last - i
            copy_du(c).wait_recv()
            mask = jnp.concatenate([layer_keep[0]] * 2, 0)
            backward_pair(c, du[c].astype(jnp.float32) * mask)
            copy_dz(SOURCE_GRAD, c).start()

            @pl.when(lax.rem(c, GROUP) == 0)
            def _():
                group = c // GROUP
                copy_part(LAYER_TWO, o_dz_one, group, 0, LAYER_TWO).start()
                copy_part(BETWEEN, o_dz_one, group, 1, BETWEEN).start()

            return carry

        lax.fori_loop(0, CHUNKS, behind, 0)
        own = pltpu.make_async_copy(dz.at[me], o_dz_one, local_sem.at[0])
        own.start()
        finish_rings(R_ONE)
        finish_spread(me)
        finish_blocks(FORWARD + BACKWARD, me)
        to(BETWEEN, o_u, o_u, u_send, u_recv.at[0]).wait_send()
        for copy in bulk:
            copy.wait_send()
        to(SOURCE_GRAD, dz, dz, dz_send, dz_recv.at[0]).wait_send()
        to(LAYER_TWO, dz.at[me], o_dz_one, part_send.at[0], part_recv.at[0]).wait_send()
        to(BETWEEN, dz.at[me], o_dz_one, part_send.at[1], part_recv.at[0]).wait_send()
        own.wait()

        copy_bulk(me, o_hp_two, 0, 2).wait_recv()
        for group in range(groups):
            copy_part(me, o_dz_two, group, 0, me).wait_recv()
            copy_dx(me, group, 0).wait_recv()

    @pl.when(pipe == LAYER_TWO)
    def _():
        me = LAYER_TWO
        start_spread(me)
        set_up()
        set_up_above()
        share_blocks(R_TWO)
        receive_rest(R_TWO)
        clear()

        def ahead(c, carry):
            copy_z(c).wait_recv()

            @pl.when((c >= LATER) & (c < LATER + TURNS))
            def _():
                start_turn(me, c - LATER)

            @pl.when(c == LATER)
            def _():
                start_near(me)

            forward_pair(c, layer_keep[1], False, o_hp_two, o_out)
            return carry

        lax.fori_loop(0, CHUNKS, ahead, 0)
        bulk = [
            copy_bulk(LAYER_ONE, o_hp_two, 0, 2), copy_bulk(SOURCE_GRAD, o_hp_two, 1, 2),
            copy_bulk(BETWEEN, o_hp_two, 2, 2), copy_bulk(BETWEEN, o_out, 3, 3),
        ]
        for copy in bulk:
            copy.start()
        await_blocks(R_TWO_T)
        clear()

        def behind(i, carry):
            c = last - i
            backward_pair(c, above[pl.ds(pl.multiple_of(c * 2 * ROWS, 2 * ROWS), 2 * ROWS), :])
            copy_dz(BETWEEN, c).start()

            @pl.when(lax.rem(c, GROUP) == 0)
            def _():
                group = c // GROUP
                copy_part(LAYER_ONE, o_dz_two, group, 0, LAYER_ONE).start()
                copy_part(SOURCE_GRAD, o_dz_two, group, 1, SOURCE_GRAD).start()

            return carry

        lax.fori_loop(0, CHUNKS, behind, 0)
        own = pltpu.make_async_copy(dz.at[me], o_dz_two, local_sem.at[0])
        own.start()
        finish_rings(R_TWO)
        finish_spread(me)
        finish_blocks(FORWARD + BACKWARD, me)
        for copy in bulk:
            copy.wait_send()
        to(BETWEEN, dz, dz, dz_send, dz_recv.at[0]).wait_send()
        to(LAYER_ONE, dz.at[me], o_dz_two, part_send.at[0], part_recv.at[0]).wait_send()
        to(SOURCE_GRAD, dz.at[me], o_dz_two, part_send.at[1], part_recv.at[0]).wait_send()
        own.wait()

        copy_bulk(me, o_u, 0, 0).wait_recv()
        copy_bulk(me, o_hp_one, 0, 1).wait_recv()
        for group in range(groups):
            copy_part(me, o_dz_one, group, 0, me).wait_recv()
            copy_dx(me, group, 0).wait_recv()

    @pl.when(pipe == BETWEEN)
    def _():
        me = BETWEEN
        start_spread(me)
        set_up()
        share_blocks(W_TWO)
        receive_rest(W_TWO)

        def ahead(c, carry):
            copy_u(c).wait_recv()
            for g in range(4):
                zx[c, :, pl.ds(g * WIDE, WIDE)] = dot(o_u[c], w_front[g])
            copy_z(c).start()

            @pl.when((c >= LATER) & (c < LATER + TURNS))
            def _():
                start_turn(me, c - LATER)

            @pl.when(c == LATER)
            def _():
                start_near(me)

            return carry

        lax.fori_loop(0, CHUNKS, ahead, 0)
        await_blocks(W_TWO_T)

        def behind(i, carry):
            c = last - i
            copy_dz(me, c).wait_recv()
            back = None
            for g in range(4):
                part = dot(dz[g, c], w_back[g])
                back = part if back is None else back + part
            du[c] = back.astype(jnp.bfloat16)
            copy_du(c).start()
            return carry

        lax.fori_loop(0, CHUNKS, behind, 0)
        own = pltpu.make_async_copy(dz.at[me], o_dz_two, local_sem.at[0])
        own.start()
        finish_rings(W_TWO)
        finish_spread(me)
        finish_blocks(FORWARD + BACKWARD, me)
        to(LAYER_TWO, zx, zx, z_send, z_recv.at[0]).wait_send()
        to(LAYER_ONE, du, du, du_send, du_recv.at[0]).wait_send()
        own.wait()

        copy_bulk(me, o_hp_one, 0, 1).wait_recv()
        copy_bulk(me, o_hp_two, 0, 2).wait_recv()
        copy_bulk(me, o_out, 0, 3).wait_recv()
        for group in range(groups):
            copy_part(me, o_dz_one, group, 0, me).wait_recv()
            copy_dx(me, group, 0).wait_recv()

    @pl.when(pipe == SOURCE_GRAD)
    def _():
        me = SOURCE_GRAD
        start_spread(me)
        set_up()

        def pass_on(turn, carry):
            pl.semaphore_wait(go_on, 1)
            start_turn(me, turn)
            return carry

        lax.fori_loop(0, TURNS, pass_on, 0)
        start_near(me)
        await_blocks(W_ONE_T)

        def behind(i, carry):
            c = last - i
            copy_dz(me, c).wait_recv()
            back = None
            for g in range(4):
                part = dot(dz[g, c], w_front[g, :, :512])
                back = part if back is None else back + part
            dx[pl.ds(pl.multiple_of(c * 2 * ROWS, 2 * ROWS), 2 * ROWS), :] = back

            @pl.when(lax.rem(c, GROUP) == 0)
            def _():
                group = c // GROUP
                copy_dx(LAYER_ONE, group, 0).start()
                copy_dx(LAYER_TWO, group, 1).start()
                copy_dx(BETWEEN, group, 2).start()

            return carry

        lax.fori_loop(0, CHUNKS, behind, 0)
        own = pltpu.make_async_copy(dz.at[me], o_dz_one, local_sem.at[0])
        own.start()
        own_dx = pltpu.make_async_copy(dx.at[:, pl.ds(me * 128, 128)], o_dx, local_sem.at[1])
        own_dx.start()
        finish_spread(me)
        finish_blocks(FORWARD + BACKWARD, me)
        for slot, pipe_to in enumerate((LAYER_ONE, LAYER_TWO, BETWEEN)):
            to(pipe_to, o_dx, o_dx, dx_send.at[slot], dx_recv.at[0]).wait_send()
        own.wait()
        own_dx.wait()

        copy_bulk(me, o_u, 0, 0).wait_recv()
        copy_bulk(me, o_hp_one, 0, 1).wait_recv()
        copy_bulk(me, o_hp_two, 0, 2).wait_recv()
        for group in range(groups):
            copy_part(me, o_dz_two, group, 0, me).wait_recv()


def relay(blocks, inputs, in_mask, mid_mask, out_mask, cotangent, resets):
    whole = pl.BlockSpec(memory_space=pltpu.VMEM)
    rows = (CHUNKS, 2 * ROWS, WIDE)
    half, full = jnp.bfloat16, jnp.float32
    shapes = [
        jax.ShapeDtypeStruct((CHUNKS, 2 * ROWS, UNITS * UNIT), half),
        jax.ShapeDtypeStruct(rows, half),
        jax.ShapeDtypeStruct((2,) + rows, half),
        jax.ShapeDtypeStruct((STEPS * ROWS, 128), full),
    ]
    dma = pltpu.SemaphoreType.DMA
    return pl.pallas_call(
        relay_kernel,
        out_shape=shapes,
        in_specs=[pl.BlockSpec(memory_space=pl.ANY)] * 8 + [whole] * 5
        + [pl.BlockSpec(memory_space=pltpu.SMEM)],
        out_specs=[whole] * 4,
        scratch_shapes=[
            pltpu.VMEM((4, WIDE, WIDE), half),
            pltpu.VMEM((4, WIDE, WIDE), half),
            pltpu.VMEM((4, D_WIDE, WIDE), half),
            pltpu.VMEM((CHUNKS, 2 * ROWS, 4 * WIDE), full),
            pltpu.VMEM((CHUNKS, 2 * ROWS, 2 * WIDE), full),
            pltpu.VMEM((4,) + rows, half),
            pltpu.VMEM(rows, half),
            pltpu.VMEM((STEPS * ROWS, 512), full),
            pltpu.VMEM((STEPS * ROWS, WIDE), full),
            pltpu.VMEM((STEPS, 128), full),
            pltpu.VMEM((STEPS * ROWS, 128), full),
            pltpu.VMEM((CHUNKS, 2 * ROWS, 128), full),
            pltpu.VMEM((2, ROWS, WIDE), full),
            pltpu.VMEM((ROWS, WIDE), full),
            pltpu.VMEM((ROWS, WIDE), full),
            pltpu.VMEM((2 * ROWS, WIDE), full),
            pltpu.VMEM((2 * ROWS, WIDE), full),
            pltpu.VMEM((2 * ROWS, 4 * WIDE), full),
            dma((8, 2)), dma((8, 4, 2)), dma((8,)),
            dma((2, 3)), dma((2, 3)), dma((2, 2, 4)), dma((2, 2, 4)), pltpu.SemaphoreType.REGULAR,
            dma, dma((CHUNKS,)), dma, dma((CHUNKS,)), dma, dma((CHUNKS,)), dma, dma((CHUNKS,)),
            dma((5,)), dma((4,)), dma((2,)), dma((CHUNKS // GROUP,)), dma((3,)), dma((CHUNKS // GROUP,)), dma((2,)),
        ],
        compiler_params=pltpu.CompilerParams(
            vmem_limit_bytes=60 << 20, collective_id=0, has_side_effects=True
        ),
        name="relay",
    )(*blocks, inputs, in_mask, mid_mask, out_mask, cotangent, resets)


def reduce_kernel(
    left, dz, total, own, near, far, part, cross, share,
    near_send, near_recv, far_send, far_recv, part_send, part_recv, last_send, last_recv,
    cross_send, cross_recv, back_send, back_recv, wide_send, wide_recv, share_send, share_recv,
):
    pipe = lax.axis_index("pipe")
    dp = lax.axis_index("dp")
    z, x, y = dp // 16, lax.rem(dp // 4, 4), lax.rem(dp, 4)

    def device(z_, x_, y_):
        return {"pipe": pipe, "dp": z_ * 16 + lax.rem(x_ + 4, 4) * 4 + lax.rem(y_ + 4, 4)}

    along_x, along_y = (lambda d: device(z, x + d, y)), (lambda d: device(z, x, y + d))
    first, second = (along_x, along_y) * 2, (along_y, along_x) * 2
    place = ((x, y), (y, x)) * 2
    across = device(1 - z, x, y)
    size = (BIG, BIG, SMALL, SMALL)
    base = (0, 16 * BIG, THIRD + z * SHARE, THIRD + z * SHARE + 16 * SMALL)

    barrier = pltpu.get_barrier_semaphore()
    for target in (along_x(1), along_x(-1), along_y(1), along_y(-1), across):
        pl.semaphore_signal(barrier, inc=1, device_id=target, device_id_type=MESH)
    pl.semaphore_wait(barrier, 5)

    lanes_of = (pl.ds(0, WIDE), pl.ds(0, 640), pl.ds(640, 512))

    def unit(p, block, rel):
        a, b = place[p]
        index = lax.rem(a + block + 4, 4) * 4 + lax.rem(b + rel + 4, 4)
        return pl.ds(pl.multiple_of(base[p] + index * size[p], 16), size[p])

    def send(source, target, s, r, to):
        return pltpu.make_async_remote_copy(source, target, s, r, device_id=to, device_id_type=MESH)

    def add(target, rows, others, lanes=lanes_of[0]):
        def body(i, carry):
            span = pl.ds(pl.multiple_of(rows.start + i * 16, 16), 16)
            value = own[span, lanes].astype(jnp.float32)
            for ref in others:
                value = value + ref[pl.ds(pl.multiple_of(i * 16, 16), 16), lanes].astype(jnp.float32)
            target[span, lanes] = value.astype(jnp.bfloat16)
            return carry

        lax.fori_loop(0, rows.size // 16, body, 0)

    def product(u):
        columns = pl.ds(pl.multiple_of(u * UNIT, UNIT), UNIT)
        own[columns, :] = lax.dot_general(
            left[:, columns], dz[jnp.where(u < SWITCH, 0, 1)], (((0,), (0,)), ((), ())),
            preferred_element_type=jnp.float32,
        ).astype(jnp.bfloat16)

    def products(start, count):
        def body(i, carry):
            product(start + i)
            return carry

        lax.fori_loop(0, count, body, 0)

    block_units = 4 * BIG // UNIT

    def block_products(p, block):
        products(p * 4 * block_units + lax.rem(place[p][0] + block + 4, 4) * block_units, block_units)

    side = {1: (2, 1), -1: (3, 0)}
    on_side = {1: (0, 1), -1: (3, 2)}
    slot = {1: 0, -1: 1}
    started = []

    def go(copy):
        copy.start()
        started.append(copy)

    def near_copy(p, d, k):
        at = (p, slot[d], k)
        return send(own.at[unit(p, 2, side[d][k])], near.at[at].at[pl.ds(0, size[p])], near_send.at[at],
                    near_recv.at[at], first[p](d))

    def far_copy(p, d, k, block=None):
        rel = (side[-d] + side[d])[k]
        at = (p, slot[d], rel)
        return send(own.at[unit(p, d if block is None else block, rel)], far.at[at].at[pl.ds(0, size[p])],
                    far_send.at[at], far_recv.at[at], first[p](d))

    def part_copy(p, d):
        lanes = lanes_of[1 if d == 1 else 2]
        at = (p, slot[d])
        return send(own.at[unit(p, 0, 2), lanes], part.at[at].at[pl.ds(0, size[p]), lanes], part_send.at[at],
                    part_recv.at[at], second[p](d))

    def last_copy(p, d, k):
        lanes = lanes_of[(2 - k) if d == 1 else (1 + k)]
        at = (p, slot[d], k)
        return send(own.at[unit(p, 0, d), lanes], part.at[p, 2 + slot[d]].at[pl.ds(0, size[p]), lanes],
                    last_send.at[at], last_recv.at[at], second[p](d))

    def cross_copy(p):
        return send(own.at[unit(p, 0, 0)], cross.at[p], cross_send.at[p], cross_recv.at[p], across)

    def share_copy(i):
        rows = pl.ds(pl.multiple_of(THIRD + (1 - z) * SHARE + i * UNIT, UNIT), UNIT)
        return send(own.at[rows], share.at[pl.ds(i * UNIT, UNIT)], share_send.at[i], share_recv.at[i], across)

    def share_back(half):
        rows = pl.ds(pl.multiple_of(THIRD + half * SHARE, UNIT), SHARE)
        return send(total.at[rows], total.at[rows], share_send.at[4], share_recv.at[4], across)

    def back_copy(p, d, rel=0, on=0):
        at = (p, slot[d], on)
        ref = total.at[unit(p, 0, rel), lanes_of[0 if not on else 1 if d == 1 else 2]]
        return send(ref, ref, back_send.at[at], back_recv.at[at], second[p](d))

    def wide_copy(p, d, rel, block=0, on=0):
        at = (p, slot[d], rel + 4 * on)
        ref = total.at[unit(p, block, rel)]
        return send(ref, ref, wide_send.at[at], wide_recv.at[at], first[p](d))

    def start_near(parts):
        for k in range(2):
            for p in parts:
                for d in (1, -1):
                    go(near_copy(p, d, k))

    def start_far(parts):
        for k in range(2):
            for p in parts:
                for d in (1, -1):
                    go(far_copy(p, d, k))

    def finish_near(parts):
        for k in range(2):
            for p in parts:
                for d in (1, -1):
                    near_copy(p, d, k).wait_recv()
                    add(own, unit(p, d, side[d][k]), [near.at[p, slot[d], k]])
                    go(far_copy(p, d, 2 + k))

    def collect(p, rel):
        for d in (1, -1):
            far_copy(p, d, (side[-d] + side[d]).index(rel), 0).wait_recv()
        add(own, unit(p, 0, rel), [far.at[p, 0, rel], far.at[p, 1, rel]])

    def start_second(parts):
        for p in parts:
            collect(p, 2)
            for d in (1, -1):
                go(part_copy(p, d))
        for rel, d in ((3, -1), (1, 1)):
            for p in parts:
                collect(p, rel)
                go(last_copy(p, d, 0))
        for p in parts:
            collect(p, 0)

    def finish_part(parts):
        for d in (1, -1):
            for p in parts:
                part_copy(p, d).wait_recv()
                add(own, unit(p, 0, d), [part.at[p, slot[d]]], lanes_of[1 if d == 1 else 2])
                go(last_copy(p, d, 1))

    def finish_second(parts, target):
        for p in parts:
            for d in (1, -1):
                for k in range(2):
                    last_copy(p, d, k).wait_recv()
            add(target, unit(p, 0, 0), [part.at[p, 2], part.at[p, 3]])

    def start_back(parts):
        for p in parts:
            for d in (1, -1):
                go(back_copy(p, d))
            for d in (1, -1):
                go(wide_copy(p, d, 0))

    def pass_back(parts):
        for d in (1, -1):
            for p in parts:
                back_copy(p, d, -d).wait_recv()
                go(back_copy(p, d, -d, 1))
                for e in (1, -1):
                    go(wide_copy(p, e, -d % 4))

    def finish_back(parts):
        for p in parts:
            for d in (1, -1):
                back_copy(p, d, 2, 1).wait_recv()
            for d in (1, -1):
                go(wide_copy(p, d, 2))

    def pass_wide(parts):
        for k in range(2):
            for d in (1, -1):
                for p in parts:
                    rel = on_side[d][k]
                    wide_copy(p, d, rel, -d).wait_recv()
                    go(wide_copy(p, d, rel, -d, 1))

    def finish_wide(parts):
        for p in parts:
            for d in (1, -1):
                for rel in range(4):
                    if rel not in on_side[d]:
                        wide_copy(p, d, rel, -d).wait_recv()
                for rel in on_side[d]:
                    wide_copy(p, d, rel, 2, 1).wait_recv()

    big, small = (0, 1), (2, 3)
    for p in big:
        block_products(p, 2)
    start_near(big)
    for i in range(4):
        product(THIRD // UNIT + (1 - z) * 4 + i)
        go(share_copy(i))
    for d in (1, -1):
        for p in big:
            block_products(p, d)
    start_far(big)
    for p in big:
        block_products(p, 0)
    products(THIRD // UNIT + z * 4, 4)
    finish_near(big)
    for i in range(4):
        share_copy(i).wait_recv()
        rows = pl.ds(pl.multiple_of(THIRD + z * SHARE + i * UNIT, UNIT), UNIT)
        add(own, rows, [share.at[pl.ds(i * UNIT, UNIT)]])
    start_near(small)
    start_far(small)
    start_second(big)
    finish_near(small)
    finish_part(big)
    start_second(small)
    finish_second(big, own)
    for p in big:
        go(cross_copy(p))
    finish_part(small)
    finish_second(small, total)
    start_back(small)
    pass_back(small)
    for p in big:
        cross_copy(p).wait_recv()
        add(total, unit(p, 0, 0), [cross.at[p]])
    start_back(big)
    finish_back(small)
    pass_wide(small)
    pass_back(big)
    finish_wide(small)
    go(share_back(z))
    finish_back(big)
    pass_wide(big)
    finish_wide(big)
    share_back(1 - z).wait_recv()
    for copy in started:
        copy.wait_send()


def reduce_over_dp(left, dz):
    whole = pl.BlockSpec(memory_space=pltpu.VMEM)
    half = jnp.bfloat16
    dma = pltpu.SemaphoreType.DMA
    return pl.pallas_call(
        reduce_kernel,
        out_shape=jax.ShapeDtypeStruct((UNITS * UNIT, WIDE), half),
        in_specs=[whole] * 2,
        out_specs=whole,
        scratch_shapes=[
            pltpu.VMEM((UNITS * UNIT, WIDE), half),
            pltpu.VMEM((4, 2, 2, BIG, WIDE), half),
            pltpu.VMEM((4, 2, 4, BIG, WIDE), half),
            pltpu.VMEM((4, 4, BIG, WIDE), half),
            pltpu.VMEM((2, BIG, WIDE), half),
            pltpu.VMEM((SHARE, WIDE), half),
            dma((4, 2, 2)), dma((4, 2, 2)), dma((4, 2, 4)), dma((4, 2, 4)), dma((4, 2)), dma((4, 2)),
            dma((4, 2, 2)), dma((4, 2, 2)), dma((2,)), dma((2,)), dma((4, 2, 2)), dma((4, 2, 2)),
            dma((4, 2, 8)), dma((4, 2, 8)), dma((5,)), dma((5,)),
        ],
        compiler_params=pltpu.CompilerParams(
            vmem_limit_bytes=60 << 20, collective_id=1, has_side_effects=True
        ),
        name="reduce",
    )(left, dz)


def prepare_kernel(
    w_one, bias, r_one, drop_one, w_two, r_two, drop_two,
    o_w_one, o_r_one, o_r_two, o_w_two, o_r_one_t, o_r_two_t, o_w_two_t, o_w_one_t,
    square, small, apart,
):
    column = pl.program_id(0) * UNIT + lax.broadcasted_iota(jnp.int32, (WIDE, UNIT), 1)
    inside = column < HID

    def finish(o_plain, o_turned, turned_rows):
        value = jnp.where(inside, square[...], 0.0)
        o_plain[...] = value.astype(jnp.bfloat16)
        row = lax.broadcasted_iota(jnp.int32, (WIDE, UNIT), 0)
        if turned_rows < WIDE:
            value = jnp.where(row < turned_rows, value, 0.0)
        o_turned[...] = value.T.astype(jnp.bfloat16)

    square[...] = jnp.zeros_like(square)
    for weights, drop, o_plain, o_turned in (
        (r_one, drop_one, o_r_one, o_r_one_t), (r_two, drop_two, o_r_two, o_r_two_t),
    ):
        square[:HID, :] = weights[...].astype(jnp.float32) * drop[...].astype(jnp.float32) * weight_scale
        finish(o_plain, o_turned, WIDE)
    square[:HID, :] = w_two[...].astype(jnp.float32)
    square[HID : HID + 1, :] = bias[1:2].astype(jnp.float32)
    finish(o_w_two, o_w_two_t, HID)

    w_one_f = w_one[...].astype(jnp.float32)
    small[...] = jnp.zeros_like(small)
    small[:D_IN, :] = w_one_f
    small[D_IN : D_IN + 1, :] = bias[0:1].astype(jnp.float32)
    o_w_one[...] = jnp.where(inside[:D_WIDE], small[...], 0.0).astype(jnp.bfloat16)
    apart[...] = jnp.zeros_like(apart)
    for q in range(4):
        apart[q * UNIT : q * UNIT + 100, :] = small[q * 100 : q * 100 + 100, :]
    o_w_one_t[...] = jnp.where(inside[:512], apart[...], 0.0).T.astype(jnp.bfloat16)


def prepare(w_one, bias, r_one, drop_one, w_two, r_two, drop_two):
    half = jnp.bfloat16

    def slab(rows):
        return pl.BlockSpec((rows, UNIT), lambda j: (0, j))

    def turned(columns):
        return pl.BlockSpec((UNIT, columns), lambda j: (j, 0))

    square = jax.ShapeDtypeStruct((WIDE, WIDE), half)
    return pl.pallas_call(
        prepare_kernel,
        grid=(WIDE // UNIT,),
        in_specs=[slab(D_IN), slab(2), slab(HID), slab(HID), slab(HID), slab(HID), slab(HID)],
        out_specs=[slab(D_WIDE)] + [slab(WIDE)] * 3 + [turned(WIDE)] * 3 + [turned(512)],
        out_shape=[jax.ShapeDtypeStruct((D_WIDE, WIDE), half)] + [square] * 6
        + [jax.ShapeDtypeStruct((WIDE, 512), half)],
        scratch_shapes=[
            pltpu.VMEM((WIDE, UNIT), jnp.float32), pltpu.VMEM((D_WIDE, UNIT), jnp.float32),
            pltpu.VMEM((512, UNIT), jnp.float32),
        ],
        compiler_params=pltpu.CompilerParams(vmem_limit_bytes=60 << 20),
        name="prepare",
    )(w_one, bias, r_one, drop_one, w_two, r_two, drop_two)


def finish_kernel(
    hp_one, source, u_two, hp_two, drop_one, drop_two, o_in_one, o_rec_one, o_bias_one, o_in_two, o_rec_two, o_bias_two
):
    step = pl.program_id(0)

    def wide(ref):
        return ref[:, :HID].astype(jnp.float32)

    o_rec_one[...] = wide(hp_one) * drop_one[...].astype(jnp.float32) * weight_scale
    o_rec_two[...] = wide(hp_two) * drop_two[...].astype(jnp.float32) * weight_scale
    o_in_one[...] = wide(source)
    o_in_two[...] = wide(u_two)

    @pl.when(step == D_IN // UNIT)
    def _():
        o_bias_one[...] = wide(source)[D_IN % UNIT : D_IN % UNIT + 1]

    @pl.when(step == HID // UNIT)
    def _():
        o_bias_two[...] = wide(u_two)[HID % UNIT : HID % UNIT + 1]


def finish(total, drop_one, drop_two):
    def units(first, last):
        return pl.BlockSpec((UNIT, WIDE), lambda i: (first + jnp.minimum(i, last), 0))

    def rows(last):
        return pl.BlockSpec((UNIT, HID), lambda i: (jnp.minimum(i, last), 0))

    one = pl.BlockSpec((1, HID), lambda i: (0, 0))
    count, short = WIDE // UNIT, D_IN // UNIT
    square, line = jax.ShapeDtypeStruct((HID, HID), jnp.float32), jax.ShapeDtypeStruct((1, HID), jnp.float32)
    return pl.pallas_call(
        finish_kernel,
        grid=(count,),
        in_specs=[
            units(HP_ONE // UNIT, count), units(SOURCE // UNIT, short), units(U_TWO // UNIT, count),
            units(HP_TWO // UNIT, count), rows(count), rows(count),
        ],
        out_specs=[rows(short), rows(count), one, rows(count), rows(count), one],
        out_shape=[jax.ShapeDtypeStruct((D_IN, HID), jnp.float32), square, line, square, square, line],
        compiler_params=pltpu.CompilerParams(vmem_limit_bytes=60 << 20),
        name="finish",
    )(total, total, total, total, drop_one, drop_two)


def local(
    inputs, resets, in_mask, mid_mask, out_mask,
    w_ih_one, w_hh_one, bias_one, drop_one, w_ih_two, w_hh_two, bias_two, drop_two, cotangent,
):
    pipe = lax.axis_index("pipe")
    bias = jnp.stack([bias_one, bias_two])
    blocks = prepare(w_ih_one, bias, w_hh_one, drop_one, w_ih_two, w_hh_two, drop_two)
    left, out_two, dz, dx = relay(blocks, inputs, in_mask, mid_mask, out_mask, cotangent, resets)
    left = left.reshape(STEPS * ROWS, UNITS * UNIT)
    total = reduce_over_dp(left, dz.reshape(2, STEPS * ROWS, WIDE))

    u_two = left[:, U_TWO : U_TWO + WIDE].reshape(out_two.shape)
    layer = jnp.where(pipe < 2, u_two, out_two).reshape(STEPS, 2, 2, WIDE)[..., :HID]
    layer = lax.dynamic_index_in_dim(layer, pipe % 2, 1, keepdims=False)
    layer_outputs = jnp.swapaxes(layer, 0, 1)[None]
    grad_input = jnp.transpose(dx.reshape(STEPS, 2, 2, 128)[..., :100], (1, 2, 0, 3))
    keep_in = in_mask.astype(jnp.float32) * keep_scale
    keep_part = lax.dynamic_slice_in_dim(keep_in, pipe * 100, 100, 2)
    grad_input = grad_input * keep_part[:, :, None, :]

    in_one, rec_one, bias_one, in_two, rec_two, bias_two = finish(total, drop_one, drop_two)
    return (layer_outputs, grad_input, in_one, rec_one, bias_one[0], in_two, rec_two, bias_two[0])


def solution(mesh):
    placed = (
        P(None, "dp", None, None),
        P(None, "dp"),
        P(None, "dp", None),
        P(None, "dp", None),
        P(None, "dp", None),
        P(None, "pipe"),
        P(None, "pipe"),
        P("pipe"),
        P(None, "pipe"),
        P(None, "pipe"),
        P(None, "pipe"),
        P("pipe"),
        P(None, "pipe"),
        P(None, "dp", None, None),
    )
    return jax.shard_map(
        local,
        mesh=mesh,
        in_specs=placed,
        out_specs=(
            P("pipe", "dp", None, None),
            P(None, "dp", None, "pipe"),
            P(None, "pipe"),
            P(None, "pipe"),
            P("pipe"),
            P(None, "pipe"),
            P(None, "pipe"),
            P("pipe"),
        ),
        check_vma=False,
    )
```

```python
import functools

import jax
import jax.numpy as jnp
from jax import lax
from jax.experimental import pallas as pl
from jax.experimental.pallas import tpu as pltpu
from jax.sharding import PartitionSpec as P

MESH = pl.DeviceIdType.MESH
HID = 1150
WIDE = 1152
D_IN = 400
D_WIDE = 416
STEPS = 88
ROWS = 4
CHUNKS = 44
GROUP = 4
LATER = 3
TURNS = 36
UNIT = 128
HALF_UNIT = 64
UNITS = 32
HP_ONE, U_TWO, HP_TWO, SOURCE = 0, 1152, 2304, 3456
SOURCE_WIDE = 640
SLAB = 384
DEEP = 4
BIG, SMALL = 96, 16
THIRD = 32 * BIG
SHARE = 32 * SMALL

keep_scale = 4.0 / 3.0
weight_scale = 2.0

LAYER_ONE, SOURCE_GRAD, LAYER_TWO, BETWEEN = 0, 1, 2, 3
W_ONE, R_ONE, R_TWO, W_TWO, R_ONE_T, R_TWO_T, W_TWO_T, W_ONE_T = range(8)
USER = {
    W_ONE: LAYER_ONE,
    R_ONE: LAYER_ONE,
    R_TWO: LAYER_TWO,
    W_TWO: BETWEEN,
    R_ONE_T: LAYER_ONE,
    R_TWO_T: LAYER_TWO,
    W_TWO_T: BETWEEN,
    W_ONE_T: SOURCE_GRAD,
}
FORWARD = (W_ONE,)
BACKWARD = (R_TWO_T, W_TWO_T, R_ONE_T, W_ONE_T)


def sigmoid(value):
    return 0.5 * jnp.tanh(0.5 * value) + 0.5


def dot(left, right):
    return jnp.dot(left, right, preferred_element_type=jnp.float32)


def relay_kernel(
    w_one, bias, tails, r_one, drop_one, r_two, drop_two, w_two,
    inputs, in_mask, mid_mask, out_mask, cotangent, resets,
    o_left, o_out, o_dz, o_dx, turned, turned_in,
    raw_weights, raw_drop, raw_sem, plain, plain_in, turn, small, apart, turn_sem,
    w_front, w_back, zx, extra, dz, du, dx, above, line, spread, keep, layer_keep, hidden, cell, stage_a, stage_b, stage_z,
    block_send, block_recv, block_local, cross_send, cross_recv, ring_send, ring_recv, go_on,
    u_send, u_recv, z_send, z_recv, dz_send, dz_recv, du_send, du_recv,
    bulk_send, bulk_recv, part_send, part_recv, dx_send, dx_recv, local_sem,
):
    o_hp_one, o_u, o_hp_two = (o_left.at[:, :, pl.ds(start, WIDE)] for start in (HP_ONE, U_TWO, HP_TWO))
    o_dz_one, o_dz_two = o_dz.at[0], o_dz.at[1]
    pipe = lax.axis_index("pipe")
    dp = lax.axis_index("dp")
    dp_count = lax.axis_size("dp")
    dp_far = lax.rem(dp + dp_count // 2, dp_count)

    barrier = pltpu.get_barrier_semaphore()
    for step in range(1, 4):
        pl.semaphore_signal(
            barrier, inc=1, device_id={"pipe": lax.rem(pipe + step, 4), "dp": dp}, device_id_type=MESH
        )
    for step in range(4):
        pl.semaphore_signal(
            barrier, inc=1, device_id={"pipe": lax.rem(pipe + step, 4), "dp": dp_far}, device_id_type=MESH
        )
    z, x, y = dp // 16, lax.rem(dp // 4, 4), lax.rem(dp, 4)
    rings = (
        lambda d: {"pipe": pipe, "dp": z * 16 + lax.rem(x + d + 4, 4) * 4 + y},
        lambda d: {"pipe": pipe, "dp": z * 16 + x * 4 + lax.rem(y + d + 4, 4)},
    )
    for ring in rings:
        for d in (1, -1):
            pl.semaphore_signal(barrier, inc=1, device_id=ring(d), device_id_type=MESH)

    def make_plain(m, also=None):
        weights, drop = ((r_one, drop_one), (r_two, drop_two), (w_two, None))[m]
        plain[m, :, pl.ds(HID // UNIT * UNIT, UNIT)] = jnp.zeros((WIDE, UNIT), jnp.bfloat16)

        def copies(i):
            slot = lax.rem(i, DEEP)
            span = pl.ds(pl.multiple_of(i * UNIT, UNIT), UNIT)
            return [
                pltpu.make_async_copy(array.at[span], raw.at[slot], raw_sem.at[k, slot])
                for k, (array, raw) in enumerate(((weights, raw_weights), (drop, raw_drop)))
                if array is not None
            ]

        def start(i):
            for copy in copies(i):
                copy.start()

        whole = HID // UNIT

        def body(i, carry):
            for copy in copies(i):
                copy.wait()
            slot = lax.rem(i, DEEP)
            value = raw_weights[slot]
            if drop is not None:
                value = value.astype(jnp.float32) * raw_drop[slot].astype(jnp.float32) * weight_scale
            plain[m, pl.ds(pl.multiple_of(i * UNIT, UNIT), UNIT), pl.ds(0, HID)] = value.astype(jnp.bfloat16)
            pl.when(i + DEEP < whole)(lambda: start(i + DEEP))
            if also is not None:
                also(i)
            return carry

        for i in range(DEEP):
            start(i)
        plain[m, pl.ds(whole * UNIT, UNIT)] = tails[m]
        lax.fori_loop(0, whole, body, 0)
        if also is not None:
            also(whole)

    def turn_copy(m, i, slot):
        rows = pl.ds(pl.multiple_of(i * UNIT, UNIT), UNIT)
        return pltpu.make_async_copy(turn.at[slot], turned.at[m, rows], turn_sem.at[slot])

    def make_turned(m, order, i):
        slot = lax.rem(order * (WIDE // UNIT) + i, 2)
        if order:
            turn_copy(m, i, slot).wait()
        else:
            pl.when(i >= 2)(lambda: turn_copy(m, i, slot).wait())
        value = plain[m, :, pl.ds(pl.multiple_of(i * UNIT, UNIT), UNIT)].astype(jnp.float32).T
        column = lax.broadcasted_iota(jnp.int32, (UNIT, WIDE), 1)
        turn[slot] = jnp.where(column < HID, value, 0.0).astype(jnp.bfloat16)
        turn_copy(m, i, slot).start()

    def turn_in_copy(i):
        slot = lax.rem(i, 2)
        rows = pl.ds(pl.multiple_of(i * UNIT, UNIT), UNIT)
        return pltpu.make_async_copy(turn.at[slot, :, pl.ds(0, 512)], turned_in.at[rows], turn_sem.at[slot])

    def make_plain_in():
        plain_in[...] = jnp.zeros_like(plain_in)
        plain_in[:D_IN, :HID] = w_one[...]
        row = lax.broadcasted_iota(jnp.int32, (D_WIDE - D_IN, HID), 0)
        below = jnp.where(row == 0, bias[0:1].astype(jnp.float32), 0.0)
        plain_in[D_IN:, :HID] = below.astype(jnp.bfloat16)

    def make_turned_in(i, carry):
        small[...] = plain_in[:D_IN, pl.ds(pl.multiple_of(i * UNIT, UNIT), UNIT)].astype(jnp.float32)
        for q in range(4):
            apart[q * UNIT : q * UNIT + 100, :] = small[q * 100 : q * 100 + 100, :]
        pl.when(i >= 2)(lambda: turn_in_copy(i).wait())
        turn[lax.rem(i, 2), :, pl.ds(0, 512)] = apart[...].T.astype(jnp.bfloat16)
        turn_in_copy(i).start()
        return carry

    def finish_turned(m, order):
        def body(i, carry):
            make_turned(m, order, i)
            return carry

        lax.fori_loop(0, WIDE // UNIT, body, 0)
        for slot in range(2):
            turn_copy(m, 0, slot).wait()
        apart[...] = jnp.zeros_like(apart)
        lax.fori_loop(0, WIDE // UNIT, make_turned_in, 0)
        for i in range(2):
            turn_in_copy(i).wait()

    @pl.when(pipe >= 2)
    def _():
        make_plain(0)

    @pl.when(pipe < 2)
    def _():
        make_plain(2)

    make_plain_in()
    pl.semaphore_wait(barrier, 11)

    blocks = {
        W_ONE: plain_in, R_ONE: plain.at[0], R_TWO: plain.at[1], W_TWO: plain.at[2],
        R_ONE_T: turned.at[0], R_TWO_T: turned.at[1], W_TWO_T: turned.at[2], W_ONE_T: turned_in,
    }

    def landing(kind, p):
        if kind == W_ONE:
            return w_back.at[p, pl.ds(0, D_WIDE)]
        if kind in (R_ONE, R_TWO, W_TWO):
            return w_front.at[p]
        if kind == W_ONE_T:
            return w_front.at[p, :, pl.ds(0, 512)]
        return w_back.at[p]

    def block_copies(kind, p, turn=None):
        user = USER[kind]
        source_ref, target = blocks[kind], landing(kind, p)
        if p == user:
            return [pltpu.make_async_copy(source_ref, target, block_local.at[kind])]
        if p // 2 == user // 2:
            return [
                pltpu.make_async_remote_copy(
                    source_ref, target, block_send.at[kind, 0], block_recv.at[kind, p, 0],
                    device_id={"pipe": user, "dp": dp}, device_id_type=MESH,
                )
            ]
        rows = source_ref.shape[0] // 2
        if turn is None:
            spans = [pl.ds(part * rows, rows) for part in range(2)]
        else:
            piece = rows // TURNS
            spans = [pl.ds(pl.multiple_of(part * rows + turn * piece, piece), piece) for part in range(2)]
        return [
            pltpu.make_async_remote_copy(
                source_ref.at[spans[part]], target.at[spans[part]],
                block_send.at[kind, part], block_recv.at[kind, p, part],
                device_id={"pipe": user, "dp": (dp, dp_far)[part]}, device_id_type=MESH,
            )
            for part in range(2)
        ]

    def rows_at(first, count=UNIT):
        return pl.ds(pl.multiple_of(first, 64), count)

    def part_rows(ring, step):
        place = (x, y)[ring]
        return UNIT * (1 + 4 * ring + lax.rem(place + step + 4, 4))

    def from_other_plane(kind):
        return [p for p in range(4) if p // 2 != USER[kind] // 2]

    def cross_copy(kind, p, k, slot):
        rows = rows_at((part_rows(0, 0), part_rows(1, 0), 0)[k])
        return pltpu.make_async_remote_copy(
            blocks[kind].at[rows], w_front.at[p, rows], cross_send.at[slot, k], cross_recv.at[p % 2, k],
            device_id={"pipe": USER[kind], "dp": (dp, dp_far)[p % 2]}, device_id_type=MESH,
        )

    def ring_copy(p, ring, d, on):
        k = 2 * on + (0 if d == 1 else 1)
        if on:
            rows = rows_at(part_rows(ring, -d) + (0 if d == 1 else HALF_UNIT), HALF_UNIT)
        else:
            rows = rows_at(part_rows(ring, 0))
        ref = w_front.at[p, rows]
        return pltpu.make_async_remote_copy(
            ref, ref, ring_send.at[p % 2, ring, k], ring_recv.at[p % 2, ring, k],
            device_id=rings[ring](d), device_id_type=MESH,
        )

    def ring_arrival(p, ring, d, on):
        k = 2 * on + (0 if d == 1 else 1)
        if on:
            rows = rows_at(part_rows(ring, 2) + (0 if d == 1 else HALF_UNIT), HALF_UNIT)
        else:
            rows = rows_at(part_rows(ring, -d))
        ref = w_front.at[p, rows]
        return pltpu.make_async_remote_copy(
            ref, ref, ring_send.at[p % 2, ring, k], ring_recv.at[p % 2, ring, k],
            device_id=rings[ring](d), device_id_type=MESH,
        )

    SPREAD = (W_TWO, R_TWO, R_ONE)

    def start_cross(me, kind, ks):
        slot = (R_TWO, W_TWO, R_ONE).index(kind) % 2
        for k in ks:
            cross_copy(kind, me, k, slot).start()

    def start_spread(me):
        if me // 2 == 1:
            start_cross(me, R_ONE, (0, 1))
            start_blocks(FORWARD, me)
            start_cross(me, R_ONE, (2,))
            make_plain(2, functools.partial(make_turned, 0, 0))
            block_copies(W_TWO, me)[0].start()
            make_plain(1, functools.partial(make_turned, 2, 1))
            block_copies(R_TWO, me)[0].start()
            finish_turned(1, 2)
        else:
            start_cross(me, W_TWO, (0, 1))
            start_blocks(FORWARD, me)
            make_plain(1, functools.partial(make_turned, 2, 0))
            start_cross(me, R_TWO, (0, 1))
            start_cross(me, W_TWO, (2,))
            start_cross(me, R_TWO, (2,))
            make_plain(0, functools.partial(make_turned, 1, 1))
            block_copies(R_ONE, me)[0].start()
            finish_turned(0, 2)

    def finish_spread(me):
        kinds = [kind for kind in SPREAD if me // 2 != USER[kind] // 2]
        for kind in kinds:
            slot = (R_TWO, W_TWO, R_ONE).index(kind) % 2
            for k in range(3):
                cross_copy(kind, me, k, slot).wait_send()
        for kind in SPREAD:
            if me // 2 == USER[kind] // 2 and me != USER[kind]:
                block_copies(kind, me)[0].wait_send()

    def share_blocks(kind):
        others = from_other_plane(kind)
        for ring in range(2):
            for p in others:
                cross_copy(kind, p, ring, 0).wait_recv()
                for d in (1, -1):
                    ring_copy(p, ring, d, 0).start()
        for d in (1, -1):
            for p in others:
                for ring in range(2):
                    ring_arrival(p, ring, d, 0).wait_recv()
                    ring_copy(p, ring, d, 1).start()

    def receive_rest(kind):
        me = USER[kind]
        others = from_other_plane(kind)
        for p in others:
            cross_copy(kind, p, 2, 0).wait_recv()
            for ring in range(2):
                for d in (1, -1):
                    ring_arrival(p, ring, d, 1).wait_recv()
        for p in (me, me ^ 1):
            copy = block_copies(kind, p)[0]
            if p == me:
                copy.wait()
            else:
                copy.wait_recv()

    def finish_rings(kind):
        for p in from_other_plane(kind):
            for ring in range(2):
                for d in (1, -1):
                    for on in range(2):
                        ring_copy(p, ring, d, on).wait_send()

    def start_blocks(kinds, p):
        for kind in kinds:
            for copy in block_copies(kind, p):
                copy.start()

    def start_near(p):
        for kind in BACKWARD:
            if p // 2 == USER[kind] // 2:
                for copy in block_copies(kind, p):
                    copy.start()

    def start_turn(p, turn):
        for kind in BACKWARD:
            if p // 2 != USER[kind] // 2:
                for copy in block_copies(kind, p, turn):
                    copy.start()

    def finish_blocks(kinds, p):
        for kind in kinds:
            if p != USER[kind]:
                for copy in block_copies(kind, p):
                    copy.wait_send()

    def await_blocks(kind):
        for p in range(4):
            for copy in block_copies(kind, p):
                if p == USER[kind]:
                    copy.wait()
                else:
                    copy.wait_recv()

    def to(pipe_to, source_ref, target, send, recv):
        return pltpu.make_async_remote_copy(
            source_ref, target, send, recv,
            device_id={"pipe": pipe_to, "dp": dp}, device_id_type=MESH,
        )

    def copy_u(c):
        return to(BETWEEN, o_u.at[c], o_u.at[c], u_send, u_recv.at[c])

    def copy_z(c):
        return to(LAYER_TWO, zx.at[c], zx.at[c], z_send, z_recv.at[c])

    def copy_dz(pipe_to, c):
        return to(pipe_to, dz.at[:, c], dz.at[:, c], dz_send, dz_recv.at[c])

    def copy_du(c):
        return to(LAYER_ONE, du.at[c], du.at[c], du_send, du_recv.at[c])

    def copy_part(pipe_to, output, group, slot, gate):
        span = pl.ds(group * GROUP, GROUP)
        return to(pipe_to, dz.at[gate, span], output.at[span], part_send.at[slot], part_recv.at[group])

    def copy_dx(pipe_to, group, slot):
        count = GROUP * 2 * ROWS
        span = pl.ds(pl.multiple_of(group * count, count), count)
        return to(
            pipe_to, dx.at[span, pl.ds(pipe_to * 128, 128)], o_dx.at[span], dx_send.at[slot], dx_recv.at[group]
        )

    def copy_bulk(pipe_to, ref, slot, which):
        return to(pipe_to, ref, ref, bulk_send.at[slot], bulk_recv.at[which])

    def keep_rows(c, j):
        return jnp.broadcast_to(keep[c, ROWS * j : ROWS * j + ROWS, 0:1], (ROWS, WIDE))

    def by_time(target, width, whole, value_of):
        for start in range(0, whole, 128):
            count = min(128, width - start)
            if count < 128:
                line[...] = jnp.zeros_like(line)
            for i in range(ROWS):
                value = value_of(i, slice(start, start + count))
                if count < 128:
                    line[:, :count] = value
                    value = line[...]
                spread[pl.ds(i, STEPS, stride=ROWS), :] = value
            target[:, start : start + 128] = spread[...]

    def set_up():
        shape = (CHUNKS, 2 * ROWS, 128)
        row = lax.broadcasted_iota(jnp.int32, shape, 1)
        time = 2 * lax.broadcasted_iota(jnp.int32, shape, 0) + row // ROWS
        stream = lax.rem(row, ROWS)
        reset = jnp.zeros(shape, jnp.int32)
        for i in range(ROWS):
            reset = jnp.where(stream == i, resets[i // 2, i % 2], reset)
        keep[...] = jnp.where(time == reset, 0.0, 1.0)
        layer_keep[...] = jnp.zeros_like(layer_keep)
        for i in range(ROWS):
            h, s = i // 2, i % 2
            for m, mask in enumerate((mid_mask, out_mask)):
                layer_keep[m, i : i + 1, :HID] = mask[h, s : s + 1, :].astype(jnp.float32) * keep_scale

        def masked(i, lanes):
            h, s = i // 2, i % 2
            kept = in_mask[h, s : s + 1, lanes].astype(jnp.float32) * keep_scale
            return (inputs[h, s, :, lanes] * kept).astype(jnp.bfloat16).astype(jnp.float32)

        by_time(dx, D_IN, 512, masked)
        column = lax.broadcasted_iota(jnp.int32, (STEPS * ROWS, 512), 1)
        value = jnp.where(column == D_IN, 1.0, dx[...])
        dx[...] = value
        o_left[:, :, pl.ds(SOURCE, 512)] = value.astype(jnp.bfloat16).reshape(CHUNKS, 2 * ROWS, 512)
        o_left[:, :, pl.ds(SOURCE + 512, 128)] = jnp.zeros((CHUNKS, 2 * ROWS, 128), jnp.bfloat16)

    def set_up_above():
        def masked(i, lanes):
            return cotangent[i // 2, i % 2, :, lanes].astype(jnp.float32) * layer_keep[1, i : i + 1, lanes]

        by_time(above, HID, WIDE, masked)

    def clear():
        hidden[...] = jnp.zeros_like(hidden)
        cell[...] = jnp.zeros_like(cell)

    def forward_pair(c, mask, with_one, o_hp, o_layer):
        column = lax.broadcasted_iota(jnp.int32, (ROWS, WIDE), 1)
        for j in range(2):
            rows = pl.ds(ROWS * j, ROWS)
            kept = keep_rows(c, j)
            hidden_prev = hidden[...] * kept
            cell_prev = cell[...] * kept
            left = hidden_prev.astype(jnp.bfloat16)
            gates = [
                dot(left, w_front[g]) + zx[c, rows, pl.ds(g * WIDE, WIDE)] for g in range(4)
            ]
            gate_in, gate_forget = sigmoid(gates[0]), sigmoid(gates[1])
            gate_cand, gate_out = jnp.tanh(gates[2]), sigmoid(gates[3])
            cell_now = gate_forget * cell_prev + gate_in * gate_cand
            cell_tanh = jnp.tanh(cell_now)
            hidden_now = (gate_out * cell_tanh).astype(jnp.bfloat16).astype(jnp.float32)
            cell[...] = cell_now
            hidden[...] = hidden_now
            stage_a[rows, :] = hidden_prev
            layer = hidden_now * mask
            if with_one:
                layer = jnp.where(column == HID, 1.0, layer)
            stage_b[rows, :] = layer
            zx[c, rows, pl.ds(0, WIDE)] = gate_cand * gate_in * (1.0 - gate_in)
            zx[c, rows, pl.ds(WIDE, WIDE)] = cell_prev * gate_forget * (1.0 - gate_forget)
            zx[c, rows, pl.ds(2 * WIDE, WIDE)] = gate_in * (1.0 - gate_cand * gate_cand)
            zx[c, rows, pl.ds(3 * WIDE, WIDE)] = cell_tanh * gate_out * (1.0 - gate_out)
            extra[c, rows, pl.ds(0, WIDE)] = gate_out * (1.0 - cell_tanh * cell_tanh)
            extra[c, rows, pl.ds(WIDE, WIDE)] = gate_forget * kept
        o_hp[c] = stage_a[...].astype(jnp.bfloat16)
        o_layer[c] = stage_b[...].astype(jnp.bfloat16)

    def backward_pair(c, upstream):
        for j in (1, 0):
            rows = pl.ds(ROWS * j, ROWS)
            total = hidden[...] + upstream[ROWS * j : ROWS * j + ROWS]
            out_grad = total * zx[c, rows, pl.ds(3 * WIDE, WIDE)]
            cell_total = cell[...] + total * extra[c, rows, pl.ds(0, WIDE)]
            cell[...] = cell_total * extra[c, rows, pl.ds(WIDE, WIDE)]
            grads = [cell_total * zx[c, rows, pl.ds(g * WIDE, WIDE)] for g in range(3)] + [out_grad]
            back = None
            for g in range(4):
                stage_z[rows, pl.ds(g * WIDE, WIDE)] = grads[g]
                part = dot(grads[g].astype(jnp.bfloat16), w_back[g])
                back = part if back is None else back + part
            hidden[...] = back * keep_rows(c, j)
        for g in range(4):
            dz[g, c] = stage_z[:, pl.ds(g * WIDE, WIDE)].astype(jnp.bfloat16)

    last = CHUNKS - 1
    groups = CHUNKS // GROUP

    @pl.when(pipe == LAYER_ONE)
    def _():
        me = LAYER_ONE
        start_spread(me)
        set_up()
        share_blocks(R_ONE)
        await_blocks(W_ONE)
        source = dx[:, :D_WIDE].astype(jnp.bfloat16)
        for g in range(4):
            zx[:, :, pl.ds(g * WIDE, WIDE)] = dot(source, w_back[g, :D_WIDE]).reshape(CHUNKS, 2 * ROWS, WIDE)
        receive_rest(R_ONE)
        clear()

        def ahead(c, carry):
            forward_pair(c, layer_keep[0], True, o_hp_one, o_u)
            copy_u(c).start()

            @pl.when((c >= LATER) & (c < LATER + TURNS))
            def _():
                pl.semaphore_signal(
                    go_on, inc=1, device_id={"pipe": SOURCE_GRAD, "dp": dp}, device_id_type=MESH
                )
                start_turn(me, c - LATER)

            @pl.when(c == LATER)
            def _():
                start_near(me)

            return carry

        lax.fori_loop(0, CHUNKS, ahead, 0)
        bulk = [
            copy_bulk(SOURCE_GRAD, o_u, 0, 0), copy_bulk(LAYER_TWO, o_u, 1, 0),
            copy_bulk(SOURCE_GRAD, o_hp_one, 2, 1), copy_bulk(LAYER_TWO, o_hp_one, 3, 1),
            copy_bulk(BETWEEN, o_hp_one, 4, 1),
        ]
        for copy in bulk:
            copy.start()
        await_blocks(R_ONE_T)
        clear()

        def behind(i, carry):
            c = last - i
            copy_du(c).wait_recv()
            mask = jnp.concatenate([layer_keep[0]] * 2, 0)
            backward_pair(c, du[c].astype(jnp.float32) * mask)
            copy_dz(SOURCE_GRAD, c).start()

            @pl.when(lax.rem(c, GROUP) == 0)
            def _():
                group = c // GROUP
                copy_part(LAYER_TWO, o_dz_one, group, 0, LAYER_TWO).start()
                copy_part(BETWEEN, o_dz_one, group, 1, BETWEEN).start()

            return carry

        lax.fori_loop(0, CHUNKS, behind, 0)
        own = pltpu.make_async_copy(dz.at[me], o_dz_one, local_sem.at[0])
        own.start()
        finish_rings(R_ONE)
        finish_spread(me)
        finish_blocks(FORWARD + BACKWARD, me)
        to(BETWEEN, o_u, o_u, u_send, u_recv.at[0]).wait_send()
        for copy in bulk:
            copy.wait_send()
        to(SOURCE_GRAD, dz, dz, dz_send, dz_recv.at[0]).wait_send()
        to(LAYER_TWO, dz.at[me], o_dz_one, part_send.at[0], part_recv.at[0]).wait_send()
        to(BETWEEN, dz.at[me], o_dz_one, part_send.at[1], part_recv.at[0]).wait_send()
        own.wait()

        copy_bulk(me, o_hp_two, 0, 2).wait_recv()
        for group in range(groups):
            copy_part(me, o_dz_two, group, 0, me).wait_recv()
            copy_dx(me, group, 0).wait_recv()

    @pl.when(pipe == LAYER_TWO)
    def _():
        me = LAYER_TWO
        start_spread(me)
        set_up()
        set_up_above()
        share_blocks(R_TWO)
        receive_rest(R_TWO)
        clear()

        def ahead(c, carry):
            copy_z(c).wait_recv()

            @pl.when((c >= LATER) & (c < LATER + TURNS))
            def _():
                start_turn(me, c - LATER)

            @pl.when(c == LATER)
            def _():
                start_near(me)

            forward_pair(c, layer_keep[1], False, o_hp_two, o_out)
            return carry

        lax.fori_loop(0, CHUNKS, ahead, 0)
        bulk = [
            copy_bulk(LAYER_ONE, o_hp_two, 0, 2), copy_bulk(SOURCE_GRAD, o_hp_two, 1, 2),
            copy_bulk(BETWEEN, o_hp_two, 2, 2), copy_bulk(BETWEEN, o_out, 3, 3),
        ]
        for copy in bulk:
            copy.start()
        await_blocks(R_TWO_T)
        clear()

        def behind(i, carry):
            c = last - i
            backward_pair(c, above[pl.ds(pl.multiple_of(c * 2 * ROWS, 2 * ROWS), 2 * ROWS), :])
            copy_dz(BETWEEN, c).start()

            @pl.when(lax.rem(c, GROUP) == 0)
            def _():
                group = c // GROUP
                copy_part(LAYER_ONE, o_dz_two, group, 0, LAYER_ONE).start()
                copy_part(SOURCE_GRAD, o_dz_two, group, 1, SOURCE_GRAD).start()

            return carry

        lax.fori_loop(0, CHUNKS, behind, 0)
        own = pltpu.make_async_copy(dz.at[me], o_dz_two, local_sem.at[0])
        own.start()
        finish_rings(R_TWO)
        finish_spread(me)
        finish_blocks(FORWARD + BACKWARD, me)
        for copy in bulk:
            copy.wait_send()
        to(BETWEEN, dz, dz, dz_send, dz_recv.at[0]).wait_send()
        to(LAYER_ONE, dz.at[me], o_dz_two, part_send.at[0], part_recv.at[0]).wait_send()
        to(SOURCE_GRAD, dz.at[me], o_dz_two, part_send.at[1], part_recv.at[0]).wait_send()
        own.wait()

        copy_bulk(me, o_u, 0, 0).wait_recv()
        copy_bulk(me, o_hp_one, 0, 1).wait_recv()
        for group in range(groups):
            copy_part(me, o_dz_one, group, 0, me).wait_recv()
            copy_dx(me, group, 0).wait_recv()

    @pl.when(pipe == BETWEEN)
    def _():
        me = BETWEEN
        start_spread(me)
        set_up()
        share_blocks(W_TWO)
        receive_rest(W_TWO)

        def ahead(c, carry):
            copy_u(c).wait_recv()
            for g in range(4):
                zx[c, :, pl.ds(g * WIDE, WIDE)] = dot(o_u[c], w_front[g])
            copy_z(c).start()

            @pl.when((c >= LATER) & (c < LATER + TURNS))
            def _():
                start_turn(me, c - LATER)

            @pl.when(c == LATER)
            def _():
                start_near(me)

            return carry

        lax.fori_loop(0, CHUNKS, ahead, 0)
        await_blocks(W_TWO_T)

        def behind(i, carry):
            c = last - i
            copy_dz(me, c).wait_recv()
            back = None
            for g in range(4):
                part = dot(dz[g, c], w_back[g])
                back = part if back is None else back + part
            du[c] = back.astype(jnp.bfloat16)
            copy_du(c).start()
            return carry

        lax.fori_loop(0, CHUNKS, behind, 0)
        own = pltpu.make_async_copy(dz.at[me], o_dz_two, local_sem.at[0])
        own.start()
        finish_rings(W_TWO)
        finish_spread(me)
        finish_blocks(FORWARD + BACKWARD, me)
        to(LAYER_TWO, zx, zx, z_send, z_recv.at[0]).wait_send()
        to(LAYER_ONE, du, du, du_send, du_recv.at[0]).wait_send()
        own.wait()

        copy_bulk(me, o_hp_one, 0, 1).wait_recv()
        copy_bulk(me, o_hp_two, 0, 2).wait_recv()
        copy_bulk(me, o_out, 0, 3).wait_recv()
        for group in range(groups):
            copy_part(me, o_dz_one, group, 0, me).wait_recv()
            copy_dx(me, group, 0).wait_recv()

    @pl.when(pipe == SOURCE_GRAD)
    def _():
        me = SOURCE_GRAD
        start_spread(me)
        set_up()

        def pass_on(turn, carry):
            pl.semaphore_wait(go_on, 1)
            start_turn(me, turn)
            return carry

        lax.fori_loop(0, TURNS, pass_on, 0)
        start_near(me)
        await_blocks(W_ONE_T)

        def behind(i, carry):
            c = last - i
            copy_dz(me, c).wait_recv()
            back = None
            for g in range(4):
                part = dot(dz[g, c], w_front[g, :, :512])
                back = part if back is None else back + part
            dx[pl.ds(pl.multiple_of(c * 2 * ROWS, 2 * ROWS), 2 * ROWS), :] = back

            @pl.when(lax.rem(c, GROUP) == 0)
            def _():
                group = c // GROUP
                copy_dx(LAYER_ONE, group, 0).start()
                copy_dx(LAYER_TWO, group, 1).start()
                copy_dx(BETWEEN, group, 2).start()

            return carry

        lax.fori_loop(0, CHUNKS, behind, 0)
        own = pltpu.make_async_copy(dz.at[me], o_dz_one, local_sem.at[0])
        own.start()
        own_dx = pltpu.make_async_copy(dx.at[:, pl.ds(me * 128, 128)], o_dx, local_sem.at[1])
        own_dx.start()
        finish_spread(me)
        finish_blocks(FORWARD + BACKWARD, me)
        for slot, pipe_to in enumerate((LAYER_ONE, LAYER_TWO, BETWEEN)):
            to(pipe_to, o_dx, o_dx, dx_send.at[slot], dx_recv.at[0]).wait_send()
        own.wait()
        own_dx.wait()

        copy_bulk(me, o_u, 0, 0).wait_recv()
        copy_bulk(me, o_hp_one, 0, 1).wait_recv()
        copy_bulk(me, o_hp_two, 0, 2).wait_recv()
        for group in range(groups):
            copy_part(me, o_dz_two, group, 0, me).wait_recv()


def relay(w_one, bias, tails, r_one, drop_one, r_two, drop_two, w_two, inputs, in_mask, mid_mask, out_mask, cotangent, resets):
    whole, away = pl.BlockSpec(memory_space=pltpu.VMEM), pl.BlockSpec(memory_space=pl.ANY)
    rows = (CHUNKS, 2 * ROWS, WIDE)
    half, full = jnp.bfloat16, jnp.float32
    shapes = [
        jax.ShapeDtypeStruct((CHUNKS, 2 * ROWS, UNITS * UNIT), half),
        jax.ShapeDtypeStruct(rows, half),
        jax.ShapeDtypeStruct((2,) + rows, half),
        jax.ShapeDtypeStruct((STEPS * ROWS, 128), full),
        jax.ShapeDtypeStruct((3, WIDE, WIDE), half),
        jax.ShapeDtypeStruct((WIDE, 512), half),
    ]
    dma = pltpu.SemaphoreType.DMA
    return pl.pallas_call(
        relay_kernel,
        out_shape=shapes,
        in_specs=[whole] * 3 + [away] * 5 + [whole] * 5
        + [pl.BlockSpec(memory_space=pltpu.SMEM)],
        out_specs=[whole] * 4 + [away] * 2,
        scratch_shapes=[
            pltpu.VMEM((DEEP, UNIT, HID), half),
            pltpu.VMEM((DEEP, UNIT, HID), jnp.int32),
            dma((2, DEEP)),
            pltpu.VMEM((3, WIDE, WIDE), half),
            pltpu.VMEM((D_WIDE, WIDE), half),
            pltpu.VMEM((2, UNIT, WIDE), half),
            pltpu.VMEM((D_IN, UNIT), full),
            pltpu.VMEM((512, UNIT), full),
            dma((2,)),
            pltpu.VMEM((4, WIDE, WIDE), half),
            pltpu.VMEM((4, WIDE, WIDE), half),
            pltpu.VMEM((CHUNKS, 2 * ROWS, 4 * WIDE), full),
            pltpu.VMEM((CHUNKS, 2 * ROWS, 2 * WIDE), full),
            pltpu.VMEM((4,) + rows, half),
            pltpu.VMEM(rows, half),
            pltpu.VMEM((STEPS * ROWS, 512), full),
            pltpu.VMEM((STEPS * ROWS, WIDE), full),
            pltpu.VMEM((STEPS, 128), full),
            pltpu.VMEM((STEPS * ROWS, 128), full),
            pltpu.VMEM((CHUNKS, 2 * ROWS, 128), full),
            pltpu.VMEM((2, ROWS, WIDE), full),
            pltpu.VMEM((ROWS, WIDE), full),
            pltpu.VMEM((ROWS, WIDE), full),
            pltpu.VMEM((2 * ROWS, WIDE), full),
            pltpu.VMEM((2 * ROWS, WIDE), full),
            pltpu.VMEM((2 * ROWS, 4 * WIDE), full),
            dma((8, 2)), dma((8, 4, 2)), dma((8,)),
            dma((2, 3)), dma((2, 3)), dma((2, 2, 4)), dma((2, 2, 4)), pltpu.SemaphoreType.REGULAR,
            dma, dma((CHUNKS,)), dma, dma((CHUNKS,)), dma, dma((CHUNKS,)), dma, dma((CHUNKS,)),
            dma((5,)), dma((4,)), dma((2,)), dma((CHUNKS // GROUP,)), dma((3,)), dma((CHUNKS // GROUP,)), dma((2,)),
        ],
        compiler_params=pltpu.CompilerParams(
            vmem_limit_bytes=60 << 20, collective_id=0, has_side_effects=True
        ),
        name="relay",
    )(w_one, bias, tails, r_one, drop_one, r_two, drop_two, w_two, inputs, in_mask, mid_mask, out_mask, cotangent, resets)


def reduce_kernel(
    left, dz, total, own, near, far, part, cross, share,
    near_send, near_recv, far_send, far_recv, part_send, part_recv, last_send, last_recv,
    cross_send, cross_recv, back_send, back_recv, wide_send, wide_recv, share_send, share_recv,
):
    pipe = lax.axis_index("pipe")
    dp = lax.axis_index("dp")
    z, x, y = dp // 16, lax.rem(dp // 4, 4), lax.rem(dp, 4)

    def device(z_, x_, y_):
        return {"pipe": pipe, "dp": z_ * 16 + lax.rem(x_ + 4, 4) * 4 + lax.rem(y_ + 4, 4)}

    along_x, along_y = (lambda d: device(z, x + d, y)), (lambda d: device(z, x, y + d))
    first, second = (along_x, along_y) * 2, (along_y, along_x) * 2
    place = ((x, y), (y, x)) * 2
    across = device(1 - z, x, y)
    size = (BIG, BIG, SMALL, SMALL)
    base = (0, 16 * BIG, THIRD + z * SHARE, THIRD + z * SHARE + 16 * SMALL)

    barrier = pltpu.get_barrier_semaphore()
    for target in (along_x(1), along_x(-1), along_y(1), along_y(-1), across):
        pl.semaphore_signal(barrier, inc=1, device_id=target, device_id_type=MESH)
    pl.semaphore_wait(barrier, 5)

    lanes_of = (pl.ds(0, WIDE), pl.ds(0, 640), pl.ds(640, 512))

    def unit(p, block, rel):
        a, b = place[p]
        index = lax.rem(a + block + 4, 4) * 4 + lax.rem(b + rel + 4, 4)
        return pl.ds(pl.multiple_of(base[p] + index * size[p], 16), size[p])

    def send(source, target, s, r, to):
        return pltpu.make_async_remote_copy(source, target, s, r, device_id=to, device_id_type=MESH)

    def add(target, rows, others, lanes=lanes_of[0]):
        def body(i, carry):
            span = pl.ds(pl.multiple_of(rows.start + i * 16, 16), 16)
            value = own[span, lanes].astype(jnp.float32)
            for ref in others:
                value = value + ref[pl.ds(pl.multiple_of(i * 16, 16), 16), lanes].astype(jnp.float32)
            target[span, lanes] = value.astype(jnp.bfloat16)
            return carry

        lax.fori_loop(0, rows.size // 16, body, 0)

    def product(u):
        columns = pl.ds(pl.multiple_of(u * UNIT, UNIT), UNIT)
        own[columns, :] = lax.dot_general(
            left[:, columns], dz[jnp.where((u >= U_TWO // UNIT) & (u < SOURCE // UNIT), 1, 0)], (((0,), (0,)), ((), ())),
            preferred_element_type=jnp.float32,
        ).astype(jnp.bfloat16)

    def products(start, count):
        def body(i, carry):
            product(start + i)
            return carry

        lax.fori_loop(0, count, body, 0)

    block_units = 4 * BIG // UNIT

    def block_products(p, block):
        products(p * 4 * block_units + lax.rem(place[p][0] + block + 4, 4) * block_units, block_units)

    side = {1: (2, 1), -1: (3, 0)}
    on_side = {1: (0, 1), -1: (3, 2)}
    slot = {1: 0, -1: 1}
    started = []

    def go(copy):
        copy.start()
        started.append(copy)

    def near_copy(p, d, k):
        at = (p, slot[d], k)
        return send(own.at[unit(p, 2, side[d][k])], near.at[at].at[pl.ds(0, size[p])], near_send.at[at],
                    near_recv.at[at], first[p](d))

    def far_copy(p, d, k, block=None):
        rel = (side[-d] + side[d])[k]
        at = (p, slot[d], rel)
        return send(own.at[unit(p, d if block is None else block, rel)], far.at[at].at[pl.ds(0, size[p])],
                    far_send.at[at], far_recv.at[at], first[p](d))

    def part_copy(p, d):
        lanes = lanes_of[1 if d == 1 else 2]
        at = (p, slot[d])
        return send(own.at[unit(p, 0, 2), lanes], part.at[at].at[pl.ds(0, size[p]), lanes], part_send.at[at],
                    part_recv.at[at], second[p](d))

    def last_copy(p, d, k):
        lanes = lanes_of[(2 - k) if d == 1 else (1 + k)]
        at = (p, slot[d], k)
        return send(own.at[unit(p, 0, d), lanes], part.at[p, 2 + slot[d]].at[pl.ds(0, size[p]), lanes],
                    last_send.at[at], last_recv.at[at], second[p](d))

    def cross_copy(p):
        return send(own.at[unit(p, 0, 0)], cross.at[p], cross_send.at[p], cross_recv.at[p], across)

    def share_copy(i):
        rows = pl.ds(pl.multiple_of(THIRD + (1 - z) * SHARE + i * UNIT, UNIT), UNIT)
        return send(own.at[rows], share.at[pl.ds(i * UNIT, UNIT)], share_send.at[i], share_recv.at[i], across)

    def share_back(half):
        rows = pl.ds(pl.multiple_of(THIRD + half * SHARE, UNIT), SHARE)
        return send(total.at[rows], total.at[rows], share_send.at[4], share_recv.at[4], across)

    def back_copy(p, d, rel=0, on=0):
        at = (p, slot[d], on)
        ref = total.at[unit(p, 0, rel), lanes_of[0 if not on else 1 if d == 1 else 2]]
        return send(ref, ref, back_send.at[at], back_recv.at[at], second[p](d))

    def wide_copy(p, d, rel, block=0, on=0):
        at = (p, slot[d], rel + 4 * on)
        ref = total.at[unit(p, block, rel)]
        return send(ref, ref, wide_send.at[at], wide_recv.at[at], first[p](d))

    def start_near(parts):
        for k in range(2):
            for p in parts:
                for d in (1, -1):
                    go(near_copy(p, d, k))

    def start_far(parts):
        for k in range(2):
            for p in parts:
                for d in (1, -1):
                    go(far_copy(p, d, k))

    def finish_near(parts):
        for k in range(2):
            for p in parts:
                for d in (1, -1):
                    near_copy(p, d, k).wait_recv()
                    add(own, unit(p, d, side[d][k]), [near.at[p, slot[d], k]])
                    go(far_copy(p, d, 2 + k))

    def collect(p, rel):
        for d in (1, -1):
            far_copy(p, d, (side[-d] + side[d]).index(rel), 0).wait_recv()
        add(own, unit(p, 0, rel), [far.at[p, 0, rel], far.at[p, 1, rel]])

    def start_second(parts):
        for p in parts:
            collect(p, 2)
            for d in (1, -1):
                go(part_copy(p, d))
        for rel, d in ((3, -1), (1, 1)):
            for p in parts:
                collect(p, rel)
                go(last_copy(p, d, 0))
        for p in parts:
            collect(p, 0)

    def finish_part(parts):
        for d in (1, -1):
            for p in parts:
                part_copy(p, d).wait_recv()
                add(own, unit(p, 0, d), [part.at[p, slot[d]]], lanes_of[1 if d == 1 else 2])
                go(last_copy(p, d, 1))

    def finish_second(parts, target):
        for p in parts:
            for d in (1, -1):
                for k in range(2):
                    last_copy(p, d, k).wait_recv()
            add(target, unit(p, 0, 0), [part.at[p, 2], part.at[p, 3]])

    def start_back(parts):
        for p in parts:
            for d in (1, -1):
                go(back_copy(p, d))
            for d in (1, -1):
                go(wide_copy(p, d, 0))

    def pass_back(parts):
        for d in (1, -1):
            for p in parts:
                back_copy(p, d, -d).wait_recv()
                go(back_copy(p, d, -d, 1))
                for e in (1, -1):
                    go(wide_copy(p, e, -d % 4))

    def finish_back(parts):
        for p in parts:
            for d in (1, -1):
                back_copy(p, d, 2, 1).wait_recv()
            for d in (1, -1):
                go(wide_copy(p, d, 2))

    def pass_wide(parts):
        for k in range(2):
            for d in (1, -1):
                for p in parts:
                    rel = on_side[d][k]
                    wide_copy(p, d, rel, -d).wait_recv()
                    go(wide_copy(p, d, rel, -d, 1))

    def finish_wide(parts):
        for p in parts:
            for d in (1, -1):
                for rel in range(4):
                    if rel not in on_side[d]:
                        wide_copy(p, d, rel, -d).wait_recv()
                for rel in on_side[d]:
                    wide_copy(p, d, rel, 2, 1).wait_recv()

    big, small = (0, 1), (2, 3)
    for p in big:
        block_products(p, 2)
    start_near(big)
    for i in range(4):
        product(THIRD // UNIT + (1 - z) * 4 + i)
        go(share_copy(i))
    for d in (1, -1):
        for p in big:
            block_products(p, d)
    start_far(big)
    for p in big:
        block_products(p, 0)
    products(THIRD // UNIT + z * 4, 4)
    finish_near(big)
    for i in range(4):
        share_copy(i).wait_recv()
        rows = pl.ds(pl.multiple_of(THIRD + z * SHARE + i * UNIT, UNIT), UNIT)
        add(own, rows, [share.at[pl.ds(i * UNIT, UNIT)]])
    start_near(small)
    start_far(small)
    start_second(big)
    finish_near(small)
    finish_part(big)
    start_second(small)
    finish_second(big, own)
    for p in big:
        go(cross_copy(p))
    finish_part(small)
    finish_second(small, total)
    start_back(small)
    pass_back(small)
    for p in big:
        cross_copy(p).wait_recv()
        add(total, unit(p, 0, 0), [cross.at[p]])
    start_back(big)
    finish_back(small)
    pass_wide(small)
    pass_back(big)
    finish_wide(small)
    go(share_back(z))
    finish_back(big)
    pass_wide(big)
    finish_wide(big)
    share_back(1 - z).wait_recv()
    for copy in started:
        copy.wait_send()


def reduce_over_dp(left, dz):
    whole = pl.BlockSpec(memory_space=pltpu.VMEM)
    half = jnp.bfloat16
    dma = pltpu.SemaphoreType.DMA
    return pl.pallas_call(
        reduce_kernel,
        out_shape=jax.ShapeDtypeStruct((UNITS * UNIT, WIDE), half),
        in_specs=[whole] * 2,
        out_specs=whole,
        scratch_shapes=[
            pltpu.VMEM((UNITS * UNIT, WIDE), half),
            pltpu.VMEM((4, 2, 2, BIG, WIDE), half),
            pltpu.VMEM((4, 2, 4, BIG, WIDE), half),
            pltpu.VMEM((4, 4, BIG, WIDE), half),
            pltpu.VMEM((2, BIG, WIDE), half),
            pltpu.VMEM((SHARE, WIDE), half),
            dma((4, 2, 2)), dma((4, 2, 2)), dma((4, 2, 4)), dma((4, 2, 4)), dma((4, 2)), dma((4, 2)),
            dma((4, 2, 2)), dma((4, 2, 2)), dma((2,)), dma((2,)), dma((4, 2, 2)), dma((4, 2, 2)),
            dma((4, 2, 8)), dma((4, 2, 8)), dma((5,)), dma((5,)),
        ],
        compiler_params=pltpu.CompilerParams(
            vmem_limit_bytes=60 << 20, collective_id=1, has_side_effects=True
        ),
        name="reduce",
    )(left, dz)


def finish_kernel(
    hp_one, source, u_two, hp_two, drop_one, drop_two, o_in_one, o_rec_one, o_bias_one, o_in_two, o_rec_two, o_bias_two
):
    step = pl.program_id(0)

    def wide(ref):
        return ref[:, :HID].astype(jnp.float32)

    o_rec_one[...] = wide(hp_one) * drop_one[...].astype(jnp.float32) * weight_scale
    o_rec_two[...] = wide(hp_two) * drop_two[...].astype(jnp.float32) * weight_scale
    o_in_one[...] = wide(source)
    o_in_two[...] = wide(u_two)

    @pl.when(step == D_IN // SLAB)
    def _():
        o_bias_one[...] = wide(source)[D_IN % SLAB : D_IN % SLAB + 1]

    @pl.when(step == HID // SLAB)
    def _():
        o_bias_two[...] = wide(u_two)[HID % SLAB : HID % SLAB + 1]


def finish(total, drop_one, drop_two):
    def units(first, last):
        return pl.BlockSpec((SLAB, WIDE), lambda i: (first + jnp.minimum(i, last), 0))

    def rows(last):
        return pl.BlockSpec((SLAB, HID), lambda i: (jnp.minimum(i, last), 0))

    one = pl.BlockSpec((1, HID), lambda i: (0, 0))
    count, short = WIDE // SLAB - 1, D_IN // SLAB
    square, line = jax.ShapeDtypeStruct((HID, HID), jnp.float32), jax.ShapeDtypeStruct((1, HID), jnp.float32)
    return pl.pallas_call(
        finish_kernel,
        grid=(count + 1,),
        in_specs=[
            units(HP_ONE // SLAB, count), units(SOURCE // SLAB, short), units(U_TWO // SLAB, count),
            units(HP_TWO // SLAB, count), rows(count), rows(count),
        ],
        out_specs=[rows(short), rows(count), one, rows(count), rows(count), one],
        out_shape=[jax.ShapeDtypeStruct((D_IN, HID), jnp.float32), square, line, square, square, line],
        compiler_params=pltpu.CompilerParams(vmem_limit_bytes=60 << 20),
        name="finish",
    )(total, total, total, total, drop_one, drop_two)


def local(
    inputs, resets, in_mask, mid_mask, out_mask,
    w_ih_one, w_hh_one, bias_one, drop_one, w_ih_two, w_hh_two, bias_two, drop_two, cotangent,
):
    pipe = lax.axis_index("pipe")
    bias = jnp.stack([bias_one, bias_two])
    last = WIDE - UNIT
    tails = jnp.stack([
        jnp.pad(w_hh_one[last:] * drop_one[last:].astype(jnp.bfloat16) * weight_scale, ((0, 2), (0, 2))),
        jnp.pad(w_hh_two[last:] * drop_two[last:].astype(jnp.bfloat16) * weight_scale, ((0, 2), (0, 2))),
        jnp.pad(jnp.concatenate([w_ih_two[last:], bias_two[None]], 0), ((0, 1), (0, 2))),
    ])
    left, out_two, dz, dx, _, _ = relay(
        w_ih_one, bias, tails, w_hh_one, drop_one, w_hh_two, drop_two, w_ih_two,
        inputs, in_mask, mid_mask, out_mask, cotangent, resets,
    )
    left = left.reshape(STEPS * ROWS, UNITS * UNIT)
    total = reduce_over_dp(left, dz.reshape(2, STEPS * ROWS, WIDE))

    u_two = left[:, U_TWO : U_TWO + WIDE].reshape(out_two.shape)
    layer = jnp.where(pipe < 2, u_two, out_two).reshape(STEPS, 2, 2, WIDE)[..., :HID]
    layer = lax.dynamic_index_in_dim(layer, pipe % 2, 1, keepdims=False)
    layer_outputs = jnp.swapaxes(layer, 0, 1)[None]
    grad_input = jnp.transpose(dx.reshape(STEPS, 2, 2, 128)[..., :100], (1, 2, 0, 3))
    keep_in = in_mask.astype(jnp.float32) * keep_scale
    keep_part = lax.dynamic_slice_in_dim(keep_in, pipe * 100, 100, 2)
    grad_input = grad_input * keep_part[:, :, None, :]

    in_one, rec_one, bias_one, in_two, rec_two, bias_two = finish(total, drop_one, drop_two)
    return (layer_outputs, grad_input, in_one, rec_one, bias_one[0], in_two, rec_two, bias_two[0])


def solution(mesh):
    placed = (
        P(None, "dp", None, None),
        P(None, "dp"),
        P(None, "dp", None),
        P(None, "dp", None),
        P(None, "dp", None),
        P(None, "pipe"),
        P(None, "pipe"),
        P("pipe"),
        P(None, "pipe"),
        P(None, "pipe"),
        P(None, "pipe"),
        P("pipe"),
        P(None, "pipe"),
        P(None, "dp", None, None),
    )
    return jax.shard_map(
        local,
        mesh=mesh,
        in_specs=placed,
        out_specs=(
            P("pipe", "dp", None, None),
            P(None, "dp", None, "pipe"),
            P(None, "pipe"),
            P(None, "pipe"),
            P("pipe"),
            P(None, "pipe"),
            P(None, "pipe"),
            P("pipe"),
        ),
        check_vma=False,
    )
```

```python
import functools

import jax
import jax.numpy as jnp
from jax import lax
from jax.experimental import pallas as pl
from jax.experimental.pallas import tpu as pltpu
from jax.sharding import PartitionSpec as P

MESH = pl.DeviceIdType.MESH
HID = 1150
WIDE = 1152
D_IN = 400
D_WIDE = 416
STEPS = 88
ROWS = 4
CHUNKS = 44
GROUP = 4
LATER = 3
TURNS = 36
UNIT = 128
HALF_UNIT = 64
UNITS = 32
HP_ONE, U_TWO, HP_TWO, SOURCE = 0, 1152, 2304, 3456
SOURCE_WIDE = 640
SLAB = 384
DEEP = 4
BIG, SMALL = 96, 16
THIRD = 32 * BIG
SHARE = 32 * SMALL

keep_scale = 4.0 / 3.0
weight_scale = 2.0

LAYER_ONE, SOURCE_GRAD, LAYER_TWO, BETWEEN = 0, 1, 2, 3
W_ONE, R_ONE, R_TWO, W_TWO, R_ONE_T, R_TWO_T, W_TWO_T, W_ONE_T = range(8)
USER = {
    W_ONE: LAYER_ONE,
    R_ONE: LAYER_ONE,
    R_TWO: LAYER_TWO,
    W_TWO: BETWEEN,
    R_ONE_T: LAYER_ONE,
    R_TWO_T: LAYER_TWO,
    W_TWO_T: BETWEEN,
    W_ONE_T: SOURCE_GRAD,
}
FORWARD = (W_ONE,)
BACKWARD = (R_TWO_T, W_TWO_T, R_ONE_T, W_ONE_T)


def sigmoid(value):
    return 0.5 * jnp.tanh(0.5 * value) + 0.5


def dot(left, right):
    return jnp.dot(left, right, preferred_element_type=jnp.float32)


def relay_kernel(
    plain_in, tails, r_one, drop_one, r_two, drop_two, w_two,
    inputs, in_mask, mid_mask, out_mask, cotangent, resets,
    o_left, o_out, o_dz, o_dx, turned, turned_in,
    raw_weights, raw_drop, raw_sem, plain, turn, small, apart, turn_sem,
    w_front, w_back, zx, extra, dz, du, dx, above, line, spread, keep, layer_keep, hidden, cell, stage_a, stage_b, stage_z,
    block_send, block_recv, block_local, cross_send, cross_recv, ring_send, ring_recv, go_on,
    u_send, u_recv, z_send, z_recv, dz_send, dz_recv, du_send, du_recv,
    bulk_send, bulk_recv, part_send, part_recv, dx_send, dx_recv, local_sem,
):
    o_hp_one, o_u, o_hp_two = (o_left.at[:, :, pl.ds(start, WIDE)] for start in (HP_ONE, U_TWO, HP_TWO))
    o_dz_one, o_dz_two = o_dz.at[0], o_dz.at[1]
    pipe = lax.axis_index("pipe")
    dp = lax.axis_index("dp")
    dp_count = lax.axis_size("dp")
    dp_far = lax.rem(dp + dp_count // 2, dp_count)

    barrier = pltpu.get_barrier_semaphore()
    for step in range(1, 4):
        pl.semaphore_signal(
            barrier, inc=1, device_id={"pipe": lax.rem(pipe + step, 4), "dp": dp}, device_id_type=MESH
        )
    for step in range(4):
        pl.semaphore_signal(
            barrier, inc=1, device_id={"pipe": lax.rem(pipe + step, 4), "dp": dp_far}, device_id_type=MESH
        )
    z, x, y = dp // 16, lax.rem(dp // 4, 4), lax.rem(dp, 4)
    rings = (
        lambda d: {"pipe": pipe, "dp": z * 16 + lax.rem(x + d + 4, 4) * 4 + y},
        lambda d: {"pipe": pipe, "dp": z * 16 + x * 4 + lax.rem(y + d + 4, 4)},
    )
    for ring in rings:
        for d in (1, -1):
            pl.semaphore_signal(barrier, inc=1, device_id=ring(d), device_id_type=MESH)

    def make_plain(m, also=None):
        weights, drop = ((r_one, drop_one), (r_two, drop_two), (w_two, None))[m]
        plain[m, :, pl.ds(HID // UNIT * UNIT, UNIT)] = jnp.zeros((WIDE, UNIT), jnp.bfloat16)

        def copies(i):
            slot = lax.rem(i, DEEP)
            span = pl.ds(pl.multiple_of(i * UNIT, UNIT), UNIT)
            return [
                pltpu.make_async_copy(array.at[span], raw.at[slot], raw_sem.at[k, slot])
                for k, (array, raw) in enumerate(((weights, raw_weights), (drop, raw_drop)))
                if array is not None
            ]

        def start(i):
            for copy in copies(i):
                copy.start()

        whole = HID // UNIT

        def body(i, carry):
            for copy in copies(i):
                copy.wait()
            slot = lax.rem(i, DEEP)
            value = raw_weights[slot]
            if drop is not None:
                value = value.astype(jnp.float32) * raw_drop[slot].astype(jnp.float32) * weight_scale
            plain[m, pl.ds(pl.multiple_of(i * UNIT, UNIT), UNIT), pl.ds(0, HID)] = value.astype(jnp.bfloat16)
            pl.when(i + DEEP < whole)(lambda: start(i + DEEP))
            if also is not None:
                also(i)
            return carry

        for i in range(DEEP):
            start(i)
        plain[m, pl.ds(whole * UNIT, UNIT)] = tails[m]
        lax.fori_loop(0, whole, body, 0)
        if also is not None:
            also(whole)

    def turn_copy(m, i, slot):
        rows = pl.ds(pl.multiple_of(i * UNIT, UNIT), UNIT)
        return pltpu.make_async_copy(turn.at[slot], turned.at[m, rows], turn_sem.at[slot])

    def make_turned(m, order, i):
        slot = lax.rem(order * (WIDE // UNIT) + i, 2)
        if order:
            turn_copy(m, i, slot).wait()
        else:
            pl.when(i >= 2)(lambda: turn_copy(m, i, slot).wait())
        value = plain[m, :, pl.ds(pl.multiple_of(i * UNIT, UNIT), UNIT)].astype(jnp.float32).T
        column = lax.broadcasted_iota(jnp.int32, (UNIT, WIDE), 1)
        turn[slot] = jnp.where(column < HID, value, 0.0).astype(jnp.bfloat16)
        turn_copy(m, i, slot).start()

    def turn_in_copy(i):
        slot = lax.rem(i, 2)
        rows = pl.ds(pl.multiple_of(i * UNIT, UNIT), UNIT)
        return pltpu.make_async_copy(turn.at[slot, :, pl.ds(0, 512)], turned_in.at[rows], turn_sem.at[slot])

    def make_turned_in(i, carry):
        small[...] = plain_in[:D_IN, pl.ds(pl.multiple_of(i * UNIT, UNIT), UNIT)].astype(jnp.float32)
        for q in range(4):
            apart[q * UNIT : q * UNIT + 100, :] = small[q * 100 : q * 100 + 100, :]
        pl.when(i >= 2)(lambda: turn_in_copy(i).wait())
        turn[lax.rem(i, 2), :, pl.ds(0, 512)] = apart[...].T.astype(jnp.bfloat16)
        turn_in_copy(i).start()
        return carry

    def finish_turned(m, order):
        def body(i, carry):
            make_turned(m, order, i)
            return carry

        lax.fori_loop(0, WIDE // UNIT, body, 0)
        for slot in range(2):
            turn_copy(m, 0, slot).wait()
        apart[...] = jnp.zeros_like(apart)
        lax.fori_loop(0, WIDE // UNIT, make_turned_in, 0)
        for i in range(2):
            turn_in_copy(i).wait()

    @pl.when(pipe >= 2)
    def _():
        make_plain(0)

    @pl.when(pipe < 2)
    def _():
        make_plain(2)

    pl.semaphore_wait(barrier, 11)

    blocks = {
        W_ONE: plain_in, R_ONE: plain.at[0], R_TWO: plain.at[1], W_TWO: plain.at[2],
        R_ONE_T: turned.at[0], R_TWO_T: turned.at[1], W_TWO_T: turned.at[2], W_ONE_T: turned_in,
    }

    def landing(kind, p):
        if kind == W_ONE:
            return w_back.at[p, pl.ds(0, D_WIDE)]
        if kind in (R_ONE, R_TWO, W_TWO):
            return w_front.at[p]
        if kind == W_ONE_T:
            return w_front.at[p, :, pl.ds(0, 512)]
        return w_back.at[p]

    def block_copies(kind, p, turn=None):
        user = USER[kind]
        source_ref, target = blocks[kind], landing(kind, p)
        if p == user:
            return [pltpu.make_async_copy(source_ref, target, block_local.at[kind])]
        if p // 2 == user // 2:
            return [
                pltpu.make_async_remote_copy(
                    source_ref, target, block_send.at[kind, 0], block_recv.at[kind, p, 0],
                    device_id={"pipe": user, "dp": dp}, device_id_type=MESH,
                )
            ]
        rows = source_ref.shape[0] // 2
        if turn is None:
            spans = [pl.ds(part * rows, rows) for part in range(2)]
        else:
            piece = rows // TURNS
            spans = [pl.ds(pl.multiple_of(part * rows + turn * piece, piece), piece) for part in range(2)]
        return [
            pltpu.make_async_remote_copy(
                source_ref.at[spans[part]], target.at[spans[part]],
                block_send.at[kind, part], block_recv.at[kind, p, part],
                device_id={"pipe": user, "dp": (dp, dp_far)[part]}, device_id_type=MESH,
            )
            for part in range(2)
        ]

    def rows_at(first, count=UNIT):
        return pl.ds(pl.multiple_of(first, 64), count)

    def part_rows(ring, step):
        place = (x, y)[ring]
        return UNIT * (1 + 4 * ring + lax.rem(place + step + 4, 4))

    def from_other_plane(kind):
        return [p for p in range(4) if p // 2 != USER[kind] // 2]

    def cross_copy(kind, p, k, slot):
        rows = rows_at((part_rows(0, 0), part_rows(1, 0), 0)[k])
        return pltpu.make_async_remote_copy(
            blocks[kind].at[rows], w_front.at[p, rows], cross_send.at[slot, k], cross_recv.at[p % 2, k],
            device_id={"pipe": USER[kind], "dp": (dp, dp_far)[p % 2]}, device_id_type=MESH,
        )

    def ring_copy(p, ring, d, on):
        k = 2 * on + (0 if d == 1 else 1)
        if on:
            rows = rows_at(part_rows(ring, -d) + (0 if d == 1 else HALF_UNIT), HALF_UNIT)
        else:
            rows = rows_at(part_rows(ring, 0))
        ref = w_front.at[p, rows]
        return pltpu.make_async_remote_copy(
            ref, ref, ring_send.at[p % 2, ring, k], ring_recv.at[p % 2, ring, k],
            device_id=rings[ring](d), device_id_type=MESH,
        )

    def ring_arrival(p, ring, d, on):
        k = 2 * on + (0 if d == 1 else 1)
        if on:
            rows = rows_at(part_rows(ring, 2) + (0 if d == 1 else HALF_UNIT), HALF_UNIT)
        else:
            rows = rows_at(part_rows(ring, -d))
        ref = w_front.at[p, rows]
        return pltpu.make_async_remote_copy(
            ref, ref, ring_send.at[p % 2, ring, k], ring_recv.at[p % 2, ring, k],
            device_id=rings[ring](d), device_id_type=MESH,
        )

    SPREAD = (W_TWO, R_TWO, R_ONE)

    def start_cross(me, kind, ks):
        slot = (R_TWO, W_TWO, R_ONE).index(kind) % 2
        for k in ks:
            cross_copy(kind, me, k, slot).start()

    def start_spread(me):
        if me // 2 == 1:
            start_cross(me, R_ONE, (0, 1))
            start_blocks(FORWARD, me)
            start_cross(me, R_ONE, (2,))
            make_plain(2, functools.partial(make_turned, 0, 0))
            block_copies(W_TWO, me)[0].start()
            make_plain(1, functools.partial(make_turned, 2, 1))
            block_copies(R_TWO, me)[0].start()
            finish_turned(1, 2)
        else:
            start_cross(me, W_TWO, (0, 1))
            start_blocks(FORWARD, me)
            make_plain(1, functools.partial(make_turned, 2, 0))
            start_cross(me, R_TWO, (0, 1))
            start_cross(me, W_TWO, (2,))
            start_cross(me, R_TWO, (2,))
            make_plain(0, functools.partial(make_turned, 1, 1))
            block_copies(R_ONE, me)[0].start()
            finish_turned(0, 2)

    def finish_spread(me):
        kinds = [kind for kind in SPREAD if me // 2 != USER[kind] // 2]
        for kind in kinds:
            slot = (R_TWO, W_TWO, R_ONE).index(kind) % 2
            for k in range(3):
                cross_copy(kind, me, k, slot).wait_send()
        for kind in SPREAD:
            if me // 2 == USER[kind] // 2 and me != USER[kind]:
                block_copies(kind, me)[0].wait_send()

    def share_blocks(kind):
        others = from_other_plane(kind)
        for ring in range(2):
            for p in others:
                cross_copy(kind, p, ring, 0).wait_recv()
                for d in (1, -1):
                    ring_copy(p, ring, d, 0).start()
        for d in (1, -1):
            for p in others:
                for ring in range(2):
                    ring_arrival(p, ring, d, 0).wait_recv()
                    ring_copy(p, ring, d, 1).start()

    def receive_rest(kind):
        me = USER[kind]
        others = from_other_plane(kind)
        for p in others:
            cross_copy(kind, p, 2, 0).wait_recv()
            for ring in range(2):
                for d in (1, -1):
                    ring_arrival(p, ring, d, 1).wait_recv()
        for p in (me, me ^ 1):
            copy = block_copies(kind, p)[0]
            if p == me:
                copy.wait()
            else:
                copy.wait_recv()

    def finish_rings(kind):
        for p in from_other_plane(kind):
            for ring in range(2):
                for d in (1, -1):
                    for on in range(2):
                        ring_copy(p, ring, d, on).wait_send()

    def start_blocks(kinds, p):
        for kind in kinds:
            for copy in block_copies(kind, p):
                copy.start()

    def start_near(p):
        for kind in BACKWARD:
            if p // 2 == USER[kind] // 2:
                for copy in block_copies(kind, p):
                    copy.start()

    def start_turn(p, turn):
        for kind in BACKWARD:
            if p // 2 != USER[kind] // 2:
                for copy in block_copies(kind, p, turn):
                    copy.start()

    def finish_blocks(kinds, p):
        for kind in kinds:
            if p != USER[kind]:
                for copy in block_copies(kind, p):
                    copy.wait_send()

    def await_blocks(kind):
        for p in range(4):
            for copy in block_copies(kind, p):
                if p == USER[kind]:
                    copy.wait()
                else:
                    copy.wait_recv()

    def to(pipe_to, source_ref, target, send, recv):
        return pltpu.make_async_remote_copy(
            source_ref, target, send, recv,
            device_id={"pipe": pipe_to, "dp": dp}, device_id_type=MESH,
        )

    def copy_u(c):
        return to(BETWEEN, o_u.at[c], o_u.at[c], u_send, u_recv.at[c])

    def copy_z(c):
        return to(LAYER_TWO, zx.at[c], zx.at[c], z_send, z_recv.at[c])

    def copy_dz(pipe_to, c):
        return to(pipe_to, dz.at[:, c], dz.at[:, c], dz_send, dz_recv.at[c])

    def copy_du(c):
        return to(LAYER_ONE, du.at[c], du.at[c], du_send, du_recv.at[c])

    def copy_part(pipe_to, output, group, slot, gate):
        span = pl.ds(group * GROUP, GROUP)
        return to(pipe_to, dz.at[gate, span], output.at[span], part_send.at[slot], part_recv.at[group])

    def copy_dx(pipe_to, group, slot):
        count = GROUP * 2 * ROWS
        span = pl.ds(pl.multiple_of(group * count, count), count)
        return to(
            pipe_to, dx.at[span, pl.ds(pipe_to * 128, 128)], o_dx.at[span], dx_send.at[slot], dx_recv.at[group]
        )

    def copy_bulk(pipe_to, ref, slot, which):
        return to(pipe_to, ref, ref, bulk_send.at[slot], bulk_recv.at[which])

    def keep_rows(c, j):
        return jnp.broadcast_to(keep[c, ROWS * j : ROWS * j + ROWS, 0:1], (ROWS, WIDE))

    def by_time(target, width, whole, value_of):
        for start in range(0, whole, 128):
            count = min(128, width - start)
            if count < 128:
                line[...] = jnp.zeros_like(line)
            for i in range(ROWS):
                value = value_of(i, slice(start, start + count))
                if count < 128:
                    line[:, :count] = value
                    value = line[...]
                spread[pl.ds(i, STEPS, stride=ROWS), :] = value
            target[:, start : start + 128] = spread[...]

    def set_up():
        shape = (CHUNKS, 2 * ROWS, 128)
        row = lax.broadcasted_iota(jnp.int32, shape, 1)
        time = 2 * lax.broadcasted_iota(jnp.int32, shape, 0) + row // ROWS
        stream = lax.rem(row, ROWS)
        reset = jnp.zeros(shape, jnp.int32)
        for i in range(ROWS):
            reset = jnp.where(stream == i, resets[i // 2, i % 2], reset)
        keep[...] = jnp.where(time == reset, 0.0, 1.0)
        layer_keep[...] = jnp.zeros_like(layer_keep)
        for i in range(ROWS):
            h, s = i // 2, i % 2
            for m, mask in enumerate((mid_mask, out_mask)):
                layer_keep[m, i : i + 1, :HID] = mask[h, s : s + 1, :].astype(jnp.float32) * keep_scale

        def masked(i, lanes):
            h, s = i // 2, i % 2
            kept = in_mask[h, s : s + 1, lanes].astype(jnp.float32) * keep_scale
            return (inputs[h, s, :, lanes] * kept).astype(jnp.bfloat16).astype(jnp.float32)

        by_time(dx, D_IN, 512, masked)
        column = lax.broadcasted_iota(jnp.int32, (STEPS * ROWS, 512), 1)
        value = jnp.where(column == D_IN, 1.0, dx[...])
        dx[...] = value
        o_left[:, :, pl.ds(SOURCE, 512)] = value.astype(jnp.bfloat16).reshape(CHUNKS, 2 * ROWS, 512)
        o_left[:, :, pl.ds(SOURCE + 512, 128)] = jnp.zeros((CHUNKS, 2 * ROWS, 128), jnp.bfloat16)

    def set_up_above():
        def masked(i, lanes):
            return cotangent[i // 2, i % 2, :, lanes].astype(jnp.float32) * layer_keep[1, i : i + 1, lanes]

        by_time(above, HID, WIDE, masked)

    def clear():
        hidden[...] = jnp.zeros_like(hidden)
        cell[...] = jnp.zeros_like(cell)

    def forward_pair(c, mask, with_one, o_hp, o_layer):
        column = lax.broadcasted_iota(jnp.int32, (ROWS, WIDE), 1)
        for j in range(2):
            rows = pl.ds(ROWS * j, ROWS)
            kept = keep_rows(c, j)
            hidden_prev = hidden[...] * kept
            cell_prev = cell[...] * kept
            left = hidden_prev.astype(jnp.bfloat16)
            gates = [
                dot(left, w_front[g]) + zx[c, rows, pl.ds(g * WIDE, WIDE)] for g in range(4)
            ]
            gate_in, gate_forget = sigmoid(gates[0]), sigmoid(gates[1])
            gate_cand, gate_out = jnp.tanh(gates[2]), sigmoid(gates[3])
            cell_now = gate_forget * cell_prev + gate_in * gate_cand
            cell_tanh = jnp.tanh(cell_now)
            hidden_now = (gate_out * cell_tanh).astype(jnp.bfloat16).astype(jnp.float32)
            cell[...] = cell_now
            hidden[...] = hidden_now
            stage_a[rows, :] = hidden_prev
            layer = hidden_now * mask
            if with_one:
                layer = jnp.where(column == HID, 1.0, layer)
            stage_b[rows, :] = layer
            zx[c, rows, pl.ds(0, WIDE)] = gate_cand * gate_in * (1.0 - gate_in)
            zx[c, rows, pl.ds(WIDE, WIDE)] = cell_prev * gate_forget * (1.0 - gate_forget)
            zx[c, rows, pl.ds(2 * WIDE, WIDE)] = gate_in * (1.0 - gate_cand * gate_cand)
            zx[c, rows, pl.ds(3 * WIDE, WIDE)] = cell_tanh * gate_out * (1.0 - gate_out)
            extra[c, rows, pl.ds(0, WIDE)] = gate_out * (1.0 - cell_tanh * cell_tanh)
            extra[c, rows, pl.ds(WIDE, WIDE)] = gate_forget * kept
        o_hp[c] = stage_a[...].astype(jnp.bfloat16)
        o_layer[c] = stage_b[...].astype(jnp.bfloat16)

    def backward_pair(c, upstream):
        for j in (1, 0):
            rows = pl.ds(ROWS * j, ROWS)
            total = hidden[...] + upstream[ROWS * j : ROWS * j + ROWS]
            out_grad = total * zx[c, rows, pl.ds(3 * WIDE, WIDE)]
            cell_total = cell[...] + total * extra[c, rows, pl.ds(0, WIDE)]
            cell[...] = cell_total * extra[c, rows, pl.ds(WIDE, WIDE)]
            grads = [cell_total * zx[c, rows, pl.ds(g * WIDE, WIDE)] for g in range(3)] + [out_grad]
            back = None
            for g in range(4):
                stage_z[rows, pl.ds(g * WIDE, WIDE)] = grads[g]
                part = dot(grads[g].astype(jnp.bfloat16), w_back[g])
                back = part if back is None else back + part
            hidden[...] = back * keep_rows(c, j)
        for g in range(4):
            dz[g, c] = stage_z[:, pl.ds(g * WIDE, WIDE)].astype(jnp.bfloat16)

    last = CHUNKS - 1
    groups = CHUNKS // GROUP

    @pl.when(pipe == LAYER_ONE)
    def _():
        me = LAYER_ONE
        start_spread(me)
        set_up()
        share_blocks(R_ONE)
        await_blocks(W_ONE)
        source = dx[:, :D_WIDE].astype(jnp.bfloat16)
        for g in range(4):
            zx[:, :, pl.ds(g * WIDE, WIDE)] = dot(source, w_back[g, :D_WIDE]).reshape(CHUNKS, 2 * ROWS, WIDE)
        receive_rest(R_ONE)
        clear()

        def ahead(c, carry):
            forward_pair(c, layer_keep[0], True, o_hp_one, o_u)
            copy_u(c).start()

            @pl.when((c >= LATER) & (c < LATER + TURNS))
            def _():
                pl.semaphore_signal(
                    go_on, inc=1, device_id={"pipe": SOURCE_GRAD, "dp": dp}, device_id_type=MESH
                )
                start_turn(me, c - LATER)

            @pl.when(c == LATER)
            def _():
                start_near(me)

            return carry

        lax.fori_loop(0, CHUNKS, ahead, 0)
        bulk = [
            copy_bulk(SOURCE_GRAD, o_u, 0, 0), copy_bulk(LAYER_TWO, o_u, 1, 0),
            copy_bulk(SOURCE_GRAD, o_hp_one, 2, 1), copy_bulk(LAYER_TWO, o_hp_one, 3, 1),
            copy_bulk(BETWEEN, o_hp_one, 4, 1),
        ]
        for copy in bulk:
            copy.start()
        await_blocks(R_ONE_T)
        clear()

        def behind(i, carry):
            c = last - i
            copy_du(c).wait_recv()
            mask = jnp.concatenate([layer_keep[0]] * 2, 0)
            backward_pair(c, du[c].astype(jnp.float32) * mask)
            copy_dz(SOURCE_GRAD, c).start()

            @pl.when(lax.rem(c, GROUP) == 0)
            def _():
                group = c // GROUP
                copy_part(LAYER_TWO, o_dz_one, group, 0, LAYER_TWO).start()
                copy_part(BETWEEN, o_dz_one, group, 1, BETWEEN).start()

            return carry

        lax.fori_loop(0, CHUNKS, behind, 0)
        own = pltpu.make_async_copy(dz.at[me], o_dz_one, local_sem.at[0])
        own.start()
        finish_rings(R_ONE)
        finish_spread(me)
        finish_blocks(FORWARD + BACKWARD, me)
        to(BETWEEN, o_u, o_u, u_send, u_recv.at[0]).wait_send()
        for copy in bulk:
            copy.wait_send()
        to(SOURCE_GRAD, dz, dz, dz_send, dz_recv.at[0]).wait_send()
        to(LAYER_TWO, dz.at[me], o_dz_one, part_send.at[0], part_recv.at[0]).wait_send()
        to(BETWEEN, dz.at[me], o_dz_one, part_send.at[1], part_recv.at[0]).wait_send()
        own.wait()

        copy_bulk(me, o_hp_two, 0, 2).wait_recv()
        for group in range(groups):
            copy_part(me, o_dz_two, group, 0, me).wait_recv()
            copy_dx(me, group, 0).wait_recv()

    @pl.when(pipe == LAYER_TWO)
    def _():
        me = LAYER_TWO
        start_spread(me)
        set_up()
        set_up_above()
        share_blocks(R_TWO)
        receive_rest(R_TWO)
        clear()

        def ahead(c, carry):
            copy_z(c).wait_recv()

            @pl.when((c >= LATER) & (c < LATER + TURNS))
            def _():
                start_turn(me, c - LATER)

            @pl.when(c == LATER)
            def _():
                start_near(me)

            forward_pair(c, layer_keep[1], False, o_hp_two, o_out)
            return carry

        lax.fori_loop(0, CHUNKS, ahead, 0)
        bulk = [
            copy_bulk(LAYER_ONE, o_hp_two, 0, 2), copy_bulk(SOURCE_GRAD, o_hp_two, 1, 2),
            copy_bulk(BETWEEN, o_hp_two, 2, 2), copy_bulk(BETWEEN, o_out, 3, 3),
        ]
        for copy in bulk:
            copy.start()
        await_blocks(R_TWO_T)
        clear()

        def behind(i, carry):
            c = last - i
            backward_pair(c, above[pl.ds(pl.multiple_of(c * 2 * ROWS, 2 * ROWS), 2 * ROWS), :])
            copy_dz(BETWEEN, c).start()

            @pl.when(lax.rem(c, GROUP) == 0)
            def _():
                group = c // GROUP
                copy_part(LAYER_ONE, o_dz_two, group, 0, LAYER_ONE).start()
                copy_part(SOURCE_GRAD, o_dz_two, group, 1, SOURCE_GRAD).start()

            return carry

        lax.fori_loop(0, CHUNKS, behind, 0)
        own = pltpu.make_async_copy(dz.at[me], o_dz_two, local_sem.at[0])
        own.start()
        finish_rings(R_TWO)
        finish_spread(me)
        finish_blocks(FORWARD + BACKWARD, me)
        for copy in bulk:
            copy.wait_send()
        to(BETWEEN, dz, dz, dz_send, dz_recv.at[0]).wait_send()
        to(LAYER_ONE, dz.at[me], o_dz_two, part_send.at[0], part_recv.at[0]).wait_send()
        to(SOURCE_GRAD, dz.at[me], o_dz_two, part_send.at[1], part_recv.at[0]).wait_send()
        own.wait()

        copy_bulk(me, o_u, 0, 0).wait_recv()
        copy_bulk(me, o_hp_one, 0, 1).wait_recv()
        for group in range(groups):
            copy_part(me, o_dz_one, group, 0, me).wait_recv()
            copy_dx(me, group, 0).wait_recv()

    @pl.when(pipe == BETWEEN)
    def _():
        me = BETWEEN
        start_spread(me)
        set_up()
        share_blocks(W_TWO)
        receive_rest(W_TWO)

        def ahead(c, carry):
            copy_u(c).wait_recv()
            for g in range(4):
                zx[c, :, pl.ds(g * WIDE, WIDE)] = dot(o_u[c], w_front[g])
            copy_z(c).start()

            @pl.when((c >= LATER) & (c < LATER + TURNS))
            def _():
                start_turn(me, c - LATER)

            @pl.when(c == LATER)
            def _():
                start_near(me)

            return carry

        lax.fori_loop(0, CHUNKS, ahead, 0)
        await_blocks(W_TWO_T)

        def behind(i, carry):
            c = last - i
            copy_dz(me, c).wait_recv()
            back = None
            for g in range(4):
                part = dot(dz[g, c], w_back[g])
                back = part if back is None else back + part
            du[c] = back.astype(jnp.bfloat16)
            copy_du(c).start()
            return carry

        lax.fori_loop(0, CHUNKS, behind, 0)
        own = pltpu.make_async_copy(dz.at[me], o_dz_two, local_sem.at[0])
        own.start()
        finish_rings(W_TWO)
        finish_spread(me)
        finish_blocks(FORWARD + BACKWARD, me)
        to(LAYER_TWO, zx, zx, z_send, z_recv.at[0]).wait_send()
        to(LAYER_ONE, du, du, du_send, du_recv.at[0]).wait_send()
        own.wait()

        copy_bulk(me, o_hp_one, 0, 1).wait_recv()
        copy_bulk(me, o_hp_two, 0, 2).wait_recv()
        copy_bulk(me, o_out, 0, 3).wait_recv()
        for group in range(groups):
            copy_part(me, o_dz_one, group, 0, me).wait_recv()
            copy_dx(me, group, 0).wait_recv()

    @pl.when(pipe == SOURCE_GRAD)
    def _():
        me = SOURCE_GRAD
        start_spread(me)
        set_up()

        def pass_on(turn, carry):
            pl.semaphore_wait(go_on, 1)
            start_turn(me, turn)
            return carry

        lax.fori_loop(0, TURNS, pass_on, 0)
        start_near(me)
        await_blocks(W_ONE_T)

        def behind(i, carry):
            c = last - i
            copy_dz(me, c).wait_recv()
            back = None
            for g in range(4):
                part = dot(dz[g, c], w_front[g, :, :512])
                back = part if back is None else back + part
            dx[pl.ds(pl.multiple_of(c * 2 * ROWS, 2 * ROWS), 2 * ROWS), :] = back

            @pl.when(lax.rem(c, GROUP) == 0)
            def _():
                group = c // GROUP
                copy_dx(LAYER_ONE, group, 0).start()
                copy_dx(LAYER_TWO, group, 1).start()
                copy_dx(BETWEEN, group, 2).start()

            return carry

        lax.fori_loop(0, CHUNKS, behind, 0)
        own = pltpu.make_async_copy(dz.at[me], o_dz_one, local_sem.at[0])
        own.start()
        own_dx = pltpu.make_async_copy(dx.at[:, pl.ds(me * 128, 128)], o_dx, local_sem.at[1])
        own_dx.start()
        finish_spread(me)
        finish_blocks(FORWARD + BACKWARD, me)
        for slot, pipe_to in enumerate((LAYER_ONE, LAYER_TWO, BETWEEN)):
            to(pipe_to, o_dx, o_dx, dx_send.at[slot], dx_recv.at[0]).wait_send()
        own.wait()
        own_dx.wait()

        copy_bulk(me, o_u, 0, 0).wait_recv()
        copy_bulk(me, o_hp_one, 0, 1).wait_recv()
        copy_bulk(me, o_hp_two, 0, 2).wait_recv()
        for group in range(groups):
            copy_part(me, o_dz_two, group, 0, me).wait_recv()


def relay(w_one, tails, r_one, drop_one, r_two, drop_two, w_two, inputs, in_mask, mid_mask, out_mask, cotangent, resets):
    whole, away = pl.BlockSpec(memory_space=pltpu.VMEM), pl.BlockSpec(memory_space=pl.ANY)
    rows = (CHUNKS, 2 * ROWS, WIDE)
    half, full = jnp.bfloat16, jnp.float32
    shapes = [
        jax.ShapeDtypeStruct((CHUNKS, 2 * ROWS, UNITS * UNIT), half),
        jax.ShapeDtypeStruct(rows, half),
        jax.ShapeDtypeStruct((2,) + rows, half),
        jax.ShapeDtypeStruct((STEPS * ROWS, 128), full),
        jax.ShapeDtypeStruct((3, WIDE, WIDE), half),
        jax.ShapeDtypeStruct((WIDE, 512), half),
    ]
    dma = pltpu.SemaphoreType.DMA
    return pl.pallas_call(
        relay_kernel,
        out_shape=shapes,
        in_specs=[whole] * 2 + [away] * 5 + [whole] * 5
        + [pl.BlockSpec(memory_space=pltpu.SMEM)],
        out_specs=[whole] * 4 + [away] * 2,
        scratch_shapes=[
            pltpu.VMEM((DEEP, UNIT, HID), half),
            pltpu.VMEM((DEEP, UNIT, HID), jnp.int32),
            dma((2, DEEP)),
            pltpu.VMEM((3, WIDE, WIDE), half),
            pltpu.VMEM((2, UNIT, WIDE), half),
            pltpu.VMEM((D_IN, UNIT), full),
            pltpu.VMEM((512, UNIT), full),
            dma((2,)),
            pltpu.VMEM((4, WIDE, WIDE), half),
            pltpu.VMEM((4, WIDE, WIDE), half),
            pltpu.VMEM((CHUNKS, 2 * ROWS, 4 * WIDE), full),
            pltpu.VMEM((CHUNKS, 2 * ROWS, 2 * WIDE), full),
            pltpu.VMEM((4,) + rows, half),
            pltpu.VMEM(rows, half),
            pltpu.VMEM((STEPS * ROWS, 512), full),
            pltpu.VMEM((STEPS * ROWS, WIDE), full),
            pltpu.VMEM((STEPS, 128), full),
            pltpu.VMEM((STEPS * ROWS, 128), full),
            pltpu.VMEM((CHUNKS, 2 * ROWS, 128), full),
            pltpu.VMEM((2, ROWS, WIDE), full),
            pltpu.VMEM((ROWS, WIDE), full),
            pltpu.VMEM((ROWS, WIDE), full),
            pltpu.VMEM((2 * ROWS, WIDE), full),
            pltpu.VMEM((2 * ROWS, WIDE), full),
            pltpu.VMEM((2 * ROWS, 4 * WIDE), full),
            dma((8, 2)), dma((8, 4, 2)), dma((8,)),
            dma((2, 3)), dma((2, 3)), dma((2, 2, 4)), dma((2, 2, 4)), pltpu.SemaphoreType.REGULAR,
            dma, dma((CHUNKS,)), dma, dma((CHUNKS,)), dma, dma((CHUNKS,)), dma, dma((CHUNKS,)),
            dma((5,)), dma((4,)), dma((2,)), dma((CHUNKS // GROUP,)), dma((3,)), dma((CHUNKS // GROUP,)), dma((2,)),
        ],
        compiler_params=pltpu.CompilerParams(
            vmem_limit_bytes=60 << 20, collective_id=0, has_side_effects=True
        ),
        name="relay",
    )(w_one, tails, r_one, drop_one, r_two, drop_two, w_two, inputs, in_mask, mid_mask, out_mask, cotangent, resets)


def reduce_kernel(
    left, dz, total, own, near, far, part, cross, share,
    near_send, near_recv, far_send, far_recv, part_send, part_recv, last_send, last_recv,
    cross_send, cross_recv, back_send, back_recv, wide_send, wide_recv, share_send, share_recv, own_sem,
):
    pipe = lax.axis_index("pipe")
    dp = lax.axis_index("dp")
    z, x, y = dp // 16, lax.rem(dp // 4, 4), lax.rem(dp, 4)

    def device(z_, x_, y_):
        return {"pipe": pipe, "dp": z_ * 16 + lax.rem(x_ + 4, 4) * 4 + lax.rem(y_ + 4, 4)}

    along_x, along_y = (lambda d: device(z, x + d, y)), (lambda d: device(z, x, y + d))
    first, second = (along_x, along_y) * 2, (along_y, along_x) * 2
    place = ((x, y), (y, x)) * 2
    across = device(1 - z, x, y)
    size = (BIG, BIG, SMALL, SMALL)
    base = (0, 16 * BIG, THIRD + z * SHARE, THIRD + z * SHARE + 16 * SMALL)

    barrier = pltpu.get_barrier_semaphore()
    for target in (along_x(1), along_x(-1), along_y(1), along_y(-1), across):
        pl.semaphore_signal(barrier, inc=1, device_id=target, device_id_type=MESH)
    pl.semaphore_wait(barrier, 5)

    lanes_of = (pl.ds(0, WIDE), pl.ds(0, 640), pl.ds(640, 512))

    def unit(p, block, rel):
        a, b = place[p]
        index = lax.rem(a + block + 4, 4) * 4 + lax.rem(b + rel + 4, 4)
        return pl.ds(pl.multiple_of(base[p] + index * size[p], 16), size[p])

    def send(source, target, s, r, to):
        return pltpu.make_async_remote_copy(source, target, s, r, device_id=to, device_id_type=MESH)

    def add(rows, others, lanes=lanes_of[0]):
        def body(i, carry):
            span = pl.ds(pl.multiple_of(rows.start + i * 16, 16), 16)
            value = own[span, lanes].astype(jnp.float32)
            for ref in others:
                value = value + ref[pl.ds(pl.multiple_of(i * 16, 16), 16), lanes].astype(jnp.float32)
            own[span, lanes] = value.astype(jnp.bfloat16)
            return carry

        lax.fori_loop(0, rows.size // 16, body, 0)

    def product(u):
        columns = pl.ds(pl.multiple_of(u * UNIT, UNIT), UNIT)
        own[columns, :] = lax.dot_general(
            left[:, columns], dz[jnp.where((u >= U_TWO // UNIT) & (u < SOURCE // UNIT), 1, 0)], (((0,), (0,)), ((), ())),
            preferred_element_type=jnp.float32,
        ).astype(jnp.bfloat16)

    def products(start, count):
        def body(i, carry):
            product(start + i)
            return carry

        lax.fori_loop(0, count, body, 0)

    block_units = 4 * BIG // UNIT

    def block_products(p, block):
        products(p * 4 * block_units + lax.rem(place[p][0] + block + 4, 4) * block_units, block_units)

    side = {1: (2, 1), -1: (3, 0)}
    on_side = {1: (0, 1), -1: (3, 2)}
    slot = {1: 0, -1: 1}
    started = []

    def go(copy):
        copy.start()
        started.append(copy)

    def near_copy(p, d, k):
        at = (p, slot[d], k)
        return send(own.at[unit(p, 2, side[d][k])], near.at[at].at[pl.ds(0, size[p])], near_send.at[at],
                    near_recv.at[at], first[p](d))

    def far_copy(p, d, k, block=None):
        rel = (side[-d] + side[d])[k]
        at = (p, slot[d], rel)
        return send(own.at[unit(p, d if block is None else block, rel)], far.at[at].at[pl.ds(0, size[p])],
                    far_send.at[at], far_recv.at[at], first[p](d))

    def part_copy(p, d):
        lanes = lanes_of[1 if d == 1 else 2]
        at = (p, slot[d])
        return send(own.at[unit(p, 0, 2), lanes], part.at[at].at[pl.ds(0, size[p]), lanes], part_send.at[at],
                    part_recv.at[at], second[p](d))

    def last_copy(p, d, k):
        lanes = lanes_of[(2 - k) if d == 1 else (1 + k)]
        at = (p, slot[d], k)
        return send(own.at[unit(p, 0, d), lanes], part.at[p, 2 + slot[d]].at[pl.ds(0, size[p]), lanes],
                    last_send.at[at], last_recv.at[at], second[p](d))

    def cross_copy(p):
        return send(own.at[unit(p, 0, 0)], cross.at[p], cross_send.at[p], cross_recv.at[p], across)

    def share_copy(i):
        rows = pl.ds(pl.multiple_of(THIRD + (1 - z) * SHARE + i * UNIT, UNIT), UNIT)
        return send(own.at[rows], share.at[pl.ds(i * UNIT, UNIT)], share_send.at[i], share_recv.at[i], across)

    def share_back(half):
        rows = pl.ds(pl.multiple_of(THIRD + half * SHARE, UNIT), SHARE)
        return send(total.at[rows], total.at[rows], share_send.at[4], share_recv.at[4], across)

    def back_copy(p, d, rel=0, on=0):
        at = (p, slot[d], on)
        lanes = lanes_of[0 if not on else 1 if d == 1 else 2]
        ref = total.at[unit(p, 0, rel), lanes]
        source = own.at[unit(p, 0, rel), lanes] if rel == 0 else ref
        return send(source, ref, back_send.at[at], back_recv.at[at], second[p](d))

    def wide_copy(p, d, rel, block=0, on=0):
        at = (p, slot[d], rel + 4 * on)
        ref = total.at[unit(p, block, rel)]
        source = own.at[unit(p, block, rel)] if block == 0 and rel == 0 else ref
        return send(source, ref, wide_send.at[at], wide_recv.at[at], first[p](d))

    def start_near(parts):
        for k in range(2):
            for p in parts:
                for d in (1, -1):
                    go(near_copy(p, d, k))

    def start_far(parts):
        for k in range(2):
            for p in parts:
                for d in (1, -1):
                    go(far_copy(p, d, k))

    def finish_near(parts):
        for k in range(2):
            for p in parts:
                for d in (1, -1):
                    near_copy(p, d, k).wait_recv()
                    add(unit(p, d, side[d][k]), [near.at[p, slot[d], k]])
                    go(far_copy(p, d, 2 + k))

    def collect(p, rel):
        for d in (1, -1):
            far_copy(p, d, (side[-d] + side[d]).index(rel), 0).wait_recv()
        add(unit(p, 0, rel), [far.at[p, 0, rel], far.at[p, 1, rel]])

    def start_second(parts):
        for p in parts:
            collect(p, 2)
            for d in (1, -1):
                go(part_copy(p, d))
        for rel, d in ((3, -1), (1, 1)):
            for p in parts:
                collect(p, rel)
                go(last_copy(p, d, 0))
        for p in parts:
            collect(p, 0)

    def finish_part(parts):
        for d in (1, -1):
            for p in parts:
                part_copy(p, d).wait_recv()
                add(unit(p, 0, d), [part.at[p, slot[d]]], lanes_of[1 if d == 1 else 2])
                go(last_copy(p, d, 1))

    def finish_second(parts):
        for p in parts:
            for d in (1, -1):
                for k in range(2):
                    last_copy(p, d, k).wait_recv()
            add(unit(p, 0, 0), [part.at[p, 2], part.at[p, 3]])

    def keep_copy(p):
        rows = unit(p, 0, 0)
        return pltpu.make_async_copy(own.at[rows], total.at[rows], own_sem.at[p])

    def start_back(parts):
        for p in parts:
            for d in (1, -1):
                go(back_copy(p, d))
            for d in (1, -1):
                go(wide_copy(p, d, 0))
            keep_copy(p).start()

    def pass_back(parts):
        for d in (1, -1):
            for p in parts:
                back_copy(p, d, -d).wait_recv()
                go(back_copy(p, d, -d, 1))
                for e in (1, -1):
                    go(wide_copy(p, e, -d % 4))

    def finish_back(parts):
        for p in parts:
            for d in (1, -1):
                back_copy(p, d, 2, 1).wait_recv()
            for d in (1, -1):
                go(wide_copy(p, d, 2))

    def pass_wide(parts):
        for k in range(2):
            for d in (1, -1):
                for p in parts:
                    rel = on_side[d][k]
                    wide_copy(p, d, rel, -d).wait_recv()
                    go(wide_copy(p, d, rel, -d, 1))

    def finish_wide(parts):
        for p in parts:
            for d in (1, -1):
                for rel in range(4):
                    if rel not in on_side[d]:
                        wide_copy(p, d, rel, -d).wait_recv()
                for rel in on_side[d]:
                    wide_copy(p, d, rel, 2, 1).wait_recv()

    big, small = (0, 1), (2, 3)
    for p in big:
        block_products(p, 2)
    start_near(big)
    for i in range(4):
        product(THIRD // UNIT + (1 - z) * 4 + i)
        go(share_copy(i))
    for d in (1, -1):
        for p in big:
            block_products(p, d)
    start_far(big)
    for p in big:
        block_products(p, 0)
    products(THIRD // UNIT + z * 4, 4)
    finish_near(big)
    for i in range(4):
        share_copy(i).wait_recv()
        rows = pl.ds(pl.multiple_of(THIRD + z * SHARE + i * UNIT, UNIT), UNIT)
        add(rows, [share.at[pl.ds(i * UNIT, UNIT)]])
    start_near(small)
    start_far(small)
    start_second(big)
    finish_near(small)
    finish_part(big)
    start_second(small)
    finish_second(big)
    for p in big:
        cross_copy(p).start()
    finish_part(small)
    finish_second(small)
    start_back(small)
    pass_back(small)
    for p in big:
        cross_copy(p).wait()
        add(unit(p, 0, 0), [cross.at[p]])
    start_back(big)
    finish_back(small)
    pass_wide(small)
    pass_back(big)
    finish_wide(small)
    for p in small:
        keep_copy(p).wait()
    go(share_back(z))
    finish_back(big)
    pass_wide(big)
    finish_wide(big)
    for p in big:
        keep_copy(p).wait()
    share_back(1 - z).wait_recv()
    for copy in started:
        copy.wait_send()


def reduce_over_dp(left, dz):
    whole = pl.BlockSpec(memory_space=pltpu.VMEM)
    half = jnp.bfloat16
    dma = pltpu.SemaphoreType.DMA
    return pl.pallas_call(
        reduce_kernel,
        out_shape=jax.ShapeDtypeStruct((UNITS * UNIT, WIDE), half),
        in_specs=[whole] * 2,
        out_specs=pl.BlockSpec(memory_space=pl.ANY),
        scratch_shapes=[
            pltpu.VMEM((UNITS * UNIT, WIDE), half),
            pltpu.VMEM((4, 2, 2, BIG, WIDE), half),
            pltpu.VMEM((4, 2, 4, BIG, WIDE), half),
            pltpu.VMEM((4, 4, BIG, WIDE), half),
            pltpu.VMEM((2, BIG, WIDE), half),
            pltpu.VMEM((SHARE, WIDE), half),
            dma((4, 2, 2)), dma((4, 2, 2)), dma((4, 2, 4)), dma((4, 2, 4)), dma((4, 2)), dma((4, 2)),
            dma((4, 2, 2)), dma((4, 2, 2)), dma((2,)), dma((2,)), dma((4, 2, 2)), dma((4, 2, 2)),
            dma((4, 2, 8)), dma((4, 2, 8)), dma((5,)), dma((5,)), dma((4,)),
        ],
        compiler_params=pltpu.CompilerParams(
            vmem_limit_bytes=60 << 20, collective_id=1, has_side_effects=True
        ),
        name="reduce",
    )(left, dz)


def finish_kernel(
    hp_one, source, u_two, hp_two, drop_one, drop_two, o_in_one, o_rec_one, o_bias_one, o_in_two, o_rec_two, o_bias_two
):
    step = pl.program_id(0)

    def wide(ref):
        return ref[:, :HID].astype(jnp.float32)

    o_rec_one[...] = wide(hp_one) * drop_one[...].astype(jnp.float32) * weight_scale
    o_rec_two[...] = wide(hp_two) * drop_two[...].astype(jnp.float32) * weight_scale
    o_in_one[...] = wide(source)
    o_in_two[...] = wide(u_two)

    @pl.when(step == D_IN // SLAB)
    def _():
        o_bias_one[...] = wide(source)[D_IN % SLAB]

    @pl.when(step == HID // SLAB)
    def _():
        o_bias_two[...] = wide(u_two)[HID % SLAB]


def finish(total, drop_one, drop_two):
    def units(first, last):
        return pl.BlockSpec((SLAB, WIDE), lambda i: (first + jnp.minimum(i, last), 0))

    def rows(last):
        return pl.BlockSpec((SLAB, HID), lambda i: (jnp.minimum(i, last), 0))

    one = pl.BlockSpec((HID,), lambda i: (0,))
    count, short = WIDE // SLAB - 1, D_IN // SLAB
    square, line = jax.ShapeDtypeStruct((HID, HID), jnp.float32), jax.ShapeDtypeStruct((HID,), jnp.float32)
    return pl.pallas_call(
        finish_kernel,
        grid=(count + 1,),
        in_specs=[
            units(HP_ONE // SLAB, count), units(SOURCE // SLAB, short), units(U_TWO // SLAB, count),
            units(HP_TWO // SLAB, count), rows(count), rows(count),
        ],
        out_specs=[rows(short), rows(count), one, rows(count), rows(count), one],
        out_shape=[jax.ShapeDtypeStruct((D_IN, HID), jnp.float32), square, line, square, square, line],
        compiler_params=pltpu.CompilerParams(vmem_limit_bytes=60 << 20),
        name="finish",
    )(total, total, total, total, drop_one, drop_two)


def local(
    inputs, resets, in_mask, mid_mask, out_mask,
    w_ih_one, w_hh_one, bias_one, drop_one, w_ih_two, w_hh_two, bias_two, drop_two, cotangent,
):
    pipe = lax.axis_index("pipe")
    w_one = jnp.concatenate([w_ih_one, bias_one[None]], 0)
    w_one = jnp.pad(w_one, ((0, D_WIDE - D_IN - 1), (0, WIDE - HID)))
    last = WIDE - UNIT
    tails = jnp.stack([
        jnp.pad(w_hh_one[last:] * drop_one[last:].astype(jnp.bfloat16) * weight_scale, ((0, 2), (0, 2))),
        jnp.pad(w_hh_two[last:] * drop_two[last:].astype(jnp.bfloat16) * weight_scale, ((0, 2), (0, 2))),
        jnp.pad(jnp.concatenate([w_ih_two[last:], bias_two[None]], 0), ((0, 1), (0, 2))),
    ])
    left, out_two, dz, dx, _, _ = relay(
        w_one, tails, w_hh_one, drop_one, w_hh_two, drop_two, w_ih_two,
        inputs, in_mask, mid_mask, out_mask, cotangent, resets,
    )
    left = left.reshape(STEPS * ROWS, UNITS * UNIT)
    total = reduce_over_dp(left, dz.reshape(2, STEPS * ROWS, WIDE))

    u_two = left[:, U_TWO : U_TWO + WIDE].reshape(out_two.shape)
    layer = jnp.where(pipe < 2, u_two, out_two).reshape(STEPS, 2, 2, WIDE)[..., :HID]
    layer = lax.dynamic_index_in_dim(layer, pipe % 2, 1, keepdims=False)
    layer_outputs = jnp.swapaxes(layer, 0, 1)[None]
    grad_input = jnp.transpose(dx.reshape(STEPS, 2, 2, 128)[..., :100], (1, 2, 0, 3))
    keep_in = in_mask.astype(jnp.float32) * keep_scale
    keep_part = lax.dynamic_slice_in_dim(keep_in, pipe * 100, 100, 2)
    grad_input = grad_input * keep_part[:, :, None, :]

    in_one, rec_one, bias_one, in_two, rec_two, bias_two = finish(total, drop_one, drop_two)
    return (layer_outputs, grad_input, in_one, rec_one, bias_one, in_two, rec_two, bias_two)


def solution(mesh):
    placed = (
        P(None, "dp", None, None),
        P(None, "dp"),
        P(None, "dp", None),
        P(None, "dp", None),
        P(None, "dp", None),
        P(None, "pipe"),
        P(None, "pipe"),
        P("pipe"),
        P(None, "pipe"),
        P(None, "pipe"),
        P(None, "pipe"),
        P("pipe"),
        P(None, "pipe"),
        P(None, "dp", None, None),
    )
    return jax.shard_map(
        local,
        mesh=mesh,
        in_specs=placed,
        out_specs=(
            P("pipe", "dp", None, None),
            P(None, "dp", None, "pipe"),
            P(None, "pipe"),
            P(None, "pipe"),
            P("pipe"),
            P(None, "pipe"),
            P(None, "pipe"),
            P("pipe"),
        ),
        check_vma=False,
    )
```

```python
import functools

import jax
import jax.numpy as jnp
from jax import lax
from jax.experimental import pallas as pl
from jax.experimental.pallas import tpu as pltpu
from jax.sharding import PartitionSpec as P

MESH = pl.DeviceIdType.MESH
HID = 1150
WIDE = 1152
D_IN = 400
D_WIDE = 416
STEPS = 88
ROWS = 4
CHUNKS = 44
GROUP = 4
LATER = 3
TURNS = 36
UNIT = 128
HALF_UNIT = 64
UNITS = 32
HP_ONE, U_TWO, HP_TWO, SOURCE = 0, 1152, 2304, 3456
SOURCE_WIDE = 640
SLAB = 384
DEEP = 4
BIG, SMALL = 96, 16
THIRD = 32 * BIG
SHARE = 32 * SMALL

keep_scale = 4.0 / 3.0
weight_scale = 2.0

LAYER_ONE, SOURCE_GRAD, LAYER_TWO, BETWEEN = 0, 1, 2, 3
W_ONE, R_ONE, R_TWO, W_TWO, R_ONE_T, R_TWO_T, W_TWO_T, W_ONE_T = range(8)
USER = {
    W_ONE: LAYER_ONE,
    R_ONE: LAYER_ONE,
    R_TWO: LAYER_TWO,
    W_TWO: BETWEEN,
    R_ONE_T: LAYER_ONE,
    R_TWO_T: LAYER_TWO,
    W_TWO_T: BETWEEN,
    W_ONE_T: SOURCE_GRAD,
}
FORWARD = (W_ONE,)
BACKWARD = (R_TWO_T, W_TWO_T, R_ONE_T, W_ONE_T)


def sigmoid(value):
    return 0.5 * jnp.tanh(0.5 * value) + 0.5


def dot(left, right):
    return jnp.dot(left, right, preferred_element_type=jnp.float32)


def relay_kernel(
    plain_in, tails, r_one, drop_one, r_two, drop_two, w_two,
    inputs, in_mask, mid_mask, out_mask, cotangent, resets,
    o_left, o_out, o_dz, o_dx, turned, turned_in,
    raw_weights, raw_drop, raw_sem, plain, turn, small, apart, turn_sem,
    w_front, w_back, zx, extra, dz, du, dx, above, line, spread, keep, layer_keep, hidden, cell, stage_a, stage_b, stage_z,
    block_send, block_recv, block_local, cross_send, cross_recv, ring_send, ring_recv, go_on,
    u_send, u_recv, z_send, z_recv, dz_send, dz_recv, du_send, du_recv,
    bulk_send, bulk_recv, part_send, part_recv, dx_send, dx_recv, local_sem,
):
    o_hp_one, o_u, o_hp_two = (o_left.at[:, :, pl.ds(start, WIDE)] for start in (HP_ONE, U_TWO, HP_TWO))
    o_dz_one, o_dz_two = o_dz.at[0], o_dz.at[1]
    pipe = lax.axis_index("pipe")
    dp = lax.axis_index("dp")
    dp_count = lax.axis_size("dp")
    dp_far = lax.rem(dp + dp_count // 2, dp_count)

    barrier = pltpu.get_barrier_semaphore()
    for step in range(1, 4):
        pl.semaphore_signal(
            barrier, inc=1, device_id={"pipe": lax.rem(pipe + step, 4), "dp": dp}, device_id_type=MESH
        )
    for step in range(4):
        pl.semaphore_signal(
            barrier, inc=1, device_id={"pipe": lax.rem(pipe + step, 4), "dp": dp_far}, device_id_type=MESH
        )
    z, x, y = dp // 16, lax.rem(dp // 4, 4), lax.rem(dp, 4)
    rings = (
        lambda d: {"pipe": pipe, "dp": z * 16 + lax.rem(x + d + 4, 4) * 4 + y},
        lambda d: {"pipe": pipe, "dp": z * 16 + x * 4 + lax.rem(y + d + 4, 4)},
    )
    for ring in rings:
        for d in (1, -1):
            pl.semaphore_signal(barrier, inc=1, device_id=ring(d), device_id_type=MESH)

    def make_plain(m, also=None):
        weights, drop = ((r_one, drop_one), (r_two, drop_two), (w_two, None))[m]
        plain[m, :, pl.ds(HID // UNIT * UNIT, UNIT)] = jnp.zeros((WIDE, UNIT), jnp.bfloat16)

        def copies(i):
            slot = lax.rem(i, DEEP)
            span = pl.ds(pl.multiple_of(i * UNIT, UNIT), UNIT)
            return [
                pltpu.make_async_copy(array.at[span], raw.at[slot], raw_sem.at[k, slot])
                for k, (array, raw) in enumerate(((weights, raw_weights), (drop, raw_drop)))
                if array is not None
            ]

        def start(i):
            for copy in copies(i):
                copy.start()

        whole = HID // UNIT

        def body(i, carry):
            for copy in copies(i):
                copy.wait()
            slot = lax.rem(i, DEEP)
            value = raw_weights[slot]
            if drop is not None:
                value = value.astype(jnp.float32) * raw_drop[slot].astype(jnp.float32) * weight_scale
            plain[m, pl.ds(pl.multiple_of(i * UNIT, UNIT), UNIT), pl.ds(0, HID)] = value.astype(jnp.bfloat16)
            pl.when(i + DEEP < whole)(lambda: start(i + DEEP))
            if also is not None:
                also(i)
            return carry

        for i in range(DEEP):
            start(i)
        plain[m, pl.ds(whole * UNIT, UNIT)] = tails[m]
        lax.fori_loop(0, whole, body, 0)
        if also is not None:
            also(whole)

    def turn_copy(m, i, slot):
        rows = pl.ds(pl.multiple_of(i * UNIT, UNIT), UNIT)
        return pltpu.make_async_copy(turn.at[slot], turned.at[m, rows], turn_sem.at[slot])

    def make_turned(m, order, i):
        slot = lax.rem(order * (WIDE // UNIT) + i, 2)
        if order:
            turn_copy(m, i, slot).wait()
        else:
            pl.when(i >= 2)(lambda: turn_copy(m, i, slot).wait())
        value = plain[m, :, pl.ds(pl.multiple_of(i * UNIT, UNIT), UNIT)].astype(jnp.float32).T
        column = lax.broadcasted_iota(jnp.int32, (UNIT, WIDE), 1)
        turn[slot] = jnp.where(column < HID, value, 0.0).astype(jnp.bfloat16)
        turn_copy(m, i, slot).start()

    def turn_in_copy(i):
        slot = lax.rem(i, 2)
        rows = pl.ds(pl.multiple_of(i * UNIT, UNIT), UNIT)
        return pltpu.make_async_copy(turn.at[slot, :, pl.ds(0, 512)], turned_in.at[rows], turn_sem.at[slot])

    def make_turned_in(i, carry):
        small[...] = plain_in[:D_IN, pl.ds(pl.multiple_of(i * UNIT, UNIT), UNIT)].astype(jnp.float32)
        for q in range(4):
            apart[q * UNIT : q * UNIT + 100, :] = small[q * 100 : q * 100 + 100, :]
        pl.when(i >= 2)(lambda: turn_in_copy(i).wait())
        turn[lax.rem(i, 2), :, pl.ds(0, 512)] = apart[...].T.astype(jnp.bfloat16)
        turn_in_copy(i).start()
        return carry

    def finish_turned(m, order):
        def body(i, carry):
            make_turned(m, order, i)
            return carry

        lax.fori_loop(0, WIDE // UNIT, body, 0)
        for slot in range(2):
            turn_copy(m, 0, slot).wait()
        apart[...] = jnp.zeros_like(apart)
        lax.fori_loop(0, WIDE // UNIT, make_turned_in, 0)
        for i in range(2):
            turn_in_copy(i).wait()

    @pl.when(pipe >= 2)
    def _():
        make_plain(0)

    @pl.when(pipe < 2)
    def _():
        make_plain(2)

    pl.semaphore_wait(barrier, 11)

    blocks = {
        W_ONE: plain_in, R_ONE: plain.at[0], R_TWO: plain.at[1], W_TWO: plain.at[2],
        R_ONE_T: turned.at[0], R_TWO_T: turned.at[1], W_TWO_T: turned.at[2], W_ONE_T: turned_in,
    }

    def landing(kind, p):
        if kind == W_ONE:
            return w_back.at[p, pl.ds(0, D_WIDE)]
        if kind in (R_ONE, R_TWO, W_TWO):
            return w_front.at[p]
        if kind == W_ONE_T:
            return w_front.at[p, :, pl.ds(0, 512)]
        return w_back.at[p]

    def block_copies(kind, p, turn=None):
        user = USER[kind]
        source_ref, target = blocks[kind], landing(kind, p)
        if p == user:
            return [pltpu.make_async_copy(source_ref, target, block_local.at[kind])]
        if p // 2 == user // 2:
            return [
                pltpu.make_async_remote_copy(
                    source_ref, target, block_send.at[kind, 0], block_recv.at[kind, p, 0],
                    device_id={"pipe": user, "dp": dp}, device_id_type=MESH,
                )
            ]
        rows = source_ref.shape[0] // 2
        if turn is None:
            spans = [pl.ds(part * rows, rows) for part in range(2)]
        else:
            piece = rows // TURNS
            spans = [pl.ds(pl.multiple_of(part * rows + turn * piece, piece), piece) for part in range(2)]
        return [
            pltpu.make_async_remote_copy(
                source_ref.at[spans[part]], target.at[spans[part]],
                block_send.at[kind, part], block_recv.at[kind, p, part],
                device_id={"pipe": user, "dp": (dp, dp_far)[part]}, device_id_type=MESH,
            )
            for part in range(2)
        ]

    def rows_at(first, count=UNIT):
        return pl.ds(pl.multiple_of(first, 64), count)

    def part_rows(ring, step):
        place = (x, y)[ring]
        return UNIT * (1 + 4 * ring + lax.rem(place + step + 4, 4))

    def from_other_plane(kind):
        return [p for p in range(4) if p // 2 != USER[kind] // 2]

    def cross_copy(kind, p, k, slot):
        rows = rows_at((part_rows(0, 0), part_rows(1, 0), 0)[k])
        return pltpu.make_async_remote_copy(
            blocks[kind].at[rows], w_front.at[p, rows], cross_send.at[slot, k], cross_recv.at[p % 2, k],
            device_id={"pipe": USER[kind], "dp": (dp, dp_far)[p % 2]}, device_id_type=MESH,
        )

    def ring_copy(p, ring, d, on):
        k = 2 * on + (0 if d == 1 else 1)
        if on:
            rows = rows_at(part_rows(ring, -d) + (0 if d == 1 else HALF_UNIT), HALF_UNIT)
        else:
            rows = rows_at(part_rows(ring, 0))
        ref = w_front.at[p, rows]
        return pltpu.make_async_remote_copy(
            ref, ref, ring_send.at[p % 2, ring, k], ring_recv.at[p % 2, ring, k],
            device_id=rings[ring](d), device_id_type=MESH,
        )

    def ring_arrival(p, ring, d, on):
        k = 2 * on + (0 if d == 1 else 1)
        if on:
            rows = rows_at(part_rows(ring, 2) + (0 if d == 1 else HALF_UNIT), HALF_UNIT)
        else:
            rows = rows_at(part_rows(ring, -d))
        ref = w_front.at[p, rows]
        return pltpu.make_async_remote_copy(
            ref, ref, ring_send.at[p % 2, ring, k], ring_recv.at[p % 2, ring, k],
            device_id=rings[ring](d), device_id_type=MESH,
        )

    SPREAD = (W_TWO, R_TWO, R_ONE)

    def start_cross(me, kind, ks):
        slot = (R_TWO, W_TWO, R_ONE).index(kind) % 2
        for k in ks:
            cross_copy(kind, me, k, slot).start()

    def start_spread(me):
        if me // 2 == 1:
            start_cross(me, R_ONE, (0, 1))
            start_blocks(FORWARD, me)
            start_cross(me, R_ONE, (2,))
            make_plain(2, functools.partial(make_turned, 0, 0))
            block_copies(W_TWO, me)[0].start()
            make_plain(1, functools.partial(make_turned, 2, 1))
            block_copies(R_TWO, me)[0].start()
            finish_turned(1, 2)
        else:
            start_cross(me, W_TWO, (0, 1))
            start_blocks(FORWARD, me)
            make_plain(1, functools.partial(make_turned, 2, 0))
            start_cross(me, R_TWO, (0, 1))
            start_cross(me, W_TWO, (2,))
            start_cross(me, R_TWO, (2,))
            make_plain(0, functools.partial(make_turned, 1, 1))
            block_copies(R_ONE, me)[0].start()
            finish_turned(0, 2)

    def finish_spread(me):
        kinds = [kind for kind in SPREAD if me // 2 != USER[kind] // 2]
        for kind in kinds:
            slot = (R_TWO, W_TWO, R_ONE).index(kind) % 2
            for k in range(3):
                cross_copy(kind, me, k, slot).wait_send()
        for kind in SPREAD:
            if me // 2 == USER[kind] // 2 and me != USER[kind]:
                block_copies(kind, me)[0].wait_send()

    def share_blocks(kind):
        others = from_other_plane(kind)
        for ring in range(2):
            for p in others:
                cross_copy(kind, p, ring, 0).wait_recv()
                for d in (1, -1):
                    ring_copy(p, ring, d, 0).start()
        for d in (1, -1):
            for p in others:
                for ring in range(2):
                    ring_arrival(p, ring, d, 0).wait_recv()
                    ring_copy(p, ring, d, 1).start()

    def receive_rest(kind):
        me = USER[kind]
        others = from_other_plane(kind)
        for p in others:
            cross_copy(kind, p, 2, 0).wait_recv()
            for ring in range(2):
                for d in (1, -1):
                    ring_arrival(p, ring, d, 1).wait_recv()
        for p in (me, me ^ 1):
            copy = block_copies(kind, p)[0]
            if p == me:
                copy.wait()
            else:
                copy.wait_recv()

    def finish_rings(kind):
        for p in from_other_plane(kind):
            for ring in range(2):
                for d in (1, -1):
                    for on in range(2):
                        ring_copy(p, ring, d, on).wait_send()

    def start_blocks(kinds, p):
        for kind in kinds:
            for copy in block_copies(kind, p):
                copy.start()

    def start_near(p):
        for kind in BACKWARD:
            if p // 2 == USER[kind] // 2:
                for copy in block_copies(kind, p):
                    copy.start()

    def start_turn(p, turn):
        for kind in BACKWARD:
            if p // 2 != USER[kind] // 2:
                for copy in block_copies(kind, p, turn):
                    copy.start()

    def finish_blocks(kinds, p):
        for kind in kinds:
            if p != USER[kind]:
                for copy in block_copies(kind, p):
                    copy.wait_send()

    def await_blocks(kind):
        for p in range(4):
            for copy in block_copies(kind, p):
                if p == USER[kind]:
                    copy.wait()
                else:
                    copy.wait_recv()

    def to(pipe_to, source_ref, target, send, recv):
        return pltpu.make_async_remote_copy(
            source_ref, target, send, recv,
            device_id={"pipe": pipe_to, "dp": dp}, device_id_type=MESH,
        )

    def copy_u(c):
        return to(BETWEEN, o_u.at[c], o_u.at[c], u_send, u_recv.at[c])

    def copy_z(c):
        return to(LAYER_TWO, zx.at[c], zx.at[c], z_send, z_recv.at[c])

    def copy_dz(pipe_to, c):
        return to(pipe_to, dz.at[:, c], dz.at[:, c], dz_send, dz_recv.at[c])

    def copy_du(c):
        return to(LAYER_ONE, du.at[c], du.at[c], du_send, du_recv.at[c])

    def copy_part(pipe_to, output, group, slot, gate):
        span = pl.ds(group * GROUP, GROUP)
        return to(pipe_to, dz.at[gate, span], output.at[span], part_send.at[slot], part_recv.at[group])

    def copy_dx(pipe_to, group, slot):
        count = GROUP * 2 * ROWS
        span = pl.ds(pl.multiple_of(group * count, count), count)
        return to(
            pipe_to, dx.at[span, pl.ds(pipe_to * 128, 128)], o_dx.at[span], dx_send.at[slot], dx_recv.at[group]
        )

    def copy_bulk(pipe_to, ref, slot, which):
        return to(pipe_to, ref, ref, bulk_send.at[slot], bulk_recv.at[which])

    def keep_rows(c, j):
        return jnp.broadcast_to(keep[c, ROWS * j : ROWS * j + ROWS, 0:1], (ROWS, WIDE))

    def by_time(target, width, whole, value_of):
        for start in range(0, whole, 128):
            count = min(128, width - start)
            if count < 128:
                line[...] = jnp.zeros_like(line)
            for i in range(ROWS):
                value = value_of(i, slice(start, start + count))
                if count < 128:
                    line[:, :count] = value
                    value = line[...]
                spread[pl.ds(i, STEPS, stride=ROWS), :] = value
            target[:, start : start + 128] = spread[...]

    def set_up():
        shape = (CHUNKS, 2 * ROWS, 128)
        row = lax.broadcasted_iota(jnp.int32, shape, 1)
        time = 2 * lax.broadcasted_iota(jnp.int32, shape, 0) + row // ROWS
        stream = lax.rem(row, ROWS)
        reset = jnp.zeros(shape, jnp.int32)
        for i in range(ROWS):
            reset = jnp.where(stream == i, resets[i // 2, i % 2], reset)
        keep[...] = jnp.where(time == reset, 0.0, 1.0)
        layer_keep[...] = jnp.zeros_like(layer_keep)
        for i in range(ROWS):
            h, s = i // 2, i % 2
            for m, mask in enumerate((mid_mask, out_mask)):
                layer_keep[m, i : i + 1, :HID] = mask[h, s : s + 1, :].astype(jnp.float32) * keep_scale

        def masked(i, lanes):
            h, s = i // 2, i % 2
            kept = in_mask[h, s : s + 1, lanes].astype(jnp.float32) * keep_scale
            return (inputs[h, s, :, lanes] * kept).astype(jnp.bfloat16).astype(jnp.float32)

        by_time(dx, D_IN, 512, masked)
        column = lax.broadcasted_iota(jnp.int32, (STEPS * ROWS, 512), 1)
        value = jnp.where(column == D_IN, 1.0, dx[...])
        dx[...] = value
        o_left[:, :, pl.ds(SOURCE, 512)] = value.astype(jnp.bfloat16).reshape(CHUNKS, 2 * ROWS, 512)
        o_left[:, :, pl.ds(SOURCE + 512, 128)] = jnp.zeros((CHUNKS, 2 * ROWS, 128), jnp.bfloat16)

    def set_up_above():
        def masked(i, lanes):
            return cotangent[i // 2, i % 2, :, lanes].astype(jnp.float32) * layer_keep[1, i : i + 1, lanes]

        by_time(above, HID, WIDE, masked)

    def clear():
        hidden[...] = jnp.zeros_like(hidden)
        cell[...] = jnp.zeros_like(cell)

    def forward_pair(c, mask, with_one, o_hp, o_layer):
        column = lax.broadcasted_iota(jnp.int32, (ROWS, WIDE), 1)
        for j in range(2):
            rows = pl.ds(ROWS * j, ROWS)
            kept = keep_rows(c, j)
            hidden_prev = hidden[...] * kept
            cell_prev = cell[...] * kept
            left = hidden_prev.astype(jnp.bfloat16)
            gates = [
                dot(left, w_front[g]) + zx[c, rows, pl.ds(g * WIDE, WIDE)] for g in range(4)
            ]
            gate_in, gate_forget = sigmoid(gates[0]), sigmoid(gates[1])
            gate_cand, gate_out = jnp.tanh(gates[2]), sigmoid(gates[3])
            cell_now = gate_forget * cell_prev + gate_in * gate_cand
            cell_tanh = jnp.tanh(cell_now)
            hidden_now = (gate_out * cell_tanh).astype(jnp.bfloat16).astype(jnp.float32)
            cell[...] = cell_now
            hidden[...] = hidden_now
            stage_a[rows, :] = hidden_prev
            layer = hidden_now * mask
            if with_one:
                layer = jnp.where(column == HID, 1.0, layer)
            stage_b[rows, :] = layer
            zx[c, rows, pl.ds(0, WIDE)] = gate_cand * gate_in * (1.0 - gate_in)
            zx[c, rows, pl.ds(WIDE, WIDE)] = cell_prev * gate_forget * (1.0 - gate_forget)
            zx[c, rows, pl.ds(2 * WIDE, WIDE)] = gate_in * (1.0 - gate_cand * gate_cand)
            zx[c, rows, pl.ds(3 * WIDE, WIDE)] = cell_tanh * gate_out * (1.0 - gate_out)
            extra[c, rows, pl.ds(0, WIDE)] = gate_out * (1.0 - cell_tanh * cell_tanh)
            extra[c, rows, pl.ds(WIDE, WIDE)] = gate_forget * kept
        o_hp[c] = stage_a[...].astype(jnp.bfloat16)
        o_layer[c] = stage_b[...].astype(jnp.bfloat16)

    def backward_pair(c, upstream):
        for j in (1, 0):
            rows = pl.ds(ROWS * j, ROWS)
            total = hidden[...] + upstream[ROWS * j : ROWS * j + ROWS]
            out_grad = total * zx[c, rows, pl.ds(3 * WIDE, WIDE)]
            cell_total = cell[...] + total * extra[c, rows, pl.ds(0, WIDE)]
            cell[...] = cell_total * extra[c, rows, pl.ds(WIDE, WIDE)]
            grads = [cell_total * zx[c, rows, pl.ds(g * WIDE, WIDE)] for g in range(3)] + [out_grad]
            back = None
            for g in range(4):
                stage_z[rows, pl.ds(g * WIDE, WIDE)] = grads[g]
                part = dot(grads[g].astype(jnp.bfloat16), w_back[g])
                back = part if back is None else back + part
            hidden[...] = back * keep_rows(c, j)
        for g in range(4):
            dz[g, c] = stage_z[:, pl.ds(g * WIDE, WIDE)].astype(jnp.bfloat16)

    last = CHUNKS - 1
    groups = CHUNKS // GROUP

    @pl.when(pipe == LAYER_ONE)
    def _():
        me = LAYER_ONE
        start_spread(me)
        set_up()
        share_blocks(R_ONE)
        await_blocks(W_ONE)
        source = dx[:, :D_WIDE].astype(jnp.bfloat16)
        for g in range(4):
            zx[:, :, pl.ds(g * WIDE, WIDE)] = dot(source, w_back[g, :D_WIDE]).reshape(CHUNKS, 2 * ROWS, WIDE)
        receive_rest(R_ONE)
        clear()

        def ahead(c, carry):
            forward_pair(c, layer_keep[0], True, o_hp_one, o_u)
            copy_u(c).start()

            @pl.when((c >= LATER) & (c < LATER + TURNS))
            def _():
                pl.semaphore_signal(
                    go_on, inc=1, device_id={"pipe": SOURCE_GRAD, "dp": dp}, device_id_type=MESH
                )
                start_turn(me, c - LATER)

            @pl.when(c == LATER)
            def _():
                start_near(me)

            return carry

        lax.fori_loop(0, CHUNKS, ahead, 0)
        bulk = [
            copy_bulk(SOURCE_GRAD, o_u, 0, 0), copy_bulk(LAYER_TWO, o_u, 1, 0),
            copy_bulk(SOURCE_GRAD, o_hp_one, 2, 1), copy_bulk(LAYER_TWO, o_hp_one, 3, 1),
            copy_bulk(BETWEEN, o_hp_one, 4, 1),
        ]
        for copy in bulk:
            copy.start()
        await_blocks(R_ONE_T)
        clear()

        def behind(i, carry):
            c = last - i
            copy_du(c).wait_recv()
            mask = jnp.concatenate([layer_keep[0]] * 2, 0)
            backward_pair(c, du[c].astype(jnp.float32) * mask)
            copy_dz(SOURCE_GRAD, c).start()

            @pl.when(lax.rem(c, GROUP) == 0)
            def _():
                group = c // GROUP
                copy_part(LAYER_TWO, o_dz_one, group, 0, LAYER_TWO).start()
                copy_part(BETWEEN, o_dz_one, group, 1, BETWEEN).start()

            return carry

        lax.fori_loop(0, CHUNKS, behind, 0)
        own = pltpu.make_async_copy(dz.at[me], o_dz_one, local_sem.at[0])
        own.start()
        finish_rings(R_ONE)
        finish_spread(me)
        finish_blocks(FORWARD + BACKWARD, me)
        to(BETWEEN, o_u, o_u, u_send, u_recv.at[0]).wait_send()
        for copy in bulk:
            copy.wait_send()
        to(SOURCE_GRAD, dz, dz, dz_send, dz_recv.at[0]).wait_send()
        to(LAYER_TWO, dz.at[me], o_dz_one, part_send.at[0], part_recv.at[0]).wait_send()
        to(BETWEEN, dz.at[me], o_dz_one, part_send.at[1], part_recv.at[0]).wait_send()
        own.wait()

        copy_bulk(me, o_hp_two, 0, 2).wait_recv()
        for group in range(groups):
            copy_part(me, o_dz_two, group, 0, me).wait_recv()
            copy_dx(me, group, 0).wait_recv()

    @pl.when(pipe == LAYER_TWO)
    def _():
        me = LAYER_TWO
        start_spread(me)
        set_up()
        set_up_above()
        share_blocks(R_TWO)
        receive_rest(R_TWO)
        clear()

        def ahead(c, carry):
            copy_z(c).wait_recv()

            @pl.when((c >= LATER) & (c < LATER + TURNS))
            def _():
                start_turn(me, c - LATER)

            @pl.when(c == LATER)
            def _():
                start_near(me)

            forward_pair(c, layer_keep[1], False, o_hp_two, o_out)
            return carry

        lax.fori_loop(0, CHUNKS, ahead, 0)
        bulk = [
            copy_bulk(LAYER_ONE, o_hp_two, 0, 2), copy_bulk(SOURCE_GRAD, o_hp_two, 1, 2),
            copy_bulk(BETWEEN, o_hp_two, 2, 2), copy_bulk(BETWEEN, o_out, 3, 3),
        ]
        for copy in bulk:
            copy.start()
        await_blocks(R_TWO_T)
        clear()

        def behind(i, carry):
            c = last - i
            backward_pair(c, above[pl.ds(pl.multiple_of(c * 2 * ROWS, 2 * ROWS), 2 * ROWS), :])
            copy_dz(BETWEEN, c).start()

            @pl.when(lax.rem(c, GROUP) == 0)
            def _():
                group = c // GROUP
                copy_part(LAYER_ONE, o_dz_two, group, 0, LAYER_ONE).start()
                copy_part(SOURCE_GRAD, o_dz_two, group, 1, SOURCE_GRAD).start()

            return carry

        lax.fori_loop(0, CHUNKS, behind, 0)
        own = pltpu.make_async_copy(dz.at[me], o_dz_two, local_sem.at[0])
        own.start()
        finish_rings(R_TWO)
        finish_spread(me)
        finish_blocks(FORWARD + BACKWARD, me)
        for copy in bulk:
            copy.wait_send()
        to(BETWEEN, dz, dz, dz_send, dz_recv.at[0]).wait_send()
        to(LAYER_ONE, dz.at[me], o_dz_two, part_send.at[0], part_recv.at[0]).wait_send()
        to(SOURCE_GRAD, dz.at[me], o_dz_two, part_send.at[1], part_recv.at[0]).wait_send()
        own.wait()

        copy_bulk(me, o_u, 0, 0).wait_recv()
        copy_bulk(me, o_hp_one, 0, 1).wait_recv()
        for group in range(groups):
            copy_part(me, o_dz_one, group, 0, me).wait_recv()
            copy_dx(me, group, 0).wait_recv()

    @pl.when(pipe == BETWEEN)
    def _():
        me = BETWEEN
        start_spread(me)
        set_up()
        share_blocks(W_TWO)
        receive_rest(W_TWO)

        def ahead(c, carry):
            copy_u(c).wait_recv()
            for g in range(4):
                zx[c, :, pl.ds(g * WIDE, WIDE)] = dot(o_u[c], w_front[g])
            copy_z(c).start()

            @pl.when((c >= LATER) & (c < LATER + TURNS))
            def _():
                start_turn(me, c - LATER)

            @pl.when(c == LATER)
            def _():
                start_near(me)

            return carry

        lax.fori_loop(0, CHUNKS, ahead, 0)
        await_blocks(W_TWO_T)

        def behind(i, carry):
            c = last - i
            copy_dz(me, c).wait_recv()
            back = None
            for g in range(4):
                part = dot(dz[g, c], w_back[g])
                back = part if back is None else back + part
            du[c] = back.astype(jnp.bfloat16)
            copy_du(c).start()
            return carry

        lax.fori_loop(0, CHUNKS, behind, 0)
        own = pltpu.make_async_copy(dz.at[me], o_dz_two, local_sem.at[0])
        own.start()
        finish_rings(W_TWO)
        finish_spread(me)
        finish_blocks(FORWARD + BACKWARD, me)
        to(LAYER_TWO, zx, zx, z_send, z_recv.at[0]).wait_send()
        to(LAYER_ONE, du, du, du_send, du_recv.at[0]).wait_send()
        own.wait()

        copy_bulk(me, o_hp_one, 0, 1).wait_recv()
        copy_bulk(me, o_hp_two, 0, 2).wait_recv()
        copy_bulk(me, o_out, 0, 3).wait_recv()
        for group in range(groups):
            copy_part(me, o_dz_one, group, 0, me).wait_recv()
            copy_dx(me, group, 0).wait_recv()

    @pl.when(pipe == SOURCE_GRAD)
    def _():
        me = SOURCE_GRAD
        start_spread(me)
        set_up()

        def pass_on(turn, carry):
            pl.semaphore_wait(go_on, 1)
            start_turn(me, turn)
            return carry

        lax.fori_loop(0, TURNS, pass_on, 0)
        start_near(me)
        await_blocks(W_ONE_T)

        def behind(i, carry):
            c = last - i
            copy_dz(me, c).wait_recv()
            back = None
            for g in range(4):
                part = dot(dz[g, c], w_front[g, :, :512])
                back = part if back is None else back + part
            dx[pl.ds(pl.multiple_of(c * 2 * ROWS, 2 * ROWS), 2 * ROWS), :] = back

            @pl.when(lax.rem(c, GROUP) == 0)
            def _():
                group = c // GROUP
                copy_dx(LAYER_ONE, group, 0).start()
                copy_dx(LAYER_TWO, group, 1).start()
                copy_dx(BETWEEN, group, 2).start()

            return carry

        lax.fori_loop(0, CHUNKS, behind, 0)
        own = pltpu.make_async_copy(dz.at[me], o_dz_one, local_sem.at[0])
        own.start()
        own_dx = pltpu.make_async_copy(dx.at[:, pl.ds(me * 128, 128)], o_dx, local_sem.at[1])
        own_dx.start()
        finish_spread(me)
        finish_blocks(FORWARD + BACKWARD, me)
        for slot, pipe_to in enumerate((LAYER_ONE, LAYER_TWO, BETWEEN)):
            to(pipe_to, o_dx, o_dx, dx_send.at[slot], dx_recv.at[0]).wait_send()
        own.wait()
        own_dx.wait()

        copy_bulk(me, o_u, 0, 0).wait_recv()
        copy_bulk(me, o_hp_one, 0, 1).wait_recv()
        copy_bulk(me, o_hp_two, 0, 2).wait_recv()
        for group in range(groups):
            copy_part(me, o_dz_two, group, 0, me).wait_recv()


def relay(w_one, tails, r_one, drop_one, r_two, drop_two, w_two, inputs, in_mask, mid_mask, out_mask, cotangent, resets):
    whole, away = pl.BlockSpec(memory_space=pltpu.VMEM), pl.BlockSpec(memory_space=pl.ANY)
    rows = (CHUNKS, 2 * ROWS, WIDE)
    half, full = jnp.bfloat16, jnp.float32
    shapes = [
        jax.ShapeDtypeStruct((CHUNKS, 2 * ROWS, UNITS * UNIT), half),
        jax.ShapeDtypeStruct(rows, half),
        jax.ShapeDtypeStruct((2,) + rows, half),
        jax.ShapeDtypeStruct((STEPS * ROWS, 128), full),
        jax.ShapeDtypeStruct((3, WIDE, WIDE), half),
        jax.ShapeDtypeStruct((WIDE, 512), half),
    ]
    dma = pltpu.SemaphoreType.DMA
    return pl.pallas_call(
        relay_kernel,
        out_shape=shapes,
        in_specs=[whole] * 2 + [away] * 5 + [whole] * 5
        + [pl.BlockSpec(memory_space=pltpu.SMEM)],
        out_specs=[whole] * 4 + [away] * 2,
        scratch_shapes=[
            pltpu.VMEM((DEEP, UNIT, HID), half),
            pltpu.VMEM((DEEP, UNIT, HID), jnp.int32),
            dma((2, DEEP)),
            pltpu.VMEM((3, WIDE, WIDE), half),
            pltpu.VMEM((2, UNIT, WIDE), half),
            pltpu.VMEM((D_IN, UNIT), full),
            pltpu.VMEM((512, UNIT), full),
            dma((2,)),
            pltpu.VMEM((4, WIDE, WIDE), half),
            pltpu.VMEM((4, WIDE, WIDE), half),
            pltpu.VMEM((CHUNKS, 2 * ROWS, 4 * WIDE), full),
            pltpu.VMEM((CHUNKS, 2 * ROWS, 2 * WIDE), full),
            pltpu.VMEM((4,) + rows, half),
            pltpu.VMEM(rows, half),
            pltpu.VMEM((STEPS * ROWS, 512), full),
            pltpu.VMEM((STEPS * ROWS, WIDE), full),
            pltpu.VMEM((STEPS, 128), full),
            pltpu.VMEM((STEPS * ROWS, 128), full),
            pltpu.VMEM((CHUNKS, 2 * ROWS, 128), full),
            pltpu.VMEM((2, ROWS, WIDE), full),
            pltpu.VMEM((ROWS, WIDE), full),
            pltpu.VMEM((ROWS, WIDE), full),
            pltpu.VMEM((2 * ROWS, WIDE), full),
            pltpu.VMEM((2 * ROWS, WIDE), full),
            pltpu.VMEM((2 * ROWS, 4 * WIDE), full),
            dma((8, 2)), dma((8, 4, 2)), dma((8,)),
            dma((2, 3)), dma((2, 3)), dma((2, 2, 4)), dma((2, 2, 4)), pltpu.SemaphoreType.REGULAR,
            dma, dma((CHUNKS,)), dma, dma((CHUNKS,)), dma, dma((CHUNKS,)), dma, dma((CHUNKS,)),
            dma((5,)), dma((4,)), dma((2,)), dma((CHUNKS // GROUP,)), dma((3,)), dma((CHUNKS // GROUP,)), dma((2,)),
        ],
        compiler_params=pltpu.CompilerParams(
            vmem_limit_bytes=60 << 20, collective_id=0, has_side_effects=True
        ),
        name="relay",
    )(w_one, tails, r_one, drop_one, r_two, drop_two, w_two, inputs, in_mask, mid_mask, out_mask, cotangent, resets)


def reduce_kernel(
    left, dz, total, own, near, far, part, cross, share,
    near_send, near_recv, far_send, far_recv, part_send, part_recv, last_send, last_recv,
    cross_send, cross_recv, back_send, back_recv, wide_send, wide_recv, share_send, share_recv, own_sem,
):
    pipe = lax.axis_index("pipe")
    dp = lax.axis_index("dp")
    z, x, y = dp // 16, lax.rem(dp // 4, 4), lax.rem(dp, 4)

    def device(z_, x_, y_):
        return {"pipe": pipe, "dp": z_ * 16 + lax.rem(x_ + 4, 4) * 4 + lax.rem(y_ + 4, 4)}

    along_x, along_y = (lambda d: device(z, x + d, y)), (lambda d: device(z, x, y + d))
    first, second = (along_x, along_y) * 2, (along_y, along_x) * 2
    place = ((x, y), (y, x)) * 2
    across = device(1 - z, x, y)
    size = (BIG, BIG, SMALL, SMALL)
    base = (0, 16 * BIG, THIRD + z * SHARE, THIRD + z * SHARE + 16 * SMALL)

    barrier = pltpu.get_barrier_semaphore()
    for target in (along_x(1), along_x(-1), along_y(1), along_y(-1), across):
        pl.semaphore_signal(barrier, inc=1, device_id=target, device_id_type=MESH)
    pl.semaphore_wait(barrier, 5)

    lanes_of = (pl.ds(0, WIDE), pl.ds(0, 640), pl.ds(640, 512))

    def unit(p, block, rel):
        a, b = place[p]
        index = lax.rem(a + block + 4, 4) * 4 + lax.rem(b + rel + 4, 4)
        return pl.ds(pl.multiple_of(base[p] + index * size[p], 16), size[p])

    def send(source, target, s, r, to):
        return pltpu.make_async_remote_copy(source, target, s, r, device_id=to, device_id_type=MESH)

    def add(rows, others, lanes=lanes_of[0]):
        def body(i, carry):
            span = pl.ds(pl.multiple_of(rows.start + i * 16, 16), 16)
            value = own[span, lanes].astype(jnp.float32)
            for ref in others:
                value = value + ref[pl.ds(pl.multiple_of(i * 16, 16), 16), lanes].astype(jnp.float32)
            own[span, lanes] = value.astype(jnp.bfloat16)
            return carry

        lax.fori_loop(0, rows.size // 16, body, 0)

    def product(u):
        columns = pl.ds(pl.multiple_of(u * UNIT, UNIT), UNIT)
        own[columns, :] = lax.dot_general(
            left[:, columns], dz[jnp.where((u >= U_TWO // UNIT) & (u < SOURCE // UNIT), 1, 0)], (((0,), (0,)), ((), ())),
            preferred_element_type=jnp.float32,
        ).astype(jnp.bfloat16)

    def products(start, count):
        def body(i, carry):
            product(start + i)
            return carry

        lax.fori_loop(0, count, body, 0)

    block_units = 4 * BIG // UNIT

    def block_products(p, block):
        products(p * 4 * block_units + lax.rem(place[p][0] + block + 4, 4) * block_units, block_units)

    side = {1: (2, 1), -1: (3, 0)}
    on_side = {1: (0, 1), -1: (3, 2)}
    slot = {1: 0, -1: 1}
    started = []

    def go(copy):
        copy.start()
        started.append(copy)

    def near_copy(p, d, k):
        at = (p, slot[d], k)
        return send(own.at[unit(p, 2, side[d][k])], near.at[at].at[pl.ds(0, size[p])], near_send.at[at],
                    near_recv.at[at], first[p](d))

    def far_copy(p, d, k, block=None):
        rel = (side[-d] + side[d])[k]
        at = (p, slot[d], rel)
        return send(own.at[unit(p, d if block is None else block, rel)], far.at[at].at[pl.ds(0, size[p])],
                    far_send.at[at], far_recv.at[at], first[p](d))

    def part_copy(p, d):
        lanes = lanes_of[1 if d == 1 else 2]
        at = (p, slot[d])
        return send(own.at[unit(p, 0, 2), lanes], part.at[at].at[pl.ds(0, size[p]), lanes], part_send.at[at],
                    part_recv.at[at], second[p](d))

    def last_copy(p, d, k):
        lanes = lanes_of[(2 - k) if d == 1 else (1 + k)]
        at = (p, slot[d], k)
        return send(own.at[unit(p, 0, d), lanes], part.at[p, 2 + slot[d]].at[pl.ds(0, size[p]), lanes],
                    last_send.at[at], last_recv.at[at], second[p](d))

    def cross_copy(p):
        return send(own.at[unit(p, 0, 0)], cross.at[p], cross_send.at[p], cross_recv.at[p], across)

    def share_copy(i):
        rows = pl.ds(pl.multiple_of(THIRD + (1 - z) * SHARE + i * UNIT, UNIT), UNIT)
        return send(own.at[rows], share.at[pl.ds(i * UNIT, UNIT)], share_send.at[i], share_recv.at[i], across)

    def share_back(half):
        rows = pl.ds(pl.multiple_of(THIRD + half * SHARE, UNIT), SHARE)
        return send(total.at[rows], total.at[rows], share_send.at[4], share_recv.at[4], across)

    def back_copy(p, d, rel=0, on=0):
        at = (p, slot[d], on)
        lanes = lanes_of[0 if not on else 1 if d == 1 else 2]
        ref = total.at[unit(p, 0, rel), lanes]
        source = own.at[unit(p, 0, rel), lanes] if rel == 0 else ref
        return send(source, ref, back_send.at[at], back_recv.at[at], second[p](d))

    def wide_copy(p, d, rel, block=0, on=0):
        at = (p, slot[d], rel + 4 * on)
        ref = total.at[unit(p, block, rel)]
        source = own.at[unit(p, block, rel)] if block == 0 and rel == 0 else ref
        return send(source, ref, wide_send.at[at], wide_recv.at[at], first[p](d))

    def start_near(parts):
        for k in range(2):
            for p in parts:
                for d in (1, -1):
                    go(near_copy(p, d, k))

    def start_far(parts):
        for k in range(2):
            for p in parts:
                for d in (1, -1):
                    go(far_copy(p, d, k))

    def finish_near(parts):
        for k in range(2):
            for p in parts:
                for d in (1, -1):
                    near_copy(p, d, k).wait_recv()
                    add(unit(p, d, side[d][k]), [near.at[p, slot[d], k]])
                    go(far_copy(p, d, 2 + k))

    def collect(p, rel):
        for d in (1, -1):
            far_copy(p, d, (side[-d] + side[d]).index(rel), 0).wait_recv()
        add(unit(p, 0, rel), [far.at[p, 0, rel], far.at[p, 1, rel]])

    def start_second(parts):
        for p in parts:
            collect(p, 2)
            for d in (1, -1):
                go(part_copy(p, d))
        for rel, d in ((3, -1), (1, 1)):
            for p in parts:
                collect(p, rel)
                go(last_copy(p, d, 0))
        for p in parts:
            collect(p, 0)

    def finish_part(parts):
        for d in (1, -1):
            for p in parts:
                part_copy(p, d).wait_recv()
                add(unit(p, 0, d), [part.at[p, slot[d]]], lanes_of[1 if d == 1 else 2])
                go(last_copy(p, d, 1))

    def finish_second(parts):
        for p in parts:
            for d in (1, -1):
                for k in range(2):
                    last_copy(p, d, k).wait_recv()
            add(unit(p, 0, 0), [part.at[p, 2], part.at[p, 3]])

    def keep_copy(p):
        rows = unit(p, 0, 0)
        return pltpu.make_async_copy(own.at[rows], total.at[rows], own_sem.at[p])

    def start_back(parts):
        for p in parts:
            for d in (1, -1):
                go(back_copy(p, d))
            for d in (1, -1):
                go(wide_copy(p, d, 0))
            keep_copy(p).start()

    def pass_back(parts):
        for d in (1, -1):
            for p in parts:
                back_copy(p, d, -d).wait_recv()
                go(back_copy(p, d, -d, 1))
                for e in (1, -1):
                    go(wide_copy(p, e, -d % 4))

    def finish_back(parts):
        for p in parts:
            for d in (1, -1):
                back_copy(p, d, 2, 1).wait_recv()
            for d in (1, -1):
                go(wide_copy(p, d, 2))

    def pass_wide(parts):
        for k in range(2):
            for d in (1, -1):
                for p in parts:
                    rel = on_side[d][k]
                    wide_copy(p, d, rel, -d).wait_recv()
                    go(wide_copy(p, d, rel, -d, 1))

    def finish_wide(parts):
        for p in parts:
            for d in (1, -1):
                for rel in range(4):
                    if rel not in on_side[d]:
                        wide_copy(p, d, rel, -d).wait_recv()
                for rel in on_side[d]:
                    wide_copy(p, d, rel, 2, 1).wait_recv()

    big, small = (0, 1), (2, 3)
    for p in big:
        block_products(p, 2)
    start_near(big)
    for i in range(4):
        product(THIRD // UNIT + (1 - z) * 4 + i)
        go(share_copy(i))
    for d in (1, -1):
        for p in big:
            block_products(p, d)
    start_far(big)
    for p in big:
        block_products(p, 0)
    products(THIRD // UNIT + z * 4, 4)
    finish_near(big)
    for i in range(4):
        share_copy(i).wait_recv()
        rows = pl.ds(pl.multiple_of(THIRD + z * SHARE + i * UNIT, UNIT), UNIT)
        add(rows, [share.at[pl.ds(i * UNIT, UNIT)]])
    start_near(small)
    start_far(small)
    start_second(big)
    finish_near(small)
    finish_part(big)
    start_second(small)
    finish_second(big)
    for p in big:
        cross_copy(p).start()
    finish_part(small)
    finish_second(small)
    start_back(small)
    pass_back(small)
    for p in big:
        cross_copy(p).wait()
        add(unit(p, 0, 0), [cross.at[p]])
    start_back(big)
    finish_back(small)
    pass_wide(small)
    pass_back(big)
    finish_wide(small)
    for p in small:
        keep_copy(p).wait()
    go(share_back(z))
    finish_back(big)
    pass_wide(big)
    finish_wide(big)
    for p in big:
        keep_copy(p).wait()
    share_back(1 - z).wait_recv()
    for copy in started:
        copy.wait_send()


def reduce_over_dp(left, dz):
    whole = pl.BlockSpec(memory_space=pltpu.VMEM)
    half = jnp.bfloat16
    dma = pltpu.SemaphoreType.DMA
    return pl.pallas_call(
        reduce_kernel,
        out_shape=jax.ShapeDtypeStruct((UNITS * UNIT, WIDE), half),
        in_specs=[whole] * 2,
        out_specs=pl.BlockSpec(memory_space=pl.ANY),
        scratch_shapes=[
            pltpu.VMEM((UNITS * UNIT, WIDE), half),
            pltpu.VMEM((4, 2, 2, BIG, WIDE), half),
            pltpu.VMEM((4, 2, 4, BIG, WIDE), half),
            pltpu.VMEM((4, 4, BIG, WIDE), half),
            pltpu.VMEM((2, BIG, WIDE), half),
            pltpu.VMEM((SHARE, WIDE), half),
            dma((4, 2, 2)), dma((4, 2, 2)), dma((4, 2, 4)), dma((4, 2, 4)), dma((4, 2)), dma((4, 2)),
            dma((4, 2, 2)), dma((4, 2, 2)), dma((2,)), dma((2,)), dma((4, 2, 2)), dma((4, 2, 2)),
            dma((4, 2, 8)), dma((4, 2, 8)), dma((5,)), dma((5,)), dma((4,)),
        ],
        compiler_params=pltpu.CompilerParams(
            vmem_limit_bytes=32 << 20, collective_id=1, has_side_effects=True
        ),
        name="reduce",
    )(left, dz)


def finish_kernel(
    hp_one, source, u_two, hp_two, drop_one, drop_two, o_in_one, o_rec_one, o_bias_one, o_in_two, o_rec_two, o_bias_two
):
    step = pl.program_id(0)

    def wide(ref):
        return ref[:, :HID].astype(jnp.float32)

    o_rec_one[...] = wide(hp_one) * drop_one[...].astype(jnp.float32) * weight_scale
    o_rec_two[...] = wide(hp_two) * drop_two[...].astype(jnp.float32) * weight_scale
    o_in_one[...] = wide(source)
    o_in_two[...] = wide(u_two)

    @pl.when(step == D_IN // SLAB)
    def _():
        o_bias_one[...] = wide(source)[D_IN % SLAB]

    @pl.when(step == HID // SLAB)
    def _():
        o_bias_two[...] = wide(u_two)[HID % SLAB]


def finish(total, drop_one, drop_two):
    def units(first, last):
        return pl.BlockSpec((SLAB, WIDE), lambda i: (first + jnp.minimum(i, last), 0))

    def rows(last):
        return pl.BlockSpec((SLAB, HID), lambda i: (jnp.minimum(i, last), 0))

    one = pl.BlockSpec((HID,), lambda i: (0,))
    count, short = WIDE // SLAB - 1, D_IN // SLAB
    square, line = jax.ShapeDtypeStruct((HID, HID), jnp.float32), jax.ShapeDtypeStruct((HID,), jnp.float32)
    return pl.pallas_call(
        finish_kernel,
        grid=(count + 1,),
        in_specs=[
            units(HP_ONE // SLAB, count), units(SOURCE // SLAB, short), units(U_TWO // SLAB, count),
            units(HP_TWO // SLAB, count), rows(count), rows(count),
        ],
        out_specs=[rows(short), rows(count), one, rows(count), rows(count), one],
        out_shape=[jax.ShapeDtypeStruct((D_IN, HID), jnp.float32), square, line, square, square, line],
        compiler_params=pltpu.CompilerParams(vmem_limit_bytes=30 << 20),
        name="finish",
    )(total, total, total, total, drop_one, drop_two)


def local(
    inputs, resets, in_mask, mid_mask, out_mask,
    w_ih_one, w_hh_one, bias_one, drop_one, w_ih_two, w_hh_two, bias_two, drop_two, cotangent,
):
    pipe = lax.axis_index("pipe")
    w_one = jnp.concatenate([w_ih_one, bias_one[None]], 0)
    w_one = jnp.pad(w_one, ((0, D_WIDE - D_IN - 1), (0, WIDE - HID)))
    last = WIDE - UNIT
    tails = jnp.stack([
        jnp.pad(w_hh_one[last:] * drop_one[last:].astype(jnp.bfloat16) * weight_scale, ((0, 2), (0, 2))),
        jnp.pad(w_hh_two[last:] * drop_two[last:].astype(jnp.bfloat16) * weight_scale, ((0, 2), (0, 2))),
        jnp.pad(jnp.concatenate([w_ih_two[last:], bias_two[None]], 0), ((0, 1), (0, 2))),
    ])
    left, out_two, dz, dx, _, _ = relay(
        w_one, tails, w_hh_one, drop_one, w_hh_two, drop_two, w_ih_two,
        inputs, in_mask, mid_mask, out_mask, cotangent, resets,
    )
    left = left.reshape(STEPS * ROWS, UNITS * UNIT)
    total = reduce_over_dp(left, dz.reshape(2, STEPS * ROWS, WIDE))

    u_two = left[:, U_TWO : U_TWO + WIDE].reshape(out_two.shape)
    layer = jnp.where(pipe < 2, u_two, out_two).reshape(STEPS, 2, 2, WIDE)[..., :HID]
    layer = lax.dynamic_index_in_dim(layer, pipe % 2, 1, keepdims=False)
    layer_outputs = jnp.swapaxes(layer, 0, 1)[None]
    grad_input = jnp.transpose(dx.reshape(STEPS, 2, 2, 128)[..., :100], (1, 2, 0, 3))
    keep_in = in_mask.astype(jnp.float32) * keep_scale
    keep_part = lax.dynamic_slice_in_dim(keep_in, pipe * 100, 100, 2)
    grad_input = grad_input * keep_part[:, :, None, :]

    in_one, rec_one, bias_one, in_two, rec_two, bias_two = finish(total, drop_one, drop_two)
    return (layer_outputs, grad_input, in_one, rec_one, bias_one, in_two, rec_two, bias_two)


def solution(mesh):
    placed = (
        P(None, "dp", None, None),
        P(None, "dp"),
        P(None, "dp", None),
        P(None, "dp", None),
        P(None, "dp", None),
        P(None, "pipe"),
        P(None, "pipe"),
        P("pipe"),
        P(None, "pipe"),
        P(None, "pipe"),
        P(None, "pipe"),
        P("pipe"),
        P(None, "pipe"),
        P(None, "dp", None, None),
    )
    return jax.shard_map(
        local,
        mesh=mesh,
        in_specs=placed,
        out_specs=(
            P("pipe", "dp", None, None),
            P(None, "dp", None, "pipe"),
            P(None, "pipe"),
            P(None, "pipe"),
            P("pipe"),
            P(None, "pipe"),
            P(None, "pipe"),
            P("pipe"),
        ),
        check_vma=False,
    )
```

```python
import functools

import jax
import jax.numpy as jnp
from jax import lax
from jax.experimental import pallas as pl
from jax.experimental.pallas import tpu as pltpu
from jax.sharding import PartitionSpec as P

MESH = pl.DeviceIdType.MESH
HID = 1150
WIDE = 1152
D_IN = 400
D_WIDE = 416
STEPS = 88
ROWS = 4
CHUNKS = 44
GROUP = 4
LATER = 3
TURNS = 36
UNIT = 128
HALF_UNIT = 64
UNITS = 32
HP_ONE, U_TWO, HP_TWO, SOURCE = 0, 1152, 2304, 3456
SOURCE_WIDE = 640
SLAB = 384
DEEP = 4
BIG, SMALL = 96, 16
THIRD = 32 * BIG
SHARE = 32 * SMALL

keep_scale = 4.0 / 3.0
weight_scale = 2.0

LAYER_ONE, SOURCE_GRAD, LAYER_TWO, BETWEEN = 0, 1, 2, 3
W_ONE, R_ONE, R_TWO, W_TWO, R_ONE_T, R_TWO_T, W_TWO_T, W_ONE_T = range(8)
USER = {
    W_ONE: LAYER_ONE,
    R_ONE: LAYER_ONE,
    R_TWO: LAYER_TWO,
    W_TWO: BETWEEN,
    R_ONE_T: LAYER_ONE,
    R_TWO_T: LAYER_TWO,
    W_TWO_T: BETWEEN,
    W_ONE_T: SOURCE_GRAD,
}
FORWARD = (W_ONE,)
BACKWARD = (R_TWO_T, W_TWO_T, R_ONE_T, W_ONE_T)


def sigmoid(value):
    return 0.5 * jnp.tanh(0.5 * value) + 0.5


def dot(left, right):
    return jnp.dot(left, right, preferred_element_type=jnp.float32)


def relay_kernel(
    plain_in, tails, r_one, drop_one, r_two, drop_two, w_two,
    inputs, in_mask, mid_mask, out_mask, cotangent, resets,
    o_left, o_out, o_dz, o_dx, turned, turned_in,
    raw_weights, raw_drop, raw_sem, plain, turn, small, apart, turn_sem,
    w_front, w_back, zx, extra, dz, du, dx, above, line, spread, keep, layer_keep, hidden, cell, stage_a, stage_b, stage_z,
    block_send, block_recv, block_local, cross_send, cross_recv, ring_send, ring_recv, go_on,
    u_send, u_recv, z_send, z_recv, dz_send, dz_recv, du_send, du_recv,
    bulk_send, bulk_recv, part_send, part_recv, dx_send, dx_recv, local_sem,
):
    o_hp_one, o_u, o_hp_two = (o_left.at[:, :, pl.ds(start, WIDE)] for start in (HP_ONE, U_TWO, HP_TWO))
    o_dz_one, o_dz_two = o_dz.at[0], o_dz.at[1]
    pipe = lax.axis_index("pipe")
    dp = lax.axis_index("dp")
    dp_count = lax.axis_size("dp")
    dp_far = lax.rem(dp + dp_count // 2, dp_count)

    barrier = pltpu.get_barrier_semaphore()
    for step in range(1, 4):
        pl.semaphore_signal(
            barrier, inc=1, device_id={"pipe": lax.rem(pipe + step, 4), "dp": dp}, device_id_type=MESH
        )
    for step in range(4):
        pl.semaphore_signal(
            barrier, inc=1, device_id={"pipe": lax.rem(pipe + step, 4), "dp": dp_far}, device_id_type=MESH
        )
    z, x, y = dp // 16, lax.rem(dp // 4, 4), lax.rem(dp, 4)
    rings = (
        lambda d: {"pipe": pipe, "dp": z * 16 + lax.rem(x + d + 4, 4) * 4 + y},
        lambda d: {"pipe": pipe, "dp": z * 16 + x * 4 + lax.rem(y + d + 4, 4)},
    )
    for ring in rings:
        for d in (1, -1):
            pl.semaphore_signal(barrier, inc=1, device_id=ring(d), device_id_type=MESH)

    def make_plain(m, also=None):
        weights, drop = ((r_one, drop_one), (r_two, drop_two), (w_two, None))[m]
        plain[m, :, pl.ds(HID // UNIT * UNIT, UNIT)] = jnp.zeros((WIDE, UNIT), jnp.bfloat16)

        def copies(i):
            slot = lax.rem(i, DEEP)
            span = pl.ds(pl.multiple_of(i * UNIT, UNIT), UNIT)
            return [
                pltpu.make_async_copy(array.at[span], raw.at[slot], raw_sem.at[k, slot])
                for k, (array, raw) in enumerate(((weights, raw_weights), (drop, raw_drop)))
                if array is not None
            ]

        def start(i):
            for copy in copies(i):
                copy.start()

        whole = HID // UNIT

        def body(i, carry):
            for copy in copies(i):
                copy.wait()
            slot = lax.rem(i, DEEP)
            value = raw_weights[slot]
            if drop is not None:
                value = value.astype(jnp.float32) * raw_drop[slot].astype(jnp.float32) * weight_scale
            plain[m, pl.ds(pl.multiple_of(i * UNIT, UNIT), UNIT), pl.ds(0, HID)] = value.astype(jnp.bfloat16)
            pl.when(i + DEEP < whole)(lambda: start(i + DEEP))
            if also is not None:
                also(i)
            return carry

        for i in range(DEEP):
            start(i)
        plain[m, pl.ds(whole * UNIT, UNIT)] = tails[m]
        lax.fori_loop(0, whole, body, 0)
        if also is not None:
            also(whole)

    def turn_copy(m, i, slot):
        rows = pl.ds(pl.multiple_of(i * UNIT, UNIT), UNIT)
        return pltpu.make_async_copy(turn.at[slot], turned.at[m, rows], turn_sem.at[slot])

    def make_turned(m, order, i):
        slot = lax.rem(order * (WIDE // UNIT) + i, 2)
        if order:
            turn_copy(m, i, slot).wait()
        else:
            pl.when(i >= 2)(lambda: turn_copy(m, i, slot).wait())
        value = plain[m, :, pl.ds(pl.multiple_of(i * UNIT, UNIT), UNIT)].astype(jnp.float32).T
        column = lax.broadcasted_iota(jnp.int32, (UNIT, WIDE), 1)
        turn[slot] = jnp.where(column < HID, value, 0.0).astype(jnp.bfloat16)
        turn_copy(m, i, slot).start()

    def turn_in_copy(i):
        slot = lax.rem(i, 2)
        rows = pl.ds(pl.multiple_of(i * UNIT, UNIT), UNIT)
        return pltpu.make_async_copy(turn.at[slot, :, pl.ds(0, 512)], turned_in.at[rows], turn_sem.at[slot])

    def make_turned_in(i, carry):
        small[...] = plain_in[:D_IN, pl.ds(pl.multiple_of(i * UNIT, UNIT), UNIT)].astype(jnp.float32)
        for q in range(4):
            apart[q * UNIT : q * UNIT + 100, :] = small[q * 100 : q * 100 + 100, :]
        pl.when(i >= 2)(lambda: turn_in_copy(i).wait())
        turn[lax.rem(i, 2), :, pl.ds(0, 512)] = apart[...].T.astype(jnp.bfloat16)
        turn_in_copy(i).start()
        return carry

    def finish_turned(m, order):
        def body(i, carry):
            make_turned(m, order, i)
            return carry

        lax.fori_loop(0, WIDE // UNIT, body, 0)
        for slot in range(2):
            turn_copy(m, 0, slot).wait()
        apart[...] = jnp.zeros_like(apart)
        lax.fori_loop(0, WIDE // UNIT, make_turned_in, 0)
        for i in range(2):
            turn_in_copy(i).wait()

    @pl.when(pipe >= 2)
    def _():
        make_plain(0)

    @pl.when(pipe < 2)
    def _():
        make_plain(2)

    pl.semaphore_wait(barrier, 11)

    blocks = {
        W_ONE: plain_in, R_ONE: plain.at[0], R_TWO: plain.at[1], W_TWO: plain.at[2],
        R_ONE_T: turned.at[0], R_TWO_T: turned.at[1], W_TWO_T: turned.at[2], W_ONE_T: turned_in,
    }

    def landing(kind, p):
        if kind == W_ONE:
            return w_back.at[p, pl.ds(0, D_WIDE)]
        if kind in (R_ONE, R_TWO, W_TWO):
            return w_front.at[p]
        if kind == W_ONE_T:
            return w_front.at[p, :, pl.ds(0, 512)]
        return w_back.at[p]

    def block_copies(kind, p, turn=None):
        user = USER[kind]
        source_ref, target = blocks[kind], landing(kind, p)
        if p == user:
            return [pltpu.make_async_copy(source_ref, target, block_local.at[kind])]
        if p // 2 == user // 2:
            return [
                pltpu.make_async_remote_copy(
                    source_ref, target, block_send.at[kind, 0], block_recv.at[kind, p, 0],
                    device_id={"pipe": user, "dp": dp}, device_id_type=MESH,
                )
            ]
        rows = source_ref.shape[0] // 2
        if turn is None:
            spans = [pl.ds(part * rows, rows) for part in range(2)]
        else:
            piece = rows // TURNS
            spans = [pl.ds(pl.multiple_of(part * rows + turn * piece, piece), piece) for part in range(2)]
        return [
            pltpu.make_async_remote_copy(
                source_ref.at[spans[part]], target.at[spans[part]],
                block_send.at[kind, part], block_recv.at[kind, p, part],
                device_id={"pipe": user, "dp": (dp, dp_far)[part]}, device_id_type=MESH,
            )
            for part in range(2)
        ]

    def rows_at(first, count=UNIT):
        return pl.ds(pl.multiple_of(first, 64), count)

    def part_rows(ring, step):
        place = (x, y)[ring]
        return UNIT * (1 + 4 * ring + lax.rem(place + step + 4, 4))

    def from_other_plane(kind):
        return [p for p in range(4) if p // 2 != USER[kind] // 2]

    def cross_copy(kind, p, k, slot):
        rows = rows_at((part_rows(0, 0), part_rows(1, 0), 0)[k])
        return pltpu.make_async_remote_copy(
            blocks[kind].at[rows], w_front.at[p, rows], cross_send.at[slot, k], cross_recv.at[p % 2, k],
            device_id={"pipe": USER[kind], "dp": (dp, dp_far)[p % 2]}, device_id_type=MESH,
        )

    def ring_copy(p, ring, d, on):
        k = 2 * on + (0 if d == 1 else 1)
        if on:
            rows = rows_at(part_rows(ring, -d) + (0 if d == 1 else HALF_UNIT), HALF_UNIT)
        else:
            rows = rows_at(part_rows(ring, 0))
        ref = w_front.at[p, rows]
        return pltpu.make_async_remote_copy(
            ref, ref, ring_send.at[p % 2, ring, k], ring_recv.at[p % 2, ring, k],
            device_id=rings[ring](d), device_id_type=MESH,
        )

    def ring_arrival(p, ring, d, on):
        k = 2 * on + (0 if d == 1 else 1)
        if on:
            rows = rows_at(part_rows(ring, 2) + (0 if d == 1 else HALF_UNIT), HALF_UNIT)
        else:
            rows = rows_at(part_rows(ring, -d))
        ref = w_front.at[p, rows]
        return pltpu.make_async_remote_copy(
            ref, ref, ring_send.at[p % 2, ring, k], ring_recv.at[p % 2, ring, k],
            device_id=rings[ring](d), device_id_type=MESH,
        )

    SPREAD = (W_TWO, R_TWO, R_ONE)

    def start_cross(me, kind, ks):
        slot = (R_TWO, W_TWO, R_ONE).index(kind) % 2
        for k in ks:
            cross_copy(kind, me, k, slot).start()

    def start_spread(me):
        if me // 2 == 1:
            start_cross(me, R_ONE, (0, 1))
            start_blocks(FORWARD, me)
            start_cross(me, R_ONE, (2,))
            make_plain(2, functools.partial(make_turned, 0, 0))
            block_copies(W_TWO, me)[0].start()
            make_plain(1, functools.partial(make_turned, 2, 1))
            block_copies(R_TWO, me)[0].start()
            finish_turned(1, 2)
        else:
            start_cross(me, W_TWO, (0, 1))
            start_blocks(FORWARD, me)
            make_plain(1, functools.partial(make_turned, 2, 0))
            start_cross(me, R_TWO, (0, 1))
            start_cross(me, W_TWO, (2,))
            start_cross(me, R_TWO, (2,))
            make_plain(0, functools.partial(make_turned, 1, 1))
            block_copies(R_ONE, me)[0].start()
            finish_turned(0, 2)

    def finish_spread(me):
        kinds = [kind for kind in SPREAD if me // 2 != USER[kind] // 2]
        for kind in kinds:
            slot = (R_TWO, W_TWO, R_ONE).index(kind) % 2
            for k in range(3):
                cross_copy(kind, me, k, slot).wait_send()
        for kind in SPREAD:
            if me // 2 == USER[kind] // 2 and me != USER[kind]:
                block_copies(kind, me)[0].wait_send()

    def share_blocks(kind):
        others = from_other_plane(kind)
        for ring in range(2):
            for p in others:
                cross_copy(kind, p, ring, 0).wait_recv()
                for d in (1, -1):
                    ring_copy(p, ring, d, 0).start()
        for d in (1, -1):
            for p in others:
                for ring in range(2):
                    ring_arrival(p, ring, d, 0).wait_recv()
                    ring_copy(p, ring, d, 1).start()

    def receive_rest(kind):
        me = USER[kind]
        others = from_other_plane(kind)
        for p in others:
            cross_copy(kind, p, 2, 0).wait_recv()
            for ring in range(2):
                for d in (1, -1):
                    ring_arrival(p, ring, d, 1).wait_recv()
        for p in (me, me ^ 1):
            copy = block_copies(kind, p)[0]
            if p == me:
                copy.wait()
            else:
                copy.wait_recv()

    def finish_rings(kind):
        for p in from_other_plane(kind):
            for ring in range(2):
                for d in (1, -1):
                    for on in range(2):
                        ring_copy(p, ring, d, on).wait_send()

    def start_blocks(kinds, p):
        for kind in kinds:
            for copy in block_copies(kind, p):
                copy.start()

    def start_near(p):
        for kind in BACKWARD:
            if p // 2 == USER[kind] // 2:
                for copy in block_copies(kind, p):
                    copy.start()

    def start_turn(p, turn):
        for kind in BACKWARD:
            if p // 2 != USER[kind] // 2:
                for copy in block_copies(kind, p, turn):
                    copy.start()

    def finish_blocks(kinds, p):
        for kind in kinds:
            if p != USER[kind]:
                for copy in block_copies(kind, p):
                    copy.wait_send()

    def await_blocks(kind):
        for p in range(4):
            for copy in block_copies(kind, p):
                if p == USER[kind]:
                    copy.wait()
                else:
                    copy.wait_recv()

    def to(pipe_to, source_ref, target, send, recv):
        return pltpu.make_async_remote_copy(
            source_ref, target, send, recv,
            device_id={"pipe": pipe_to, "dp": dp}, device_id_type=MESH,
        )

    def copy_u(c):
        return to(BETWEEN, o_u.at[c], o_u.at[c], u_send, u_recv.at[c])

    def copy_z(c):
        return to(LAYER_TWO, zx.at[c], zx.at[c], z_send, z_recv.at[c])

    def copy_dz(pipe_to, c):
        return to(pipe_to, dz.at[:, c], dz.at[:, c], dz_send, dz_recv.at[c])

    def copy_du(c):
        return to(LAYER_ONE, du.at[c], du.at[c], du_send, du_recv.at[c])

    def copy_part(pipe_to, output, group, slot, gate):
        span = pl.ds(group * GROUP, GROUP)
        return to(pipe_to, dz.at[gate, span], output.at[span], part_send.at[slot], part_recv.at[group])

    def copy_dx(pipe_to, group, slot):
        count = GROUP * 2 * ROWS
        span = pl.ds(pl.multiple_of(group * count, count), count)
        return to(
            pipe_to, dx.at[span, pl.ds(pipe_to * 128, 128)], o_dx.at[span], dx_send.at[slot], dx_recv.at[group]
        )

    def copy_bulk(pipe_to, ref, slot, which):
        return to(pipe_to, ref, ref, bulk_send.at[slot], bulk_recv.at[which])

    def keep_rows(c, j):
        return jnp.broadcast_to(keep[c, ROWS * j : ROWS * j + ROWS, 0:1], (ROWS, WIDE))

    def by_time(target, width, whole, value_of):
        for start in range(0, whole, 128):
            count = min(128, width - start)
            if count < 128:
                line[...] = jnp.zeros_like(line)
            for i in range(ROWS):
                value = value_of(i, slice(start, start + count))
                if count < 128:
                    line[:, :count] = value
                    value = line[...]
                spread[pl.ds(i, STEPS, stride=ROWS), :] = value
            target[:, start : start + 128] = spread[...]

    def set_up():
        shape = (CHUNKS, 2 * ROWS, 128)
        row = lax.broadcasted_iota(jnp.int32, shape, 1)
        time = 2 * lax.broadcasted_iota(jnp.int32, shape, 0) + row // ROWS
        stream = lax.rem(row, ROWS)
        reset = jnp.zeros(shape, jnp.int32)
        for i in range(ROWS):
            reset = jnp.where(stream == i, resets[i // 2, i % 2], reset)
        keep[...] = jnp.where(time == reset, 0.0, 1.0)
        layer_keep[...] = jnp.zeros_like(layer_keep)
        for i in range(ROWS):
            h, s = i // 2, i % 2
            for m, mask in enumerate((mid_mask, out_mask)):
                layer_keep[m, i : i + 1, :HID] = mask[h, s : s + 1, :].astype(jnp.float32) * keep_scale

        def masked(i, lanes):
            h, s = i // 2, i % 2
            kept = in_mask[h, s : s + 1, lanes].astype(jnp.float32) * keep_scale
            return (inputs[h, s, :, lanes] * kept).astype(jnp.bfloat16).astype(jnp.float32)

        by_time(dx, D_IN, 512, masked)
        column = lax.broadcasted_iota(jnp.int32, (STEPS * ROWS, 512), 1)
        value = jnp.where(column == D_IN, 1.0, dx[...])
        dx[...] = value
        o_left[:, :, pl.ds(SOURCE, 512)] = value.astype(jnp.bfloat16).reshape(CHUNKS, 2 * ROWS, 512)
        o_left[:, :, pl.ds(SOURCE + 512, 128)] = jnp.zeros((CHUNKS, 2 * ROWS, 128), jnp.bfloat16)

    def set_up_above():
        def masked(i, lanes):
            return cotangent[i // 2, i % 2, :, lanes].astype(jnp.float32) * layer_keep[1, i : i + 1, lanes]

        by_time(above, HID, WIDE, masked)

    def clear():
        hidden[...] = jnp.zeros_like(hidden)
        cell[...] = jnp.zeros_like(cell)

    def forward_pair(c, mask, with_one, o_hp, o_layer):
        column = lax.broadcasted_iota(jnp.int32, (ROWS, WIDE), 1)
        for j in range(2):
            rows = pl.ds(ROWS * j, ROWS)
            kept = keep_rows(c, j)
            hidden_prev = hidden[...] * kept
            cell_prev = cell[...] * kept
            left = hidden_prev.astype(jnp.bfloat16)
            gates = [
                dot(left, w_front[g]) + zx[c, rows, pl.ds(g * WIDE, WIDE)] for g in range(4)
            ]
            gate_in, gate_forget = sigmoid(gates[0]), sigmoid(gates[1])
            gate_cand, gate_out = jnp.tanh(gates[2]), sigmoid(gates[3])
            cell_now = gate_forget * cell_prev + gate_in * gate_cand
            cell_tanh = jnp.tanh(cell_now)
            hidden_now = (gate_out * cell_tanh).astype(jnp.bfloat16).astype(jnp.float32)
            cell[...] = cell_now
            hidden[...] = hidden_now
            stage_a[rows, :] = hidden_prev
            layer = hidden_now * mask
            if with_one:
                layer = jnp.where(column == HID, 1.0, layer)
            stage_b[rows, :] = layer
            zx[c, rows, pl.ds(0, WIDE)] = gate_cand * gate_in * (1.0 - gate_in)
            zx[c, rows, pl.ds(WIDE, WIDE)] = cell_prev * gate_forget * (1.0 - gate_forget)
            zx[c, rows, pl.ds(2 * WIDE, WIDE)] = gate_in * (1.0 - gate_cand * gate_cand)
            zx[c, rows, pl.ds(3 * WIDE, WIDE)] = cell_tanh * gate_out * (1.0 - gate_out)
            extra[c, rows, pl.ds(0, WIDE)] = gate_out * (1.0 - cell_tanh * cell_tanh)
            extra[c, rows, pl.ds(WIDE, WIDE)] = gate_forget * kept
        o_hp[c] = stage_a[...].astype(jnp.bfloat16)
        o_layer[c] = stage_b[...].astype(jnp.bfloat16)

    def backward_pair(c, upstream):
        for j in (1, 0):
            rows = pl.ds(ROWS * j, ROWS)
            total = hidden[...] + upstream[ROWS * j : ROWS * j + ROWS]
            out_grad = total * zx[c, rows, pl.ds(3 * WIDE, WIDE)]
            cell_total = cell[...] + total * extra[c, rows, pl.ds(0, WIDE)]
            cell[...] = cell_total * extra[c, rows, pl.ds(WIDE, WIDE)]
            grads = [cell_total * zx[c, rows, pl.ds(g * WIDE, WIDE)] for g in range(3)] + [out_grad]
            back = None
            for g in range(4):
                stage_z[rows, pl.ds(g * WIDE, WIDE)] = grads[g]
                part = dot(grads[g].astype(jnp.bfloat16), w_back[g])
                back = part if back is None else back + part
            hidden[...] = back * keep_rows(c, j)
        for g in range(4):
            dz[g, c] = stage_z[:, pl.ds(g * WIDE, WIDE)].astype(jnp.bfloat16)

    last = CHUNKS - 1
    groups = CHUNKS // GROUP

    @pl.when(pipe == LAYER_ONE)
    def _():
        me = LAYER_ONE
        start_spread(me)
        set_up()
        share_blocks(R_ONE)
        await_blocks(W_ONE)
        source = dx[:, :D_WIDE].astype(jnp.bfloat16)
        for g in range(4):
            zx[:, :, pl.ds(g * WIDE, WIDE)] = dot(source, w_back[g, :D_WIDE]).reshape(CHUNKS, 2 * ROWS, WIDE)
        receive_rest(R_ONE)
        clear()

        def ahead(c, carry):
            forward_pair(c, layer_keep[0], True, o_hp_one, o_u)
            copy_u(c).start()
            o_out[c] = stage_b[...].astype(jnp.bfloat16)

            @pl.when((c >= LATER) & (c < LATER + TURNS))
            def _():
                pl.semaphore_signal(
                    go_on, inc=1, device_id={"pipe": SOURCE_GRAD, "dp": dp}, device_id_type=MESH
                )
                start_turn(me, c - LATER)

            @pl.when(c == LATER)
            def _():
                start_near(me)

            return carry

        lax.fori_loop(0, CHUNKS, ahead, 0)
        bulk = [
            copy_bulk(SOURCE_GRAD, o_u, 0, 0), copy_bulk(LAYER_TWO, o_u, 1, 0),
            copy_bulk(SOURCE_GRAD, o_hp_one, 2, 1), copy_bulk(LAYER_TWO, o_hp_one, 3, 1),
            copy_bulk(BETWEEN, o_hp_one, 4, 1),
        ]
        for copy in bulk:
            copy.start()
        await_blocks(R_ONE_T)
        clear()

        def behind(i, carry):
            c = last - i
            copy_du(c).wait_recv()
            mask = jnp.concatenate([layer_keep[0]] * 2, 0)
            backward_pair(c, du[c].astype(jnp.float32) * mask)
            copy_dz(SOURCE_GRAD, c).start()

            @pl.when(lax.rem(c, GROUP) == 0)
            def _():
                group = c // GROUP
                copy_part(LAYER_TWO, o_dz_one, group, 0, LAYER_TWO).start()
                copy_part(BETWEEN, o_dz_one, group, 1, BETWEEN).start()

            return carry

        lax.fori_loop(0, CHUNKS, behind, 0)
        own = pltpu.make_async_copy(dz.at[me], o_dz_one, local_sem.at[0])
        own.start()
        finish_rings(R_ONE)
        finish_spread(me)
        finish_blocks(FORWARD + BACKWARD, me)
        to(BETWEEN, o_u, o_u, u_send, u_recv.at[0]).wait_send()
        for copy in bulk:
            copy.wait_send()
        to(SOURCE_GRAD, dz, dz, dz_send, dz_recv.at[0]).wait_send()
        to(LAYER_TWO, dz.at[me], o_dz_one, part_send.at[0], part_recv.at[0]).wait_send()
        to(BETWEEN, dz.at[me], o_dz_one, part_send.at[1], part_recv.at[0]).wait_send()
        own.wait()

        copy_bulk(me, o_hp_two, 0, 2).wait_recv()
        for group in range(groups):
            copy_part(me, o_dz_two, group, 0, me).wait_recv()
            copy_dx(me, group, 0).wait_recv()

    @pl.when(pipe == LAYER_TWO)
    def _():
        me = LAYER_TWO
        start_spread(me)
        set_up()
        set_up_above()
        share_blocks(R_TWO)
        receive_rest(R_TWO)
        clear()

        def ahead(c, carry):
            copy_z(c).wait_recv()

            @pl.when((c >= LATER) & (c < LATER + TURNS))
            def _():
                start_turn(me, c - LATER)

            @pl.when(c == LATER)
            def _():
                start_near(me)

            forward_pair(c, layer_keep[1], False, o_hp_two, o_out)
            return carry

        lax.fori_loop(0, CHUNKS, ahead, 0)
        bulk = [
            copy_bulk(LAYER_ONE, o_hp_two, 0, 2), copy_bulk(SOURCE_GRAD, o_hp_two, 1, 2),
            copy_bulk(BETWEEN, o_hp_two, 2, 2), copy_bulk(BETWEEN, o_out, 3, 3),
        ]
        for copy in bulk:
            copy.start()
        await_blocks(R_TWO_T)
        clear()

        def behind(i, carry):
            c = last - i
            backward_pair(c, above[pl.ds(pl.multiple_of(c * 2 * ROWS, 2 * ROWS), 2 * ROWS), :])
            copy_dz(BETWEEN, c).start()

            @pl.when(lax.rem(c, GROUP) == 0)
            def _():
                group = c // GROUP
                copy_part(LAYER_ONE, o_dz_two, group, 0, LAYER_ONE).start()
                copy_part(SOURCE_GRAD, o_dz_two, group, 1, SOURCE_GRAD).start()

            return carry

        lax.fori_loop(0, CHUNKS, behind, 0)
        own = pltpu.make_async_copy(dz.at[me], o_dz_two, local_sem.at[0])
        own.start()
        finish_rings(R_TWO)
        finish_spread(me)
        finish_blocks(FORWARD + BACKWARD, me)
        for copy in bulk:
            copy.wait_send()
        to(BETWEEN, dz, dz, dz_send, dz_recv.at[0]).wait_send()
        to(LAYER_ONE, dz.at[me], o_dz_two, part_send.at[0], part_recv.at[0]).wait_send()
        to(SOURCE_GRAD, dz.at[me], o_dz_two, part_send.at[1], part_recv.at[0]).wait_send()
        own.wait()

        copy_bulk(me, o_u, 0, 0).wait_recv()
        copy_bulk(me, o_hp_one, 0, 1).wait_recv()
        for group in range(groups):
            copy_part(me, o_dz_one, group, 0, me).wait_recv()
            copy_dx(me, group, 0).wait_recv()

    @pl.when(pipe == BETWEEN)
    def _():
        me = BETWEEN
        start_spread(me)
        set_up()
        share_blocks(W_TWO)
        receive_rest(W_TWO)

        def ahead(c, carry):
            copy_u(c).wait_recv()
            for g in range(4):
                zx[c, :, pl.ds(g * WIDE, WIDE)] = dot(o_u[c], w_front[g])
            copy_z(c).start()

            @pl.when((c >= LATER) & (c < LATER + TURNS))
            def _():
                start_turn(me, c - LATER)

            @pl.when(c == LATER)
            def _():
                start_near(me)

            return carry

        lax.fori_loop(0, CHUNKS, ahead, 0)
        await_blocks(W_TWO_T)

        def behind(i, carry):
            c = last - i
            copy_dz(me, c).wait_recv()
            back = None
            for g in range(4):
                part = dot(dz[g, c], w_back[g])
                back = part if back is None else back + part
            du[c] = back.astype(jnp.bfloat16)
            copy_du(c).start()
            return carry

        lax.fori_loop(0, CHUNKS, behind, 0)
        own = pltpu.make_async_copy(dz.at[me], o_dz_two, local_sem.at[0])
        own.start()
        finish_rings(W_TWO)
        finish_spread(me)
        finish_blocks(FORWARD + BACKWARD, me)
        to(LAYER_TWO, zx, zx, z_send, z_recv.at[0]).wait_send()
        to(LAYER_ONE, du, du, du_send, du_recv.at[0]).wait_send()
        own.wait()

        copy_bulk(me, o_hp_one, 0, 1).wait_recv()
        copy_bulk(me, o_hp_two, 0, 2).wait_recv()
        copy_bulk(me, o_out, 0, 3).wait_recv()
        for group in range(groups):
            copy_part(me, o_dz_one, group, 0, me).wait_recv()
            copy_dx(me, group, 0).wait_recv()

    @pl.when(pipe == SOURCE_GRAD)
    def _():
        me = SOURCE_GRAD
        start_spread(me)
        set_up()

        def pass_on(turn, carry):
            pl.semaphore_wait(go_on, 1)
            start_turn(me, turn)
            return carry

        lax.fori_loop(0, TURNS, pass_on, 0)
        start_near(me)
        copy_bulk(me, o_u, 0, 0).wait_recv()
        mine = pltpu.make_async_copy(o_u, o_out, local_sem.at[0])
        mine.start()
        mine.wait()
        await_blocks(W_ONE_T)

        def behind(i, carry):
            c = last - i
            copy_dz(me, c).wait_recv()
            back = None
            for g in range(4):
                part = dot(dz[g, c], w_front[g, :, :512])
                back = part if back is None else back + part
            dx[pl.ds(pl.multiple_of(c * 2 * ROWS, 2 * ROWS), 2 * ROWS), :] = back

            @pl.when(lax.rem(c, GROUP) == 0)
            def _():
                group = c // GROUP
                copy_dx(LAYER_ONE, group, 0).start()
                copy_dx(LAYER_TWO, group, 1).start()
                copy_dx(BETWEEN, group, 2).start()

            return carry

        lax.fori_loop(0, CHUNKS, behind, 0)
        own = pltpu.make_async_copy(dz.at[me], o_dz_one, local_sem.at[0])
        own.start()
        own_dx = pltpu.make_async_copy(dx.at[:, pl.ds(me * 128, 128)], o_dx, local_sem.at[1])
        own_dx.start()
        finish_spread(me)
        finish_blocks(FORWARD + BACKWARD, me)
        for slot, pipe_to in enumerate((LAYER_ONE, LAYER_TWO, BETWEEN)):
            to(pipe_to, o_dx, o_dx, dx_send.at[slot], dx_recv.at[0]).wait_send()
        own.wait()
        own_dx.wait()

        copy_bulk(me, o_hp_one, 0, 1).wait_recv()
        copy_bulk(me, o_hp_two, 0, 2).wait_recv()
        for group in range(groups):
            copy_part(me, o_dz_two, group, 0, me).wait_recv()


def relay(w_one, tails, r_one, drop_one, r_two, drop_two, w_two, inputs, in_mask, mid_mask, out_mask, cotangent, resets):
    whole, away = pl.BlockSpec(memory_space=pltpu.VMEM), pl.BlockSpec(memory_space=pl.ANY)
    rows = (CHUNKS, 2 * ROWS, WIDE)
    half, full = jnp.bfloat16, jnp.float32
    shapes = [
        jax.ShapeDtypeStruct((CHUNKS, 2 * ROWS, UNITS * UNIT), half),
        jax.ShapeDtypeStruct(rows, half),
        jax.ShapeDtypeStruct((2,) + rows, half),
        jax.ShapeDtypeStruct((STEPS * ROWS, 128), full),
        jax.ShapeDtypeStruct((3, WIDE, WIDE), half),
        jax.ShapeDtypeStruct((WIDE, 512), half),
    ]
    dma = pltpu.SemaphoreType.DMA
    return pl.pallas_call(
        relay_kernel,
        out_shape=shapes,
        in_specs=[whole] * 2 + [away] * 5 + [whole] * 5
        + [pl.BlockSpec(memory_space=pltpu.SMEM)],
        out_specs=[whole] * 4 + [away] * 2,
        scratch_shapes=[
            pltpu.VMEM((DEEP, UNIT, HID), half),
            pltpu.VMEM((DEEP, UNIT, HID), jnp.int32),
            dma((2, DEEP)),
            pltpu.VMEM((3, WIDE, WIDE), half),
            pltpu.VMEM((2, UNIT, WIDE), half),
            pltpu.VMEM((D_IN, UNIT), full),
            pltpu.VMEM((512, UNIT), full),
            dma((2,)),
            pltpu.VMEM((4, WIDE, WIDE), half),
            pltpu.VMEM((4, WIDE, WIDE), half),
            pltpu.VMEM((CHUNKS, 2 * ROWS, 4 * WIDE), full),
            pltpu.VMEM((CHUNKS, 2 * ROWS, 2 * WIDE), full),
            pltpu.VMEM((4,) + rows, half),
            pltpu.VMEM(rows, half),
            pltpu.VMEM((STEPS * ROWS, 512), full),
            pltpu.VMEM((STEPS * ROWS, WIDE), full),
            pltpu.VMEM((STEPS, 128), full),
            pltpu.VMEM((STEPS * ROWS, 128), full),
            pltpu.VMEM((CHUNKS, 2 * ROWS, 128), full),
            pltpu.VMEM((2, ROWS, WIDE), full),
            pltpu.VMEM((ROWS, WIDE), full),
            pltpu.VMEM((ROWS, WIDE), full),
            pltpu.VMEM((2 * ROWS, WIDE), full),
            pltpu.VMEM((2 * ROWS, WIDE), full),
            pltpu.VMEM((2 * ROWS, 4 * WIDE), full),
            dma((8, 2)), dma((8, 4, 2)), dma((8,)),
            dma((2, 3)), dma((2, 3)), dma((2, 2, 4)), dma((2, 2, 4)), pltpu.SemaphoreType.REGULAR,
            dma, dma((CHUNKS,)), dma, dma((CHUNKS,)), dma, dma((CHUNKS,)), dma, dma((CHUNKS,)),
            dma((5,)), dma((4,)), dma((2,)), dma((CHUNKS // GROUP,)), dma((3,)), dma((CHUNKS // GROUP,)), dma((2,)),
        ],
        compiler_params=pltpu.CompilerParams(
            vmem_limit_bytes=60 << 20, collective_id=0, has_side_effects=True
        ),
        name="relay",
    )(w_one, tails, r_one, drop_one, r_two, drop_two, w_two, inputs, in_mask, mid_mask, out_mask, cotangent, resets)


def reduce_kernel(
    left, dz, total, own, near, far, part, cross, share,
    near_send, near_recv, far_send, far_recv, part_send, part_recv, last_send, last_recv,
    cross_send, cross_recv, back_send, back_recv, wide_send, wide_recv, share_send, share_recv, own_sem,
):
    pipe = lax.axis_index("pipe")
    dp = lax.axis_index("dp")
    z, x, y = dp // 16, lax.rem(dp // 4, 4), lax.rem(dp, 4)

    def device(z_, x_, y_):
        return {"pipe": pipe, "dp": z_ * 16 + lax.rem(x_ + 4, 4) * 4 + lax.rem(y_ + 4, 4)}

    along_x, along_y = (lambda d: device(z, x + d, y)), (lambda d: device(z, x, y + d))
    first, second = (along_x, along_y) * 2, (along_y, along_x) * 2
    place = ((x, y), (y, x)) * 2
    across = device(1 - z, x, y)
    size = (BIG, BIG, SMALL, SMALL)
    base = (0, 16 * BIG, THIRD + z * SHARE, THIRD + z * SHARE + 16 * SMALL)

    barrier = pltpu.get_barrier_semaphore()
    for target in (along_x(1), along_x(-1), along_y(1), along_y(-1), across):
        pl.semaphore_signal(barrier, inc=1, device_id=target, device_id_type=MESH)
    pl.semaphore_wait(barrier, 5)

    lanes_of = (pl.ds(0, WIDE), pl.ds(0, 640), pl.ds(640, 512))

    def unit(p, block, rel):
        a, b = place[p]
        index = lax.rem(a + block + 4, 4) * 4 + lax.rem(b + rel + 4, 4)
        return pl.ds(pl.multiple_of(base[p] + index * size[p], 16), size[p])

    def send(source, target, s, r, to):
        return pltpu.make_async_remote_copy(source, target, s, r, device_id=to, device_id_type=MESH)

    def add(rows, others, lanes=lanes_of[0]):
        def body(i, carry):
            span = pl.ds(pl.multiple_of(rows.start + i * 16, 16), 16)
            value = own[span, lanes].astype(jnp.float32)
            for ref in others:
                value = value + ref[pl.ds(pl.multiple_of(i * 16, 16), 16), lanes].astype(jnp.float32)
            own[span, lanes] = value.astype(jnp.bfloat16)
            return carry

        lax.fori_loop(0, rows.size // 16, body, 0)

    def product(u):
        columns = pl.ds(pl.multiple_of(u * UNIT, UNIT), UNIT)
        own[columns, :] = lax.dot_general(
            left[:, columns], dz[jnp.where((u >= U_TWO // UNIT) & (u < SOURCE // UNIT), 1, 0)], (((0,), (0,)), ((), ())),
            preferred_element_type=jnp.float32,
        ).astype(jnp.bfloat16)

    def products(start, count):
        def body(i, carry):
            product(start + i)
            return carry

        lax.fori_loop(0, count, body, 0)

    block_units = 4 * BIG // UNIT

    def block_products(p, block):
        products(p * 4 * block_units + lax.rem(place[p][0] + block + 4, 4) * block_units, block_units)

    side = {1: (2, 1), -1: (3, 0)}
    on_side = {1: (0, 1), -1: (3, 2)}
    slot = {1: 0, -1: 1}
    started = []

    def go(copy):
        copy.start()
        started.append(copy)

    def near_copy(p, d, k):
        at = (p, slot[d], k)
        return send(own.at[unit(p, 2, side[d][k])], near.at[at].at[pl.ds(0, size[p])], near_send.at[at],
                    near_recv.at[at], first[p](d))

    def far_copy(p, d, k, block=None):
        rel = (side[-d] + side[d])[k]
        at = (p, slot[d], rel)
        return send(own.at[unit(p, d if block is None else block, rel)], far.at[at].at[pl.ds(0, size[p])],
                    far_send.at[at], far_recv.at[at], first[p](d))

    def part_copy(p, d):
        lanes = lanes_of[1 if d == 1 else 2]
        at = (p, slot[d])
        return send(own.at[unit(p, 0, 2), lanes], part.at[at].at[pl.ds(0, size[p]), lanes], part_send.at[at],
                    part_recv.at[at], second[p](d))

    def last_copy(p, d, k):
        lanes = lanes_of[(2 - k) if d == 1 else (1 + k)]
        at = (p, slot[d], k)
        return send(own.at[unit(p, 0, d), lanes], part.at[p, 2 + slot[d]].at[pl.ds(0, size[p]), lanes],
                    last_send.at[at], last_recv.at[at], second[p](d))

    def cross_copy(p):
        return send(own.at[unit(p, 0, 0)], cross.at[p], cross_send.at[p], cross_recv.at[p], across)

    def share_copy(i):
        rows = pl.ds(pl.multiple_of(THIRD + (1 - z) * SHARE + i * UNIT, UNIT), UNIT)
        return send(own.at[rows], share.at[pl.ds(i * UNIT, UNIT)], share_send.at[i], share_recv.at[i], across)

    def share_back(half):
        rows = pl.ds(pl.multiple_of(THIRD + half * SHARE, UNIT), SHARE)
        return send(total.at[rows], total.at[rows], share_send.at[4], share_recv.at[4], across)

    def back_copy(p, d, rel=0, on=0):
        at = (p, slot[d], on)
        lanes = lanes_of[0 if not on else 1 if d == 1 else 2]
        ref = total.at[unit(p, 0, rel), lanes]
        source = own.at[unit(p, 0, rel), lanes] if rel == 0 else ref
        return send(source, ref, back_send.at[at], back_recv.at[at], second[p](d))

    def wide_copy(p, d, rel, block=0, on=0):
        at = (p, slot[d], rel + 4 * on)
        ref = total.at[unit(p, block, rel)]
        source = own.at[unit(p, block, rel)] if block == 0 and rel == 0 else ref
        return send(source, ref, wide_send.at[at], wide_recv.at[at], first[p](d))

    def start_near(parts):
        for k in range(2):
            for p in parts:
                for d in (1, -1):
                    go(near_copy(p, d, k))

    def start_far(parts):
        for k in range(2):
            for p in parts:
                for d in (1, -1):
                    go(far_copy(p, d, k))

    def finish_near(parts):
        for k in range(2):
            for p in parts:
                for d in (1, -1):
                    near_copy(p, d, k).wait_recv()
                    add(unit(p, d, side[d][k]), [near.at[p, slot[d], k]])
                    go(far_copy(p, d, 2 + k))

    def collect(p, rel):
        for d in (1, -1):
            far_copy(p, d, (side[-d] + side[d]).index(rel), 0).wait_recv()
        add(unit(p, 0, rel), [far.at[p, 0, rel], far.at[p, 1, rel]])

    def start_second(parts):
        for p in parts:
            collect(p, 2)
            for d in (1, -1):
                go(part_copy(p, d))
        for rel, d in ((3, -1), (1, 1)):
            for p in parts:
                collect(p, rel)
                go(last_copy(p, d, 0))
        for p in parts:
            collect(p, 0)

    def finish_part(parts):
        for d in (1, -1):
            for p in parts:
                part_copy(p, d).wait_recv()
                add(unit(p, 0, d), [part.at[p, slot[d]]], lanes_of[1 if d == 1 else 2])
                go(last_copy(p, d, 1))

    def finish_second(parts):
        for p in parts:
            for d in (1, -1):
                for k in range(2):
                    last_copy(p, d, k).wait_recv()
            add(unit(p, 0, 0), [part.at[p, 2], part.at[p, 3]])

    def keep_copy(p):
        rows = unit(p, 0, 0)
        return pltpu.make_async_copy(own.at[rows], total.at[rows], own_sem.at[p])

    def start_back(parts):
        for p in parts:
            for d in (1, -1):
                go(back_copy(p, d))
            for d in (1, -1):
                go(wide_copy(p, d, 0))
            keep_copy(p).start()

    def pass_back(parts):
        for d in (1, -1):
            for p in parts:
                back_copy(p, d, -d).wait_recv()
                go(back_copy(p, d, -d, 1))
                for e in (1, -1):
                    go(wide_copy(p, e, -d % 4))

    def finish_back(parts):
        for p in parts:
            for d in (1, -1):
                back_copy(p, d, 2, 1).wait_recv()
            for d in (1, -1):
                go(wide_copy(p, d, 2))

    def pass_wide(parts):
        for k in range(2):
            for d in (1, -1):
                for p in parts:
                    rel = on_side[d][k]
                    wide_copy(p, d, rel, -d).wait_recv()
                    go(wide_copy(p, d, rel, -d, 1))

    def finish_wide(parts):
        for p in parts:
            for d in (1, -1):
                for rel in range(4):
                    if rel not in on_side[d]:
                        wide_copy(p, d, rel, -d).wait_recv()
                for rel in on_side[d]:
                    wide_copy(p, d, rel, 2, 1).wait_recv()

    big, small = (0, 1), (2, 3)
    for p in big:
        block_products(p, 2)
    start_near(big)
    for i in range(4):
        product(THIRD // UNIT + (1 - z) * 4 + i)
        go(share_copy(i))
    for d in (1, -1):
        for p in big:
            block_products(p, d)
    start_far(big)
    for p in big:
        block_products(p, 0)
    products(THIRD // UNIT + z * 4, 4)
    finish_near(big)
    for i in range(4):
        share_copy(i).wait_recv()
        rows = pl.ds(pl.multiple_of(THIRD + z * SHARE + i * UNIT, UNIT), UNIT)
        add(rows, [share.at[pl.ds(i * UNIT, UNIT)]])
    start_near(small)
    start_far(small)
    start_second(big)
    finish_near(small)
    finish_part(big)
    start_second(small)
    finish_second(big)
    for p in big:
        cross_copy(p).start()
    finish_part(small)
    finish_second(small)
    start_back(small)
    pass_back(small)
    for p in big:
        cross_copy(p).wait()
        add(unit(p, 0, 0), [cross.at[p]])
    start_back(big)
    finish_back(small)
    pass_wide(small)
    pass_back(big)
    finish_wide(small)
    for p in small:
        keep_copy(p).wait()
    go(share_back(z))
    finish_back(big)
    pass_wide(big)
    finish_wide(big)
    for p in big:
        keep_copy(p).wait()
    share_back(1 - z).wait_recv()
    for copy in started:
        copy.wait_send()


def reduce_over_dp(left, dz):
    whole = pl.BlockSpec(memory_space=pltpu.VMEM)
    half = jnp.bfloat16
    dma = pltpu.SemaphoreType.DMA
    return pl.pallas_call(
        reduce_kernel,
        out_shape=jax.ShapeDtypeStruct((UNITS * UNIT, WIDE), half),
        in_specs=[whole] * 2,
        out_specs=pl.BlockSpec(memory_space=pl.ANY),
        scratch_shapes=[
            pltpu.VMEM((UNITS * UNIT, WIDE), half),
            pltpu.VMEM((4, 2, 2, BIG, WIDE), half),
            pltpu.VMEM((4, 2, 4, BIG, WIDE), half),
            pltpu.VMEM((4, 4, BIG, WIDE), half),
            pltpu.VMEM((2, BIG, WIDE), half),
            pltpu.VMEM((SHARE, WIDE), half),
            dma((4, 2, 2)), dma((4, 2, 2)), dma((4, 2, 4)), dma((4, 2, 4)), dma((4, 2)), dma((4, 2)),
            dma((4, 2, 2)), dma((4, 2, 2)), dma((2,)), dma((2,)), dma((4, 2, 2)), dma((4, 2, 2)),
            dma((4, 2, 8)), dma((4, 2, 8)), dma((5,)), dma((5,)), dma((4,)),
        ],
        compiler_params=pltpu.CompilerParams(
            vmem_limit_bytes=32 << 20, collective_id=1, has_side_effects=True
        ),
        name="reduce",
    )(left, dz)


def finish_kernel(
    hp_one, source, u_two, hp_two, drop_one, drop_two, o_in_one, o_rec_one, o_bias_one, o_in_two, o_rec_two, o_bias_two
):
    step = pl.program_id(0)

    def wide(ref):
        return ref[:, :HID].astype(jnp.float32)

    o_rec_one[...] = wide(hp_one) * drop_one[...].astype(jnp.float32) * weight_scale
    o_rec_two[...] = wide(hp_two) * drop_two[...].astype(jnp.float32) * weight_scale
    o_in_one[...] = wide(source)
    o_in_two[...] = wide(u_two)

    @pl.when(step == D_IN // SLAB)
    def _():
        o_bias_one[...] = wide(source)[D_IN % SLAB]

    @pl.when(step == HID // SLAB)
    def _():
        o_bias_two[...] = wide(u_two)[HID % SLAB]


def finish(total, drop_one, drop_two):
    def units(first, last):
        return pl.BlockSpec((SLAB, WIDE), lambda i: (first + jnp.minimum(i, last), 0))

    def rows(last):
        return pl.BlockSpec((SLAB, HID), lambda i: (jnp.minimum(i, last), 0))

    one = pl.BlockSpec((HID,), lambda i: (0,))
    count, short = WIDE // SLAB - 1, D_IN // SLAB
    square, line = jax.ShapeDtypeStruct((HID, HID), jnp.float32), jax.ShapeDtypeStruct((HID,), jnp.float32)
    return pl.pallas_call(
        finish_kernel,
        grid=(count + 1,),
        in_specs=[
            units(HP_ONE // SLAB, count), units(SOURCE // SLAB, short), units(U_TWO // SLAB, count),
            units(HP_TWO // SLAB, count), rows(count), rows(count),
        ],
        out_specs=[rows(short), rows(count), one, rows(count), rows(count), one],
        out_shape=[jax.ShapeDtypeStruct((D_IN, HID), jnp.float32), square, line, square, square, line],
        compiler_params=pltpu.CompilerParams(vmem_limit_bytes=30 << 20),
        name="finish",
    )(total, total, total, total, drop_one, drop_two)


def local(
    inputs, resets, in_mask, mid_mask, out_mask,
    w_ih_one, w_hh_one, bias_one, drop_one, w_ih_two, w_hh_two, bias_two, drop_two, cotangent,
):
    pipe = lax.axis_index("pipe")
    w_one = jnp.concatenate([w_ih_one, bias_one[None]], 0)
    w_one = jnp.pad(w_one, ((0, D_WIDE - D_IN - 1), (0, WIDE - HID)))
    last = WIDE - UNIT
    tails = jnp.stack([
        jnp.pad(w_hh_one[last:] * drop_one[last:].astype(jnp.bfloat16) * weight_scale, ((0, 2), (0, 2))),
        jnp.pad(w_hh_two[last:] * drop_two[last:].astype(jnp.bfloat16) * weight_scale, ((0, 2), (0, 2))),
        jnp.pad(jnp.concatenate([w_ih_two[last:], bias_two[None]], 0), ((0, 1), (0, 2))),
    ])
    left, layer, dz, dx, _, _ = relay(
        w_one, tails, w_hh_one, drop_one, w_hh_two, drop_two, w_ih_two,
        inputs, in_mask, mid_mask, out_mask, cotangent, resets,
    )
    left = left.reshape(STEPS * ROWS, UNITS * UNIT)
    total = reduce_over_dp(left, dz.reshape(2, STEPS * ROWS, WIDE))

    layer = layer.reshape(STEPS, 2, 2, WIDE)[..., :HID]
    layer = lax.dynamic_index_in_dim(layer, pipe % 2, 1, keepdims=False)
    layer_outputs = jnp.swapaxes(layer, 0, 1)[None]
    grad_input = jnp.transpose(dx.reshape(STEPS, 2, 2, 128)[..., :100], (1, 2, 0, 3))
    keep_in = in_mask.astype(jnp.float32) * keep_scale
    keep_part = lax.dynamic_slice_in_dim(keep_in, pipe * 100, 100, 2)
    grad_input = grad_input * keep_part[:, :, None, :]

    in_one, rec_one, bias_one, in_two, rec_two, bias_two = finish(total, drop_one, drop_two)
    return (layer_outputs, grad_input, in_one, rec_one, bias_one, in_two, rec_two, bias_two)


def solution(mesh):
    placed = (
        P(None, "dp", None, None),
        P(None, "dp"),
        P(None, "dp", None),
        P(None, "dp", None),
        P(None, "dp", None),
        P(None, "pipe"),
        P(None, "pipe"),
        P("pipe"),
        P(None, "pipe"),
        P(None, "pipe"),
        P(None, "pipe"),
        P("pipe"),
        P(None, "pipe"),
        P(None, "dp", None, None),
    )
    return jax.shard_map(
        local,
        mesh=mesh,
        in_specs=placed,
        out_specs=(
            P("pipe", "dp", None, None),
            P(None, "dp", None, "pipe"),
            P(None, "pipe"),
            P(None, "pipe"),
            P("pipe"),
            P(None, "pipe"),
            P(None, "pipe"),
            P("pipe"),
        ),
        check_vma=False,
    )
```
